32 devices in a mesh: groups: 2 (over y), row: 4 (over z), sect: 2 (over x), batch: 2 (over core).
Axes of the slice: x: 2, y: 2, z: 4, core: 2. Of those that a mesh axis runs over, the one named last changes fastest.
Arguments:
- probe: float32 [2, 512, 512], P(None, 'row'), may hold values from -4.2 to 4.2
- object_delta: float32 [4, 2, 512, 2048], P(('groups', 'sect'), None, 'row'), parts along dimension 0, may hold values from -1.8 to 1.8
- measured: float32 [4, 2, 512, 512], P(('groups', 'batch'), None, 'row'), parts along dimension 0, may hold values from 0.05 to 4
- pos_y: int32 [4, 2], P(('groups', 'batch')), parts along dimension 0, may hold values from 0 to 127
- pos_x: int32 [4, 2], P(('groups', 'batch')), parts along dimension 0, may hold values from 0 to 1536
- prop_phase: float32 [512, 512], P('row'), may hold values from -3.140625 to 3.140625
Outputs:
- object_grad: float32 [4, 2, 512, 2048], P(('groups', 'sect'), None, 'row'), parts along dimension 0
The draws below stay inside these ranges and needn't reach their ends.
There are 2 independent parts, one for each index of `groups`. The reference program is written for one: setup_inputs(seed, part) draws one part's arguments, and reference() takes and returns one part's arrays. A program takes and returns all parts, laid end to end along the dimension named above; an argument that names none is the same for every part. Nothing has to cross between parts.
All inputs are finite; a program needn't handle non-finite values.
Results may differ from the reference program's by a relative error of at most 0.00017.
Values sent between devices are 32-bit elements; how exact they have to be, the bound alone decides.
No kernel may reach another device: no remote copies, remote signals or barrier semaphores. Data moves between devices by JAX's collectives and lax.ppermute only.
A program may use at most 64 MiB of HBM per device.

```python
import math
import jax
import jax.numpy as jnp
from jax import lax

WAVE = 512
SPAN = 1536
ROWS_DEV = 128
OBJX = 2048
SLICES = 2
MICRO = 2
MB = 2
N_ROW = 4
N_SECT = 2
N_BATCH = 2


def place_ends(array, rng, least, high):
    longest = array.shape.index(max(array.shape))
    spots = []
    for shift in (0, 1):
        where = [jax.random.randint(jax.random.fold_in(rng, axis), (), 0, length) for axis, length in enumerate(array.shape)]
        where[longest] = (where[longest] + shift) % array.shape[longest]
        spots.append(tuple(where))
    return array.at[spots[0]].set(least).at[spots[1]].set(high)


def steps_of(key, extent, shards, low, top_value):
    gain, own = 1.0, jax.random.fold_in(key, 6)
    for position, blocks in shards:
        heights = jnp.exp(jax.random.uniform(jax.random.fold_in(own, position), (blocks,), jnp.float32, low / len(shards), top_value / len(shards)))
        gain = gain * jnp.repeat(heights, extent[position] // blocks).reshape([-1 if axis == position else 1 for axis in range(len(extent))])
    return gain


def centred(key, extent, scale, reach, shards=(), held_as=jnp.bfloat16):
    result = jax.random.normal(key, extent, jnp.float32) * scale
    if len(shards) > 0:
        result = steps_of(key, extent, shards, -0.22, 0.18) * result
    return jnp.clip(result, min=-reach, max=reach).astype(held_as)


def setup_inputs(seed: int = 0, part: int = 0) -> dict:
    arg_keys = jax.random.split(jax.random.key(seed), 7)
    part_keys = jax.random.split(jax.random.fold_in(arg_keys[6], part), 7)
    return {
        "probe": centred(arg_keys[0], (2, WAVE, WAVE), 0.7, 4.2, ((1, 4),), jnp.float32),
        "object_delta": centred(part_keys[1], (SLICES, 2, WAVE, OBJX), 0.3, 1.8, ((0, 2), (2, 4)), jnp.float32),
        "measured": jnp.clip(jnp.exp(math.log(4.0) - 4.3820266 * jax.random.uniform(part_keys[2], (MICRO, MB, WAVE, WAVE), jnp.float32) ** steps_of(part_keys[2], (MICRO, MB, WAVE, WAVE), ((0, 2), (2, 4)), -0.2, 0.2)), 0.05, 4.0),
        "pos_y": place_ends(jax.random.randint(part_keys[3], (MICRO, MB), 0, ROWS_DEV), jax.random.fold_in(part_keys[3], 1), 0, ROWS_DEV - 1).astype(jnp.int32),
        "pos_x": place_ends(jax.random.randint(part_keys[4], (MICRO, MB), 0, SPAN + 1), jax.random.fold_in(part_keys[4], 1), 0, SPAN).astype(jnp.int32),
        "prop_phase": jnp.clip(jax.random.uniform(arg_keys[5], (WAVE, WAVE), jnp.float32, -3.140625, 3.140625), -3.140625, 3.140625),
    }


def spectrum(wave_field):
    return jnp.fft.fft2(wave_field, norm="ortho").T


def restore(spectral):
    return jnp.fft.ifft2(spectral.T, norm="ortho")


def reference(probe, object_delta, measured, pos_y, pos_x, prop_phase):
    height = WAVE // N_ROW
    padded = jnp.pad(object_delta, ((0, 0), (0, 0), (0, height), (0, 0)))
    trans = 1.0 + padded[:, 0] + 1j * padded[:, 1]
    kernel = jnp.cos(prop_phase) + 1j * jnp.sin(prop_phase)
    incident = probe[0] + 1j * probe[1]
    gradient = jnp.zeros(trans.shape, trans.dtype)
    for micro_index in range(N_BATCH):
        for probe_index in range(MB):
            start_y = pos_y[micro_index, probe_index]
            start_x = pos_x[micro_index, probe_index]
            entries = []
            patches = []
            entering = incident
            far_field = None
            for layer_index in range(N_SECT):
                patch_now = lax.dynamic_slice(trans[layer_index], (start_y, start_x), (WAVE, WAVE))
                entries.append(entering)
                patches.append(patch_now)
                far_field = spectrum(entering * patch_now)
                if layer_index < N_SECT - 1:
                    entering = restore(kernel * far_field)
            residual = far_field.real ** 2 + far_field.imag ** 2 - measured[micro_index, probe_index]
            backward = residual * far_field
            for layer_index in reversed(range(N_SECT)):
                inner = restore(backward)
                term = jnp.conj(entries[layer_index]) * inner
                anchor = (jnp.int32(layer_index), start_y, start_x)
                before = lax.dynamic_slice(gradient, anchor, (1, WAVE, WAVE))
                gradient = lax.dynamic_update_slice(gradient, before + term[None], anchor)
                if layer_index > 0:
                    backward = jnp.conj(kernel) * spectrum(jnp.conj(patches[layer_index]) * inner)
    stacked = jnp.stack([gradient.real, gradient.imag], axis=1)
    return stacked[:, :, :WAVE]
```

```python
import functools
import math

import jax
import jax.numpy as jnp
import ml_dtypes
import numpy as np
from jax import lax
from jax.experimental import pallas as pl
from jax.experimental.pallas import tpu as pltpu
from jax.sharding import PartitionSpec as P

highest = lax.Precision.HIGHEST
line_axes = ("row", "sect", "batch")
vmem_bytes = 40 * 1024 * 1024
smem = pltpu.MemorySpace.SMEM


def halves(table):
    table = table.astype(np.float64)
    upper = table.astype(ml_dtypes.bfloat16)
    lower = (table - upper.astype(np.float64)).astype(ml_dtypes.bfloat16)
    return np.stack([upper, lower])


def circle(length):
    quarter = length // 4
    index = np.arange(quarter)
    angles = (index[:, None] * index[None, :] % quarter) * (2.0 * math.pi / quarter)
    scale = 1.0 / math.sqrt(length)
    return np.cos(angles) * scale, np.sin(angles) * scale


def column_tables(length):
    cosine, sine = circle(length)
    forward = np.block([[cosine, sine], [-sine, cosine]])
    inverse = np.block([[cosine, -sine], [sine, cosine]])
    return halves(forward), halves(inverse)


def row_tables(length, shift):
    cosine, sine = circle(length)
    order = (np.arange(length // 4) + shift) % (length // 4)
    cosine, sine = cosine[:, order], sine[:, order]
    forward = np.block([[cosine, -sine], [sine, cosine]])
    inverse = np.block([[cosine.T, sine.T], [-sine.T, cosine.T]])
    return halves(forward), halves(inverse)


def twiddles(length):
    quarter = length // 4
    angles = np.arange(4)[:, None] * np.arange(quarter)[None, :] * (2.0 * math.pi / length)
    pairs = np.stack([np.cos(angles), np.sin(angles)], axis=1).astype(np.float32)
    along_lanes = pairs.reshape(8, quarter)
    along_rows = np.broadcast_to(pairs[..., None], (4, 2, quarter, 128)).copy()
    return along_lanes, along_rows


def split(value):
    upper = value.astype(jnp.bfloat16)
    lower = (value - upper.astype(jnp.float32)).astype(jnp.bfloat16)
    return upper, lower


def dot(first, second):
    return jnp.dot(first, second, preferred_element_type=jnp.float32)


def right_dot(value, table):
    upper, lower = split(value)
    return dot(upper, table[0]) + dot(lower, table[0]) + dot(upper, table[1])


def left_dot(table, value):
    upper, lower = split(value)
    return dot(table[0], upper) + dot(table[0], lower) + dot(table[1], upper)


def times(first, second):
    return (
        first[0] * second[0] - first[1] * second[1],
        first[0] * second[1] + first[1] * second[0],
    )


def conj_times(first, second):
    return (
        first[0] * second[0] + first[1] * second[1],
        first[0] * second[1] - first[1] * second[0],
    )


def plus(first, second):
    return (first[0] + second[0], first[1] + second[1])


def minus(first, second):
    return (first[0] - second[0], first[1] - second[1])


def turned(value):
    return (-value[1], value[0])


def scatter4(parts):
    sum02, dif02 = plus(parts[0], parts[2]), minus(parts[0], parts[2])
    sum13, dif13 = plus(parts[1], parts[3]), turned(minus(parts[1], parts[3]))
    return [plus(sum02, sum13), minus(dif02, dif13), minus(sum02, sum13), plus(dif02, dif13)]


def gather4(parts):
    sum02, dif02 = plus(parts[0], parts[2]), minus(parts[0], parts[2])
    sum13, dif13 = plus(parts[1], parts[3]), turned(minus(parts[1], parts[3]))
    return [plus(sum02, sum13), plus(dif02, dif13), minus(sum02, sum13), minus(dif02, dif13)]


def lane_twiddle(reference, index):
    return (reference[2 * index : 2 * index + 1, :], reference[2 * index + 1 : 2 * index + 2, :])


def forward_lanes(quarters, table, twiddle):
    rows = quarters[0][0].shape[0]
    classes = scatter4(quarters)
    packed = []
    for index, value in enumerate(classes):
        if index > 0:
            value = conj_times(lane_twiddle(twiddle, index), value)
        packed.append(jnp.concatenate(value, axis=1))
    result = right_dot(jnp.concatenate(packed, axis=0), table)
    half = result.shape[1] // 2
    return [
        (result[rows * index : rows * (index + 1), :half], result[rows * index : rows * (index + 1), half:])
        for index in range(4)
    ]


def inverse_lanes(classes, table, twiddle):
    rows = classes[0][0].shape[0]
    packed = jnp.concatenate([jnp.concatenate(value, axis=1) for value in classes], axis=0)
    result = right_dot(packed, table)
    half = result.shape[1] // 2
    parts = []
    for index in range(4):
        value = (result[rows * index : rows * (index + 1), :half], result[rows * index : rows * (index + 1), half:])
        if index > 0:
            value = times(lane_twiddle(twiddle, index), value)
        parts.append(value)
    return gather4(parts)


def forward_rows(quarters, table, twiddle):
    lanes = quarters[0][0].shape[1]
    packed = []
    for index, value in enumerate(scatter4(quarters)):
        if index > 0:
            value = conj_times((twiddle[index, 0], twiddle[index, 1]), value)
        packed.append(jnp.concatenate(value, axis=0))
    result = left_dot(table, jnp.concatenate(packed, axis=1))
    half = result.shape[0] // 2
    return [
        (result[:half, lanes * index : lanes * (index + 1)], result[half:, lanes * index : lanes * (index + 1)])
        for index in range(4)
    ]


def inverse_rows(classes, table, twiddle):
    lanes = classes[0][0].shape[1]
    packed = jnp.concatenate([jnp.concatenate(value, axis=0) for value in classes], axis=1)
    result = left_dot(table, packed)
    half = result.shape[0] // 2
    parts = []
    for index in range(4):
        value = (result[:half, lanes * index : lanes * (index + 1)], result[half:, lanes * index : lanes * (index + 1)])
        if index > 0:
            value = times((twiddle[index, 0], twiddle[index, 1]), value)
        parts.append(value)
    return gather4(parts)


def joined(parts, axis):
    return parts[0] if len(parts) == 1 else jnp.concatenate(parts, axis=axis)


def window_delta(info, near, far, height, breadth):
    lane = lax.broadcasted_iota(jnp.int32, (height, breadth), 1)
    line = lax.broadcasted_iota(jnp.int32, (height, breadth), 0)
    vacuum = (line < info[5]) & (info[1] == 1)
    use_near = lane >= info[4]
    return [
        jnp.where(vacuum, 0.0, jnp.where(use_near, near[0, part], far[0, part])) for part in range(2)
    ]


def patch_kernel(info, near, far, patch, scratch):
    height, breadth = near.shape[2], near.shape[3]
    real, imag = window_delta(info, near, far, height, breadth)
    scratch[0] = real + 1.0
    scratch[1] = imag
    first = pl.multiple_of(info[0] * (height // 2), height // 2)
    patch[...] = scratch[:, pl.ds(first, height // 2), :]


def launch_kernel(info, near, far, window, table, twiddle, message, rolled):
    height, breadth = near.shape[2], near.shape[3]
    quarter = breadth // 4
    real, imag = window_delta(info, near, far, height, breadth)
    transmit = (real + 1.0, imag)
    entering = []
    for part in range(2):
        lines = pltpu.roll(window[part], info[5], 0)[height:]
        entering.append(pltpu.roll(lines, info[4], 1))
        rolled[part] = entering[part]
    value = times(entering, transmit)
    quarters = [tuple(item[:, quarter * m : quarter * (m + 1)] for item in value) for m in range(4)]
    lower = info[0] == 0
    classes = scatter4(quarters)
    packed = []
    for index in range(2):
        chosen = tuple(jnp.where(lower, classes[index][i], classes[index + 2][i]) for i in range(2))
        low, high = lane_twiddle(twiddle, index), lane_twiddle(twiddle, index + 2)
        factor = tuple(jnp.where(lower, low[i], high[i]) for i in range(2))
        packed.append(jnp.concatenate(conj_times(factor, chosen), axis=1))
    result = right_dot(jnp.concatenate(packed, axis=0), table[0])
    for index in range(2):
        block = result[height * index : height * (index + 1)]
        message[0, :, quarter * index : quarter * (index + 1)] = block[:, :quarter]
        message[1, :, quarter * index : quarter * (index + 1)] = block[:, quarter:]


def settle_kernel(number, info, tables, twiddle, *refs):
    own_spectra, other_spectra = refs[:number], refs[number : 2 * number]
    own_terms, other_terms = refs[2 * number : 3 * number], refs[3 * number : 4 * number]
    rolled = refs[4 * number : 5 * number]
    out, scratch = refs[5 * number :]
    height, breadth = scratch.shape[1], scratch.shape[2]
    quarter = breadth // 4
    lower = info[0, 0] == 0
    lane = lax.broadcasted_iota(jnp.int32, (height, breadth), 1)
    line = lax.broadcasted_iota(jnp.int32, (height, breadth), 0)
    out[...] = jnp.zeros_like(out)
    for j in range(number):

        @pl.when(info[j, 7] == 0)
        def _():
            classes = []
            for index in range(4):
                first = quarter * (index % 2)
                pair = []
                for part in range(2):
                    own = own_spectra[j][part, :, first : first + quarter]
                    other = other_spectra[j][part, :, first : first + quarter]
                    pair.append(jnp.where(lower, own, other) if index < 2 else jnp.where(lower, other, own))
                classes.append(tuple(pair))
            table = tables[info[j, 6]]
            inner = inverse_lanes(classes, table, twiddle)
            for m in range(4):
                columns = slice(quarter * m, quarter * (m + 1))
                entering = (rolled[j][0, :, columns], rolled[j][1, :, columns])
                term = conj_times(entering, inner[m])
                scratch[0, :, columns] = term[0]
                scratch[1, :, columns] = term[1]

        @pl.when(info[j, 7] != 0)
        def _():
            own, other = own_terms[j][...], other_terms[j][...]
            scratch[:, : height // 2, :] = jnp.where(lower, own, other)
            scratch[:, height // 2 :, :] = jnp.where(lower, other, own)

        present = (line >= info[j, 5]) | (info[j, 1] != 1)
        near = pl.ds(pl.multiple_of(info[j, 2] * breadth, breadth), breadth)
        far = pl.ds(pl.multiple_of(info[j, 3] * breadth, breadth), breadth)
        use_near = lane >= info[j, 4]
        for part in range(2):
            term = jnp.where(present, scratch[part], 0.0)
            out[0, part, :, near] += jnp.where(use_near, term, 0.0)
            out[0, part, :, far] += jnp.where(use_near, 0.0, term)


def split_lines(value, lower, count):
    height = value.shape[0] // count
    firsts, seconds = [], []
    for index in range(count):
        first = value[height * index : height * index + height // 2]
        second = value[height * index + height // 2 : height * (index + 1)]
        firsts.append(jnp.where(lower, first, second))
        seconds.append(jnp.where(lower, second, first))
    return joined(firsts, 0), joined(seconds, 0)


def merge_lines(own, other, lower, count):
    height = own.shape[0] // count
    parts = []
    for index in range(count):
        first = own[height * index : height * (index + 1)]
        second = other[height * index : height * (index + 1)]
        parts.append(jnp.where(lower, first, second))
        parts.append(jnp.where(lower, second, first))
    return jnp.concatenate(parts, axis=0)


def merged_quarters(own, other, lower, count):
    lines = own.shape[1] // 4
    quarters = []
    for m in range(4):
        rows = slice(lines * m, lines * (m + 1))
        quarters.append(tuple(merge_lines(own[part, rows], other[part, rows], lower, count) for part in range(2)))
    return quarters


def hand_over(quarters, lower, count, keep, send):
    lines = keep.shape[1] // 4
    for m in range(4):
        rows = slice(lines * m, lines * (m + 1))
        for part in range(2):
            keep[part, rows], send[part, rows] = split_lines(quarters[m][part], lower, count)


def filtered(classes, phase, conjugate):
    quarter = classes[0][0].shape[0]
    result = []
    for index in range(4):
        rows = slice(quarter * index, quarter * (index + 1))
        factor = (phase[0, rows], phase[1, rows])
        result.append((conj_times if conjugate else times)(factor, classes[index]))
    return result


def enter_kernel(number, info, forward, inverse, twiddle, phase, *refs):
    blocks, (keep, send) = refs[:number], refs[number:]
    lower = info[0] == 0
    count = number // 4
    quarters = [
        tuple(joined([blocks[count * m + i][part] for i in range(count)], 0) for part in range(2)) for m in range(4)
    ]
    far = forward_rows(quarters, forward, twiddle)
    hand_over(inverse_rows(filtered(far, phase, False), inverse, twiddle), lower, count, keep, send)


def through_kernel(number, info, forward, inverse, twiddle, phase, own, other, keep, send):
    lower = info[0] == 0
    count = number // 4
    far = forward_rows(merged_quarters(own, other, lower, count), forward, twiddle)
    hand_over(inverse_rows(filtered(far, phase, False), inverse, twiddle), lower, count, keep, send)


def back_kernel(number, info, forward, inverse, twiddle, phase, own, other, keep, send):
    lower = info[0] == 0
    count = number // 4
    far = forward_rows(merged_quarters(own, other, lower, count), forward, twiddle)
    hand_over(inverse_rows(filtered(far, phase, True), inverse, twiddle), lower, count, keep, send)


def residual_kernel(number, info, forward, inverse, twiddle, observed, own, other, keep, send):
    lower = info[0] == 0
    count = number // 4
    far = forward_rows(merged_quarters(own, other, lower, count), forward, twiddle)
    quarter = far[0][0].shape[0]
    seeded = []
    for index in range(4):
        target = observed[0, :, quarter * index : quarter * (index + 1)].T
        residual = far[index][0] * far[index][0] + far[index][1] * far[index][1] - target
        seeded.append((residual * far[index][0], residual * far[index][1]))
    hand_over(inverse_rows(seeded, inverse, twiddle), lower, count, keep, send)


def leave_kernel(number, info, forward, inverse, twiddle, phase, own, other, *blocks):
    lower = info[0] == 0
    count = number // 4
    far = forward_rows(merged_quarters(own, other, lower, count), forward, twiddle)
    quarters = inverse_rows(filtered(far, phase, True), inverse, twiddle)
    height = blocks[0].shape[1]
    for m in range(4):
        for i in range(count):
            for part in range(2):
                blocks[count * m + i][part] = quarters[m][part][height * i : height * (i + 1)]


def lane_classes(own, other, lower, rows):
    quarter = own.shape[2] // 2
    classes = []
    for index in range(4):
        columns = slice(quarter * (index % 2), quarter * (index % 2) + quarter)
        pair = []
        for part in range(2):
            first, second = own[part, rows, columns], other[part, rows, columns]
            pair.append(jnp.where(lower, first, second) if index < 2 else jnp.where(lower, second, first))
        classes.append(tuple(pair))
    return classes


def lanes_out(classes, lower, rows, keep, send):
    quarter = keep.shape[2] // 2
    for index in range(2):
        columns = slice(quarter * index, quarter * (index + 1))
        for part in range(2):
            low, high = classes[index][part], classes[index + 2][part]
            keep[part, rows, columns] = jnp.where(lower, low, high)
            send[part, rows, columns] = jnp.where(lower, high, low)


def lane_quarter(refs, part, columns):
    return joined([ref[part, :, columns] for ref in refs], 0)


def meet_kernel(number, info, forward, inverse, twiddle, own, other, *refs):
    patches, (entering, keep, send) = refs[:number], refs[number:]
    lower = info[0] == 0
    count = number // 4
    lines = own.shape[1] // 4
    table_back, table_on = inverse[0], forward[0]
    quarter = own.shape[2] // 2
    for m in range(4):
        rows = slice(lines * m, lines * (m + 1))
        wave = inverse_lanes(lane_classes(own, other, lower, rows), table_back, twiddle)
        quarters = []
        for piece in range(4):
            columns = slice(quarter * piece, quarter * (piece + 1))
            group = patches[count * m : count * (m + 1)]
            transmit = tuple(lane_quarter(group, part, columns) for part in range(2))
            entering[0, rows, columns] = wave[piece][0]
            entering[1, rows, columns] = wave[piece][1]
            quarters.append(times(wave[piece], transmit))
        lanes_out(forward_lanes(quarters, table_on, twiddle), lower, rows, keep, send)


def grade_kernel(number, info, forward, inverse, twiddle, own, other, entering, *refs):
    patches, terms, (keep, send) = refs[:number], refs[number : 2 * number], refs[2 * number :]
    lower = info[0] == 0
    count = number // 4
    lines = own.shape[1] // 4
    height = lines // count
    table_back, table_on = inverse[0], forward[0]
    quarter = own.shape[2] // 2
    for m in range(4):
        rows = slice(lines * m, lines * (m + 1))
        inner = inverse_lanes(lane_classes(own, other, lower, rows), table_back, twiddle)
        quarters = []
        for piece in range(4):
            columns = slice(quarter * piece, quarter * (piece + 1))
            group = patches[count * m : count * (m + 1)]
            transmit = tuple(lane_quarter(group, part, columns) for part in range(2))
            wave = (entering[0, rows, columns], entering[1, rows, columns])
            term = conj_times(wave, inner[piece])
            for i in range(count):
                for part in range(2):
                    terms[count * m + i][part, :, columns] = term[part][height * i : height * (i + 1)]
            quarters.append(conj_times(transmit, inner[piece]))
        lanes_out(forward_lanes(quarters, table_on, twiddle), lower, rows, keep, send)


def run(kernel, outs, info, *operands):
    return pl.pallas_call(
        kernel,
        out_shape=[jax.ShapeDtypeStruct(shape, jnp.float32) for shape in outs],
        in_specs=[pl.BlockSpec(memory_space=smem)] + [pl.BlockSpec(memory_space=pltpu.VMEM)] * len(operands),
        out_specs=[pl.BlockSpec(memory_space=pltpu.VMEM)] * len(outs),
        compiler_params=pltpu.CompilerParams(vmem_limit_bytes=vmem_bytes),
    )(info, *operands)


def on_device(probe, object_delta, measured, pos_y, pos_x, prop_phase):
    number = lax.axis_size("row")
    sections = lax.axis_size("sect")
    cores = lax.axis_size("batch")
    place, section, core = (lax.axis_index(axis) for axis in line_axes)
    height, breadth = probe.shape[1], probe.shape[2]
    own_probes = measured.shape[1]
    total = cores * own_probes
    spans = object_delta.shape[3] // breadth
    half = height // 2
    wide = breadth // 2
    quarter = breadth // 4

    depth = -(-total // sections)
    top = (number - depth) // 2
    home_x = [q % sections for q in range(total)]
    home_z = [top + q // sections for q in range(total)]
    base = [(home_z[q] + (number // sections) * home_x[q]) % number for q in range(total)]
    assert len(set(base)) == total
    of_base = np.zeros(number, np.int32)
    for q in range(total):
        of_base[base[q]] = q

    def spot(z, x, c):
        return (z * sections + x) * cores + c

    every = [(q, c) for q in range(total) for c in range(cores)]

    def inward(j, layer):
        return [
            (spot((base[q] + j) % number, layer, c), spot(home_z[q], home_x[q], c)) for q, c in every
        ]

    def outward(j, layer):
        return [(target, source) for source, target in inward(j, layer)]

    def inward_line(j):
        return [
            (spot((base[q] + j) % number, home_x[q], c), spot(home_z[q], home_x[q], c)) for q, c in every
        ]

    def move(value, pairs):
        return lax.ppermute(value, line_axes, pairs)

    def swap(value):
        return lax.ppermute(value, "batch", [(i, (i + 1) % cores) for i in range(cores)])

    def ordered(own, other):
        return jnp.where(core == 0, jnp.concatenate([own, other]), jnp.concatenate([other, own]))

    column_forward, column_inverse = (jnp.asarray(table) for table in column_tables(breadth))
    row_pairs = [row_tables(breadth, (height // 4) * base[q]) for q in range(total)]
    row_forward = jnp.asarray(np.stack([pair[0] for pair in row_pairs]))
    row_inverse = jnp.asarray(np.stack([pair[1] for pair in row_pairs]))
    lane_factors, line_factors = (jnp.asarray(table) for table in twiddles(breadth))
    mine = jnp.clip((place - top) * sections + section, 0, total - 1)
    my_forward = lax.dynamic_slice_in_dim(row_forward, mine, 1, 0)
    my_inverse = lax.dynamic_slice_in_dim(row_inverse, mine, 1, 0)

    part = lax.dynamic_slice_in_dim(probe, core * half, half, 1)
    above = lax.ppermute(part, "row", [(i, (i + 1) % number) for i in range(number)])
    above_other = swap(above)
    above = jnp.where(
        core == 0,
        jnp.concatenate([above, above_other], axis=1),
        jnp.concatenate([above_other, above], axis=1),
    )
    window = jnp.concatenate([above, probe], axis=1)

    positions = jnp.stack([pos_y[0], pos_x[0]], axis=1)
    positions = ordered(positions, swap(positions))
    which = [jnp.asarray(of_base)[(place - j) % number] for j in range(number)]
    infos = []
    for j in range(number):
        offset_y, offset_x = positions[which[j], 0], positions[which[j], 1]
        block = offset_x // breadth
        infos.append(
            jnp.stack(
                [
                    core,
                    (place == 0).astype(jnp.int32),
                    block,
                    jnp.minimum(block + 1, spans - 1),
                    offset_x % breadth,
                    offset_y,
                    which[j],
                    section,
                ]
            ).astype(jnp.int32)
        )

    lane_index = jnp.arange(breadth)
    to_classes = (lane_index[:, None] == (4 * (lane_index % quarter) + lane_index // quarter)[None, :]).astype(jnp.float32)
    line_index = jnp.arange(half)

    def class_rows(which_core):
        wanted = 4 * (line_index % (half // 2)) + 2 * which_core + line_index // (half // 2)
        return (wanted[:, None] == jnp.arange(height)[None, :]).astype(jnp.float32)

    def classed(planes, which_core):
        picked = jnp.einsum("au,quv->qav", class_rows(which_core), planes, precision=highest)
        return jnp.einsum("qav,vw->qaw", picked, to_classes, precision=highest)

    def assemble(pieces):
        stacked = jnp.stack([piece.reshape(2, half // 2, breadth) for piece in pieces], axis=1)
        return stacked.reshape(2, quarter, breadth)

    phase_piece = classed(prop_phase[None], core)[0]
    phase = assemble([move(phase_piece, inward_line(j)) for j in range(number)])
    phase = jnp.transpose(phase, (2, 0, 1)).reshape(breadth, wide)
    filter_field = jnp.stack([jnp.cos(phase), jnp.sin(phase)])

    def near_spec(slot):
        return pl.BlockSpec((1, 2, height, breadth), lambda i, info: (0, 0, 0, info[slot]))

    def whole_spec(value):
        return pl.BlockSpec(value.shape, lambda i, info: (0,) * value.ndim)

    def patch_of(info):
        return pl.pallas_call(
            patch_kernel,
            out_shape=jax.ShapeDtypeStruct((2, half, breadth), jnp.float32),
            grid_spec=pltpu.PrefetchScalarGridSpec(
                num_scalar_prefetch=1,
                grid=(1,),
                in_specs=[near_spec(2), near_spec(3)],
                out_specs=pl.BlockSpec((2, half, breadth), lambda i, info: (0, 0, 0)),
                scratch_shapes=[pltpu.VMEM((2, height, breadth), jnp.float32)],
            ),
            compiler_params=pltpu.CompilerParams(vmem_limit_bytes=vmem_bytes),
        )(info, object_delta, object_delta)

    def launch_of(info):
        return pl.pallas_call(
            launch_kernel,
            out_shape=[
                jax.ShapeDtypeStruct((2, height, wide), jnp.float32),
                jax.ShapeDtypeStruct((2, height, breadth), jnp.float32),
            ],
            grid_spec=pltpu.PrefetchScalarGridSpec(
                num_scalar_prefetch=1,
                grid=(1,),
                in_specs=[
                    near_spec(2),
                    near_spec(3),
                    whole_spec(window),
                    pl.BlockSpec((1,) + row_forward.shape[1:], lambda i, info: (info[6], 0, 0, 0)),
                    whole_spec(lane_factors),
                ],
                out_specs=[
                    pl.BlockSpec((2, height, wide), lambda i, info: (0, 0, 0)),
                    pl.BlockSpec((2, height, breadth), lambda i, info: (0, 0, 0)),
                ],
            ),
            compiler_params=pltpu.CompilerParams(vmem_limit_bytes=vmem_bytes),
        )(info, object_delta, object_delta, window, row_forward, lane_factors)

    own_patches = [patch_of(infos[j]) for j in range(number)]
    patches = {
        layer: [move(own_patches[j], inward(j, layer)) for j in range(number)] for layer in range(1, sections)
    }
    launched = [launch_of(infos[j]) for j in range(number)]
    rolled = [item[1] for item in launched]
    blocks = [move(launched[j][0], inward(j, 0)) for j in range(number)]

    own_measured = classed(measured[0], core)
    other_measured = classed(measured[0], 1 - core)
    all_measured = ordered(own_measured, swap(other_measured))
    observed = assemble(
        [
            move(lax.dynamic_index_in_dim(all_measured, which[j], 0, keepdims=False), inward_line(j))
            for j in range(number)
        ]
    )

    about = jnp.stack([core]).astype(jnp.int32)
    traded = (2, breadth // 2, wide)
    column_set = (column_forward, column_inverse, line_factors)
    row_set = (my_forward, my_inverse, lane_factors)

    def rows_run(kernel, outs, field, *operands):
        lanes = 128
        steps = wide // lanes

        def lane_spec(shape):
            return pl.BlockSpec(tuple(shape[:-1]) + (lanes,), lambda i: (0,) * (len(shape) - 1) + (i,))

        if kernel is residual_kernel:
            field_spec = pl.BlockSpec((1,) + field.shape[1:], lambda i: (i, 0, 0))
        else:
            field_spec = lane_spec(field.shape)
        return pl.pallas_call(
            functools.partial(kernel, number),
            grid=(steps,),
            out_shape=[jax.ShapeDtypeStruct(shape, jnp.float32) for shape in outs],
            in_specs=[pl.BlockSpec(memory_space=smem)]
            + [pl.BlockSpec(value.shape, lambda i, nd=value.ndim: (0,) * nd) for value in column_set]
            + [field_spec]
            + [lane_spec(value.shape) for value in operands],
            out_specs=[lane_spec(shape) for shape in outs],
            compiler_params=pltpu.CompilerParams(vmem_limit_bytes=vmem_bytes),
        )(about, *column_set, field, *operands)

    entries = {}
    keep, send = rows_run(enter_kernel, [traded, traded], filter_field, *blocks)
    for layer in range(1, sections):
        other = swap(send)
        entries[layer], keep, send = run(
            functools.partial(meet_kernel, number),
            [(2, breadth // 2, breadth), traded, traded],
            about,
            *row_set,
            keep,
            other,
            *patches[layer],
        )
        other = swap(send)
        if layer < sections - 1:
            keep, send = rows_run(through_kernel, [traded, traded], filter_field, keep, other)
    keep, send = rows_run(residual_kernel, [traded, traded], observed, keep, other)

    terms = None
    for layer in range(sections - 1, 0, -1):
        other = swap(send)
        found = run(
            functools.partial(grade_kernel, number),
            [(2, half, breadth)] * number + [traded, traded],
            about,
            *row_set,
            keep,
            other,
            entries[layer],
            *patches[layer],
        )
        came = [move(found[j], outward(j, layer)) for j in range(number)]
        terms = came if terms is None else [first + second for first, second in zip(terms, came)]
        keep, send = found[number:]
        other = swap(send)
        if layer > 1:
            keep, send = rows_run(back_kernel, [traded, traded], filter_field, keep, other)
    leaving = rows_run(leave_kernel, [(2, height, wide)] * number, filter_field, keep, other)
    spectra = [move(leaving[j], outward(j, 0)) for j in range(number)]

    other_terms = [swap(value) for value in terms]
    other_spectra = [swap(value) for value in spectra]
    info_all = jnp.stack(infos)
    operands = [row_inverse, lane_factors, *spectra, *other_spectra, *terms, *other_terms, *rolled]
    return pl.pallas_call(
        functools.partial(settle_kernel, number),
        out_shape=jax.ShapeDtypeStruct(object_delta.shape, jnp.float32),
        in_specs=[pl.BlockSpec(memory_space=smem)] + [pl.BlockSpec(memory_space=pltpu.VMEM)] * len(operands),
        out_specs=pl.BlockSpec(memory_space=pltpu.VMEM),
        scratch_shapes=[pltpu.VMEM((2, height, breadth), jnp.float32)],
        compiler_params=pltpu.CompilerParams(vmem_limit_bytes=vmem_bytes),
    )(info_all, *operands)


def solution(mesh):
    in_specs = (
        P(None, "row", None),
        P(("groups", "sect"), None, "row", None),
        P(("groups", "batch"), None, "row", None),
        P(("groups", "batch"), None),
        P(("groups", "batch"), None),
        P("row", None),
    )
    out_specs = P(("groups", "sect"), None, "row", None)
    return jax.shard_map(
        on_device, mesh=mesh, in_specs=in_specs, out_specs=out_specs, check_vma=False
    )
```

```python
import functools
import math

import jax
import jax.numpy as jnp
import ml_dtypes
import numpy as np
from jax import lax
from jax.experimental import pallas as pl
from jax.experimental.pallas import tpu as pltpu
from jax.sharding import PartitionSpec as P

highest = lax.Precision.HIGHEST
line_axes = ("row", "sect", "batch")
vmem_bytes = 20 * 1024 * 1024
light = pl.CostEstimate(flops=0, transcendentals=0, bytes_accessed=0)
smem = pltpu.MemorySpace.SMEM


def halves(table):
    table = table.astype(np.float64)
    upper = table.astype(ml_dtypes.bfloat16)
    lower = (table - upper.astype(np.float64)).astype(ml_dtypes.bfloat16)
    return np.stack([upper, lower])


def circle(length):
    quarter = length // 4
    index = np.arange(quarter)
    angles = (index[:, None] * index[None, :] % quarter) * (2.0 * math.pi / quarter)
    scale = 1.0 / math.sqrt(length)
    return np.cos(angles) * scale, np.sin(angles) * scale


def column_tables(length):
    cosine, sine = circle(length)
    forward = np.block([[cosine, sine], [-sine, cosine]])
    inverse = np.block([[cosine, -sine], [sine, cosine]])
    return halves(forward), halves(inverse)


def row_tables(length):
    cosine, sine = circle(length)
    forward = np.block([[cosine, -sine], [sine, cosine]])
    inverse = np.block([[cosine.T, sine.T], [-sine.T, cosine.T]])
    return halves(forward), halves(inverse)


def twiddles(length):
    quarter = length // 4
    angles = np.arange(4)[:, None] * np.arange(quarter)[None, :] * (2.0 * math.pi / length)
    pairs = np.stack([np.cos(angles), np.sin(angles)], axis=1).astype(np.float32)
    along_lanes = pairs.reshape(8, quarter)
    along_rows = np.broadcast_to(pairs[..., None], (4, 2, quarter, 128)).copy()
    return along_lanes, along_rows


def circle_polynomials(reach):
    grid = np.cos((np.arange(64) + 0.5) * math.pi / 64.0)
    square = (grid + 1.0) * 0.5 * reach * reach
    root = np.sqrt(square)
    found = []
    for values in (np.cos(root), np.sinc(root / math.pi)):
        fitted = np.polynomial.Polynomial.fit(square, values, 9, domain=[0.0, reach * reach])
        found.append([float(item) for item in fitted.convert().coef])
    return found


def split(value):
    upper = value.astype(jnp.bfloat16)
    lower = (value - upper.astype(jnp.float32)).astype(jnp.bfloat16)
    return upper, lower


def dot(first, second):
    return jnp.dot(first, second, preferred_element_type=jnp.float32)


def right_dot(value, table):
    upper, lower = split(value)
    return dot(upper, table[0]) + dot(lower, table[0]) + dot(upper, table[1])


def left_dot(table, value):
    upper, lower = split(value)
    return dot(table[0], upper) + dot(table[0], lower) + dot(table[1], upper)


def times(first, second):
    return (
        first[0] * second[0] - first[1] * second[1],
        first[0] * second[1] + first[1] * second[0],
    )


def conj_times(first, second):
    return (
        first[0] * second[0] + first[1] * second[1],
        first[0] * second[1] - first[1] * second[0],
    )


def plus(first, second):
    return (first[0] + second[0], first[1] + second[1])


def minus(first, second):
    return (first[0] - second[0], first[1] - second[1])


def turned(value):
    return (-value[1], value[0])


def scatter4(parts):
    sum02, dif02 = plus(parts[0], parts[2]), minus(parts[0], parts[2])
    sum13, dif13 = plus(parts[1], parts[3]), turned(minus(parts[1], parts[3]))
    return [plus(sum02, sum13), minus(dif02, dif13), minus(sum02, sum13), plus(dif02, dif13)]


def gather4(parts):
    sum02, dif02 = plus(parts[0], parts[2]), minus(parts[0], parts[2])
    sum13, dif13 = plus(parts[1], parts[3]), turned(minus(parts[1], parts[3]))
    return [plus(sum02, sum13), plus(dif02, dif13), minus(sum02, sum13), minus(dif02, dif13)]


def lane_twiddle(reference, index):
    return (reference[2 * index : 2 * index + 1, :], reference[2 * index + 1 : 2 * index + 2, :])


def forward_lanes(quarters, table, twiddle):
    rows = quarters[0][0].shape[0]
    classes = scatter4(quarters)
    packed = []
    for index, value in enumerate(classes):
        if index > 0:
            value = conj_times(lane_twiddle(twiddle, index), value)
        packed.append(jnp.concatenate(value, axis=1))
    result = right_dot(jnp.concatenate(packed, axis=0), table)
    half = result.shape[1] // 2
    return [
        (result[rows * index : rows * (index + 1), :half], result[rows * index : rows * (index + 1), half:])
        for index in range(4)
    ]


def inverse_lanes(classes, table, twiddle):
    rows = classes[0][0].shape[0]
    packed = jnp.concatenate([jnp.concatenate(value, axis=1) for value in classes], axis=0)
    result = right_dot(packed, table)
    half = result.shape[1] // 2
    parts = []
    for index in range(4):
        value = (result[rows * index : rows * (index + 1), :half], result[rows * index : rows * (index + 1), half:])
        if index > 0:
            value = times(lane_twiddle(twiddle, index), value)
        parts.append(value)
    return gather4(parts)


def forward_rows(quarters, table, twiddle):
    lanes = quarters[0][0].shape[1]
    packed = []
    for index, value in enumerate(scatter4(quarters)):
        if index > 0:
            value = conj_times((twiddle[index, 0], twiddle[index, 1]), value)
        packed.append(jnp.concatenate(value, axis=0))
    result = left_dot(table, jnp.concatenate(packed, axis=1))
    half = result.shape[0] // 2
    return [
        (result[:half, lanes * index : lanes * (index + 1)], result[half:, lanes * index : lanes * (index + 1)])
        for index in range(4)
    ]


def inverse_rows(classes, table, twiddle):
    lanes = classes[0][0].shape[1]
    packed = jnp.concatenate([jnp.concatenate(value, axis=0) for value in classes], axis=1)
    result = left_dot(table, packed)
    half = result.shape[0] // 2
    parts = []
    for index in range(4):
        value = (result[:half, lanes * index : lanes * (index + 1)], result[half:, lanes * index : lanes * (index + 1)])
        if index > 0:
            value = times((twiddle[index, 0], twiddle[index, 1]), value)
        parts.append(value)
    return gather4(parts)


def joined(parts, axis):
    return parts[0] if len(parts) == 1 else jnp.concatenate(parts, axis=axis)


class Plan:
    def __init__(self, number, sections, cores, own_probes, spans, breadth):
        assert own_probes == sections and spans > 1
        self.number, self.sections, self.cores = number, sections, cores
        self.own_probes, self.spans, self.breadth = own_probes, spans, breadth
        self.stride = number // sections
        assert self.stride >= cores
        self.top = (number - cores) // 2
        self.total = cores * own_probes

    def home(self, q):
        return self.top + q // self.sections, q % self.sections

    def base(self, q):
        z, x = self.home(q)
        return (z + self.stride * x) % self.number

    def own_base(self, info):
        return lax.rem(info[1] + self.stride * info[2], self.number)

    def served(self, info, j):
        step = lax.rem(info[1] - j - self.top + 2 * self.number, self.number)
        return jnp.minimum(lax.rem(step, self.stride), self.cores - 1), lax.div(step, self.stride)

    def offsets(self, info, j):
        batch, probe = self.served(info, j)
        spot = 3 + probe + jnp.where(batch == info[0], 0, 2 * self.own_probes)
        return info[spot], info[spot + self.own_probes]

    def blocks(self, info, j):
        column = self.offsets(info, j)[1]
        near = lax.div(column, self.breadth)
        far = jnp.where(near + 1 < self.spans, near + 1, near - 1)
        return near, far, lax.rem(column, self.breadth)


def prepare_kernel(info, phase, measured, phase_piece, own_pieces, other_pieces, scratch):
    rows = phase.shape[0] // 4
    width = scratch.shape[2]
    tasks = [(phase, (phase_piece,))]
    for probe in range(measured.shape[1]):
        tasks.append((measured.at[0, probe], (own_pieces.at[probe], other_pieces.at[probe])))
    for source, targets in tasks:
        for tile in range(phase.shape[1] // width):
            columns = slice(width * tile, width * (tile + 1))
            scratch[tile] = source[:, columns]
            for index in range(2):
                part = slice(rows * index, rows * (index + 1))
                for flip, target in enumerate(targets):
                    low = scratch[tile, pl.ds(2 * flip + index, rows, stride=4), :]
                    high = scratch[tile, pl.ds(2 - 2 * flip + index, rows, stride=4), :]
                    target[part, columns] = jnp.where(info[0] == 0, low, high)


def exact_turn(value):
    length = value.shape[1]
    quarter = length // 4
    row = lax.broadcasted_iota(jnp.int32, (length, length), 0)
    column = lax.broadcasted_iota(jnp.int32, (length, length), 1)
    wanted = 4 * lax.rem(row, quarter) + lax.div(row, quarter)
    order = (wanted == column).astype(jnp.float32).astype(jnp.bfloat16)
    first = value.astype(jnp.bfloat16)
    rest = value - first.astype(jnp.float32)
    second = rest.astype(jnp.bfloat16)
    third = (rest - second.astype(jnp.float32)).astype(jnp.bfloat16)
    dims = (((1,), (1,)), ((), ()))
    parts = [
        lax.dot_general(order, item, dims, preferred_element_type=jnp.float32) for item in (first, second, third)
    ]
    return (parts[0] + parts[1]) + parts[2]


def class_rows(pieces, index):
    rows = pieces[0].shape[0] // 2
    return joined([piece[rows * index : rows * (index + 1), :] for piece in pieces], 0)


def polynomial(coefficients, value):
    result = jnp.full_like(value, coefficients[-1])
    for item in coefficients[-2::-1]:
        result = result * value + item
    return result


def filter_kernel(plan, info, *refs):
    pieces, field = refs[:-1], refs[-1]
    cosine, sine = circle_polynomials(3.1416)
    quarter = field.shape[2] // 2
    shift = plan.own_base(info) * (pieces[0].shape[1] // 2)
    for index in range(2):
        columns = slice(quarter * index, quarter * (index + 1))
        phase = pltpu.roll(exact_turn(class_rows([piece.at[2] for piece in pieces], index)), shift, 1)
        square = phase * phase
        field[0, :, columns] = polynomial(cosine, square)
        field[1, :, columns] = polynomial(sine, square) * phase


def target_kernel(plan, info, *refs):
    pieces, target = refs[:-1], refs[-1]
    quarter = target.shape[1] // 2
    rows = pieces[0].shape[1] // 4
    shift = plan.own_base(info) * rows
    for index in range(2):
        columns = slice(quarter * index, quarter * (index + 1))
        first, second = slice(rows * index, rows * (index + 1)), slice(rows * (index + 2), rows * (index + 3))
        lines = [jnp.concatenate([piece[2, first], piece[2, second]], axis=1) for piece in pieces]
        target[:, columns] = pltpu.roll(exact_turn(joined(lines, 0)), shift, 1)


def window_delta(info, plan, j, near, far):
    height, breadth = near.shape[2], near.shape[3]
    offset_y = plan.offsets(info, j)[0]
    column = plan.blocks(info, j)[2]
    lane = lax.broadcasted_iota(jnp.int32, (height, breadth), 1)
    line = lax.broadcasted_iota(jnp.int32, (height, breadth), 0)
    vacuum = (line < offset_y) & (info[1] == 0)
    use_near = lane >= column
    return [
        jnp.where(vacuum, 0.0, jnp.where(use_near, near[0, part], far[0, part])) for part in range(2)
    ]


def patch_kernel(plan, j, info, near, far, phase_piece, patch, scratch):
    height = near.shape[2]
    real, imag = window_delta(info, plan, j, near, far)
    scratch[0] = real + 1.0
    scratch[1] = imag
    first = pl.multiple_of(info[0] * (height // 2), height // 2)
    patch[:2] = scratch[:, pl.ds(first, height // 2), :]
    patch[2] = phase_piece[...]


def launch_kernel(
    plan, j, info, near, far, above, above_other, probe, own_piece, other_piece, table, twiddle, message, rolled
):
    height, breadth = near.shape[2], near.shape[3]
    quarter = breadth // 4
    real, imag = window_delta(info, plan, j, near, far)
    transmit = (real + 1.0, imag)
    offset_y = plan.offsets(info, j)[0]
    column = plan.blocks(info, j)[2]
    lower = info[0] == 0
    entering = []
    for part in range(2):
        first, second = above[part], above_other[part]
        pieces = [jnp.where(lower, first, second), jnp.where(lower, second, first), probe[part]]
        lines = pltpu.roll(jnp.concatenate(pieces, axis=0), offset_y, 0)[height:]
        entering.append(pltpu.roll(lines, column, 1))
        rolled[part] = entering[part]
    value = times(entering, transmit)
    quarters = [tuple(item[:, quarter * m : quarter * (m + 1)] for item in value) for m in range(4)]
    classes = scatter4(quarters)
    packed = []
    for index in range(2):
        chosen = tuple(jnp.where(lower, classes[index][i], classes[index + 2][i]) for i in range(2))
        low, high = lane_twiddle(twiddle, index), lane_twiddle(twiddle, index + 2)
        factor = tuple(jnp.where(lower, low[i], high[i]) for i in range(2))
        packed.append(jnp.concatenate(conj_times(factor, chosen), axis=1))
    result = right_dot(jnp.concatenate(packed, axis=0), table)
    for index in range(2):
        block = result[height * index : height * (index + 1)]
        message[0, :, quarter * index : quarter * (index + 1)] = block[:, :quarter]
        message[1, :, quarter * index : quarter * (index + 1)] = block[:, quarter:]
    piece = jnp.where(plan.served(info, j)[0] == info[0], own_piece[0], other_piece[0])
    message[2, : height // 2] = piece[:, : breadth // 2]
    message[2, height // 2 :] = piece[:, breadth // 2 :]


def settle_kernel(plan, info, table, twiddle, *refs):
    number = plan.number
    own_spectra, other_spectra = refs[:number], refs[number : 2 * number]
    own_terms, other_terms = refs[2 * number : 3 * number], refs[3 * number : 4 * number]
    rolled = refs[4 * number : 5 * number]
    out, scratch = refs[5 * number :]
    height, breadth = scratch.shape[1], scratch.shape[2]
    quarter = breadth // 4
    lower = info[0] == 0
    lane = lax.broadcasted_iota(jnp.int32, (height, breadth), 1)
    line = lax.broadcasted_iota(jnp.int32, (height, breadth), 0)
    out[...] = jnp.zeros_like(out)
    for j in range(number):

        @pl.when(info[2] == 0)
        def _():
            classes = []
            for index in range(4):
                first = quarter * (index % 2)
                pair = []
                for part in range(2):
                    own = own_spectra[j][part, :, first : first + quarter]
                    other = other_spectra[j][part, :, first : first + quarter]
                    pair.append(jnp.where(lower, own, other) if index < 2 else jnp.where(lower, other, own))
                classes.append(tuple(pair))
            inner = inverse_lanes(classes, table, twiddle)
            for m in range(4):
                columns = slice(quarter * m, quarter * (m + 1))
                entering = (rolled[j][0, :, columns], rolled[j][1, :, columns])
                term = conj_times(entering, inner[m])
                scratch[0, :, columns] = term[0]
                scratch[1, :, columns] = term[1]

        @pl.when(info[2] != 0)
        def _():
            own, other = own_terms[j][...], other_terms[j][...]
            scratch[:, : height // 2, :] = jnp.where(lower, own, other)
            scratch[:, height // 2 :, :] = jnp.where(lower, other, own)

        near_block, far_block, column = plan.blocks(info, j)
        present = (line >= plan.offsets(info, j)[0]) | (info[1] != 0)
        near = pl.ds(pl.multiple_of(near_block * breadth, breadth), breadth)
        far = pl.ds(pl.multiple_of(far_block * breadth, breadth), breadth)
        use_near = lane >= column
        for part in range(2):
            term = jnp.where(present, scratch[part], 0.0)
            out[0, part, :, near] += jnp.where(use_near, term, 0.0)
            out[0, part, :, far] += jnp.where(use_near, 0.0, term)


def split_lines(value, lower, count):
    height = value.shape[0] // count
    firsts, seconds = [], []
    for index in range(count):
        first = value[height * index : height * index + height // 2]
        second = value[height * index + height // 2 : height * (index + 1)]
        firsts.append(jnp.where(lower, first, second))
        seconds.append(jnp.where(lower, second, first))
    return joined(firsts, 0), joined(seconds, 0)


def merge_lines(own, other, lower, count):
    height = own.shape[0] // count
    parts = []
    for index in range(count):
        first = own[height * index : height * (index + 1)]
        second = other[height * index : height * (index + 1)]
        parts.append(jnp.where(lower, first, second))
        parts.append(jnp.where(lower, second, first))
    return jnp.concatenate(parts, axis=0)


def tiles(width):
    quarter = width // 2
    return [slice(quarter * index, quarter * (index + 1)) for index in range(2)]


def merged_quarters(own, other, lower, count, columns):
    lines = own.shape[1] // 4
    quarters = []
    for m in range(4):
        rows = slice(lines * m, lines * (m + 1))
        quarters.append(
            tuple(merge_lines(own[part, rows, columns], other[part, rows, columns], lower, count) for part in range(2))
        )
    return quarters


def hand_over(quarters, lower, count, columns, keep, send):
    lines = keep.shape[1] // 4
    for m in range(4):
        rows = slice(lines * m, lines * (m + 1))
        for part in range(2):
            keep[part, rows, columns], send[part, rows, columns] = split_lines(quarters[m][part], lower, count)


def filtered(classes, field, conjugate, columns):
    quarter = classes[0][0].shape[0]
    result = []
    for index in range(4):
        rows = slice(quarter * index, quarter * (index + 1))
        factor = (field[0, rows, columns], field[1, rows, columns])
        result.append((conj_times if conjugate else times)(factor, classes[index]))
    return result


def enter_kernel(number, info, forward, inverse, twiddle, field, *refs):
    blocks, (keep, send) = refs[:number], refs[number:]
    lower = info[0] == 0
    count = number // 4
    for columns in tiles(keep.shape[2]):
        quarters = [
            tuple(
                joined([blocks[count * m + i][part, :, columns] for i in range(count)], 0) for part in range(2)
            )
            for m in range(4)
        ]
        far = filtered(forward_rows(quarters, forward, twiddle), field, False, columns)
        hand_over(inverse_rows(far, inverse, twiddle), lower, count, columns, keep, send)


def through_kernel(number, conjugate, info, forward, inverse, twiddle, field, own, other, keep, send):
    lower = info[0] == 0
    count = number // 4
    for columns in tiles(keep.shape[2]):
        far = forward_rows(merged_quarters(own, other, lower, count, columns), forward, twiddle)
        far = filtered(far, field, conjugate, columns)
        hand_over(inverse_rows(far, inverse, twiddle), lower, count, columns, keep, send)


def residual_kernel(number, info, forward, inverse, twiddle, target, own, other, keep, send):
    lower = info[0] == 0
    count = number // 4
    for columns in tiles(keep.shape[2]):
        far = forward_rows(merged_quarters(own, other, lower, count, columns), forward, twiddle)
        quarter = far[0][0].shape[0]
        seeded = []
        for index in range(4):
            real, imag = far[index]
            residual = real * real + imag * imag - target[quarter * index : quarter * (index + 1), columns]
            seeded.append((residual * real, residual * imag))
        hand_over(inverse_rows(seeded, inverse, twiddle), lower, count, columns, keep, send)


def leave_kernel(number, info, forward, inverse, twiddle, field, own, other, *blocks):
    lower = info[0] == 0
    count = number // 4
    height = blocks[0].shape[1]
    for columns in tiles(own.shape[2]):
        far = forward_rows(merged_quarters(own, other, lower, count, columns), forward, twiddle)
        quarters = inverse_rows(filtered(far, field, True, columns), inverse, twiddle)
        for m in range(4):
            for i in range(count):
                for part in range(2):
                    blocks[count * m + i][part, :, columns] = quarters[m][part][height * i : height * (i + 1)]


def lane_classes(own, other, lower, rows):
    quarter = own.shape[2] // 2
    classes = []
    for index in range(4):
        columns = slice(quarter * (index % 2), quarter * (index % 2) + quarter)
        pair = []
        for part in range(2):
            first, second = own[part, rows, columns], other[part, rows, columns]
            pair.append(jnp.where(lower, first, second) if index < 2 else jnp.where(lower, second, first))
        classes.append(tuple(pair))
    return classes


def lanes_out(classes, lower, rows, keep, send):
    quarter = keep.shape[2] // 2
    for index in range(2):
        columns = slice(quarter * index, quarter * (index + 1))
        for part in range(2):
            low, high = classes[index][part], classes[index + 2][part]
            keep[part, rows, columns] = jnp.where(lower, low, high)
            send[part, rows, columns] = jnp.where(lower, high, low)


def meet_kernel(plan, info, forward, inverse, twiddle, own, other, *refs):
    number = plan.number
    patches, (entering, keep, send) = refs[:number], refs[number:]
    lower = info[0] == 0
    count = number // 4
    lines = own.shape[1] // 4
    quarter = own.shape[2] // 2
    for m in range(4):
        rows = slice(lines * m, lines * (m + 1))
        group = patches[count * m : count * (m + 1)]
        wave = inverse_lanes(lane_classes(own, other, lower, rows), inverse, twiddle)
        quarters = []
        for piece in range(4):
            columns = slice(quarter * piece, quarter * (piece + 1))
            transmit = tuple(joined([patch[part, :, columns] for patch in group], 0) for part in range(2))
            entering[0, rows, columns] = wave[piece][0]
            entering[1, rows, columns] = wave[piece][1]
            quarters.append(times(wave[piece], transmit))
        lanes_out(forward_lanes(quarters, forward, twiddle), lower, rows, keep, send)


def grade_kernel(plan, info, forward, inverse, twiddle, own, other, entering, *refs):
    number = plan.number
    patches, terms, (keep, send) = refs[:number], refs[number : 2 * number], refs[2 * number :]
    lower = info[0] == 0
    count = number // 4
    lines = own.shape[1] // 4
    height = lines // count
    quarter = own.shape[2] // 2
    for m in range(4):
        rows = slice(lines * m, lines * (m + 1))
        group = patches[count * m : count * (m + 1)]
        inner = inverse_lanes(lane_classes(own, other, lower, rows), inverse, twiddle)
        quarters = []
        for piece in range(4):
            columns = slice(quarter * piece, quarter * (piece + 1))
            transmit = tuple(joined([patch[part, :, columns] for patch in group], 0) for part in range(2))
            wave = (entering[0, rows, columns], entering[1, rows, columns])
            term = conj_times(wave, inner[piece])
            for i in range(count):
                for part in range(2):
                    terms[count * m + i][part, :, columns] = term[part][height * i : height * (i + 1)]
            quarters.append(conj_times(transmit, inner[piece]))
        lanes_out(forward_lanes(quarters, forward, twiddle), lower, rows, keep, send)


def after(value, *others):
    return lax.optimization_barrier((value, *others))[0]


def on_device(probe, object_delta, measured, pos_y, pos_x, prop_phase):
    number = lax.axis_size("row")
    sections = lax.axis_size("sect")
    cores = lax.axis_size("batch")
    place, section, core = (lax.axis_index(axis) for axis in line_axes)
    height, breadth = probe.shape[1], probe.shape[2]
    spans = object_delta.shape[3] // breadth
    half, wide = height // 2, breadth // 2
    plan = Plan(number, sections, cores, measured.shape[1], spans, breadth)
    total = plan.total
    home_z = [plan.home(q)[0] for q in range(total)]
    home_x = [plan.home(q)[1] for q in range(total)]
    base = [plan.base(q) for q in range(total)]
    assert len(set(base)) == total

    def spot(z, x, c):
        return (z * sections + x) * cores + c

    every = [(q, c) for q in range(total) for c in range(cores)]

    def inward(j, layer):
        return [
            (spot((base[q] + j) % number, layer, c), spot(home_z[q], home_x[q], c)) for q, c in every
        ]

    def outward(j, layer):
        return [(target, source) for source, target in inward(j, layer)]

    def move(value, pairs):
        return lax.ppermute(value, line_axes, pairs)

    def swap(value):
        return lax.ppermute(value, "batch", [(i, (i + 1) % cores) for i in range(cores)])

    column_forward, column_inverse = (jnp.asarray(table) for table in column_tables(breadth))
    row_forward, row_inverse = (jnp.asarray(table) for table in row_tables(breadth))
    lane_factors, line_factors = (jnp.asarray(table) for table in twiddles(breadth))

    params = pltpu.CompilerParams(vmem_limit_bytes=vmem_bytes)
    part = jnp.where(core == 0, probe[:, :half], probe[:, half:])
    above = lax.ppermute(part, "row", [(i, (i + 1) % number) for i in range(number)])
    def beside(*vectors):
        sizes = [value.shape[0] for value in vectors]
        return sum(
            jnp.pad(value, (sum(sizes[:i]), sum(sizes[i + 1 :]))) for i, value in enumerate(vectors)
        ).astype(jnp.int32)

    own_positions = beside(pos_y[0], pos_x[0])
    about = jnp.stack([core, place, section]).astype(jnp.int32)
    info = beside(about, own_positions, swap(own_positions))

    def whole(shape):
        return pl.BlockSpec(tuple(shape), lambda i, *_: (0,) * len(shape))

    def floats(*shape):
        return jax.ShapeDtypeStruct(shape, jnp.float32)

    pieces_shape = (plan.own_probes, half, breadth)
    phase_piece, own_pieces, other_pieces = pl.pallas_call(
        prepare_kernel,
        out_shape=[floats(half, breadth), floats(*pieces_shape), floats(*pieces_shape)],
        grid_spec=pltpu.PrefetchScalarGridSpec(
            num_scalar_prefetch=1,
            grid=(1,),
            in_specs=[
                whole(prop_phase.shape),
                whole(measured.shape),
            ],
            out_specs=[whole((half, breadth)), whole(pieces_shape), whole(pieces_shape)],
            scratch_shapes=[pltpu.VMEM((breadth // 128, height, 128), jnp.float32)],
        ),
        cost_estimate=light,
            compiler_params=params,
    )(after(about, part), prop_phase, measured)
    other_pieces = swap(other_pieces)

    def near_spec(j, far):
        return pl.BlockSpec(
            (1, 2, height, breadth), lambda i, info: (0, 0, 0, plan.blocks(info, j)[1 if far else 0])
        )

    def patch_of(j, info):
        return pl.pallas_call(
            functools.partial(patch_kernel, plan, j),
            out_shape=floats(3, half, breadth),
            grid_spec=pltpu.PrefetchScalarGridSpec(
                num_scalar_prefetch=1,
                grid=(1,),
                in_specs=[near_spec(j, False), near_spec(j, True), whole(phase_piece.shape)],
                out_specs=whole((3, half, breadth)),
                scratch_shapes=[pltpu.VMEM((2, height, breadth), jnp.float32)],
            ),
            cost_estimate=light,
            compiler_params=params,
        )(info, object_delta, object_delta, phase_piece)

    def launch_of(j, info):
        piece_spec = pl.BlockSpec((1, half, breadth), lambda i, info: (plan.served(info, j)[1], 0, 0))
        return pl.pallas_call(
            functools.partial(launch_kernel, plan, j),
            out_shape=[floats(3, height, wide), floats(2, height, breadth)],
            grid_spec=pltpu.PrefetchScalarGridSpec(
                num_scalar_prefetch=1,
                grid=(1,),
                in_specs=[
                    near_spec(j, False),
                    near_spec(j, True),
                    whole(above.shape),
                    whole(above.shape),
                    whole(probe.shape),
                    piece_spec,
                    piece_spec,
                    whole(row_forward.shape),
                    whole(lane_factors.shape),
                ],
                out_specs=[whole((3, height, wide)), whole((2, height, breadth))],
            ),
            cost_estimate=light,
            compiler_params=params,
        )(
            info,
            object_delta,
            object_delta,
            above,
            above_other,
            probe,
            own_pieces,
            other_pieces,
            row_forward,
            lane_factors,
        )

    later = range(1, sections)
    own_patches = [patch_of(j, info) for j in range(number)]
    patches = {layer: [] for layer in later}
    above_other = swap(after(above, *own_patches))
    launched, blocks = [], []
    for j in range(number):
        value = own_patches[j]
        if j >= 2:
            value = after(value, *(patches[layer][j - 2] for layer in later))
        for layer in later:
            patches[layer].append(move(value, inward(j, layer)))
        launched.append(launch_of(j, info if j == 0 else after(info, launched[j - 1][0])))
        message = launched[j][0]
        if j >= 2:
            message = after(message, blocks[j - 2])
        blocks.append(move(message, inward(j, 0)))
    rolled = [item[1] for item in launched]
    blocks = lax.optimization_barrier((*blocks, *(patches[layer][j] for layer in later for j in range(number))))[:number]

    traded = (2, wide, wide)
    column_set = (column_forward, column_inverse, line_factors)
    row_set = (row_forward, row_inverse, lane_factors)

    def at_home(kernel, outs, *operands):
        return pl.pallas_call(
            kernel,
            out_shape=[floats(*shape) for shape in outs],
            in_specs=[pl.BlockSpec(memory_space=smem)] + [pl.BlockSpec(memory_space=pltpu.VMEM)] * len(operands),
            out_specs=[pl.BlockSpec(memory_space=pltpu.VMEM)] * len(outs),
            cost_estimate=light,
            compiler_params=params,
        )(about, *operands)

    def through(conjugate, own, other):
        kernel = functools.partial(through_kernel, number, conjugate)
        return at_home(kernel, [traded, traded], *column_set, field, own, other)

    entries = {}
    field = at_home(
        functools.partial(filter_kernel, plan), [(2, breadth, wide)], after(patches[1][0], launched[-1][0]), *patches[1][1:]
    )[0]
    keep, send = at_home(
        functools.partial(enter_kernel, number), [traded, traded], *column_set, field, *blocks
    )
    target = at_home(functools.partial(target_kernel, plan), [(breadth, wide)], *blocks)[0]
    for layer in later:
        other = swap(send)
        entries[layer], keep, send = at_home(
            functools.partial(meet_kernel, plan),
            [(2, wide, breadth), traded, traded],
            *row_set,
            keep,
            after(other, target) if layer == 1 else other,
            *patches[layer],
        )
        other = swap(send)
        if layer < sections - 1:
            keep, send = through(False, keep, other)
    keep, send = at_home(
        functools.partial(residual_kernel, number), [traded, traded], *column_set, target, keep, other
    )

    terms = None
    for layer in reversed(later):
        other = swap(send)
        found = at_home(
            functools.partial(grade_kernel, plan),
            [(2, half, breadth)] * number + [traded, traded],
            *row_set,
            keep,
            other,
            entries[layer],
            *patches[layer],
        )
        keep, send = found[number:]
        other = swap(send)
        if layer > 1:
            came = [move(after(found[j], other), outward(j, layer)) for j in range(number)]
            terms = came if terms is None else [first + second for first, second in zip(terms, came)]
            keep, send = through(True, keep, other)
    leaving = at_home(
        functools.partial(leave_kernel, number), [(2, height, wide)] * number, *column_set, field, keep, other
    )
    came = [move(after(found[j], other if j < 2 else leaving[0]), outward(j, 1)) for j in range(number)]
    spectra = [move(leaving[j], outward(j, 0)) for j in range(number)]
    terms = came if terms is None else [first + second for first, second in zip(terms, came)]

    operands = [
        row_inverse,
        lane_factors,
        *spectra,
        *(swap(value) for value in spectra),
        *terms,
        *(swap(value) for value in terms),
        *rolled,
    ]
    return pl.pallas_call(
        functools.partial(settle_kernel, plan),
        out_shape=jax.ShapeDtypeStruct(object_delta.shape, jnp.float32),
        in_specs=[pl.BlockSpec(memory_space=smem)] + [pl.BlockSpec(memory_space=pltpu.VMEM)] * len(operands),
        out_specs=pl.BlockSpec(memory_space=pltpu.VMEM),
        scratch_shapes=[pltpu.VMEM((2, height, breadth), jnp.float32)],
        cost_estimate=light,
        compiler_params=params,
    )(info, *operands)


def solution(mesh):
    in_specs = (
        P(None, "row", None),
        P(("groups", "sect"), None, "row", None),
        P(("groups", "batch"), None, "row", None),
        P(("groups", "batch"), None),
        P(("groups", "batch"), None),
        P("row", None),
    )
    out_specs = P(("groups", "sect"), None, "row", None)
    return jax.shard_map(
        on_device, mesh=mesh, in_specs=in_specs, out_specs=out_specs, check_vma=False
    )
```

```python
import functools
import math

import jax
import jax.numpy as jnp
import ml_dtypes
import numpy as np
from jax import lax
from jax.experimental import pallas as pl
from jax.experimental.pallas import tpu as pltpu
from jax.sharding import PartitionSpec as P

highest = lax.Precision.HIGHEST
line_axes = ("row", "sect", "batch")
vmem_bytes = 20 * 1024 * 1024
light = pl.CostEstimate(flops=0, transcendentals=0, bytes_accessed=0)
smem = pltpu.MemorySpace.SMEM


def halves(table):
    table = table.astype(np.float64)
    upper = table.astype(ml_dtypes.bfloat16)
    lower = (table - upper.astype(np.float64)).astype(ml_dtypes.bfloat16)
    return np.stack([upper, lower])


def circle(length):
    quarter = length // 4
    index = np.arange(quarter)
    angles = (index[:, None] * index[None, :] % quarter) * (2.0 * math.pi / quarter)
    scale = 1.0 / math.sqrt(length)
    return np.cos(angles) * scale, np.sin(angles) * scale


def column_tables(length):
    cosine, sine = circle(length)
    forward = np.block([[cosine, sine], [-sine, cosine]])
    inverse = np.block([[cosine, -sine], [sine, cosine]])
    return halves(forward), halves(inverse)


def row_tables(length):
    cosine, sine = circle(length)
    forward = np.block([[cosine, -sine], [sine, cosine]])
    inverse = np.block([[cosine.T, sine.T], [-sine.T, cosine.T]])
    return halves(forward), halves(inverse)


def twiddles(length):
    quarter = length // 4
    angles = np.arange(4)[:, None] * np.arange(quarter)[None, :] * (2.0 * math.pi / length)
    pairs = np.stack([np.cos(angles), np.sin(angles)], axis=1).astype(np.float32)
    along_lanes = pairs.reshape(8, quarter)
    along_rows = np.broadcast_to(pairs[..., None], (4, 2, quarter, 128)).copy()
    return along_lanes, along_rows


def circle_polynomials(reach):
    grid = np.cos((np.arange(64) + 0.5) * math.pi / 64.0)
    square = (grid + 1.0) * 0.5 * reach * reach
    root = np.sqrt(square)
    found = []
    for values in (np.cos(root), np.sinc(root / math.pi)):
        fitted = np.polynomial.Polynomial.fit(square, values, 9, domain=[0.0, reach * reach])
        found.append([float(item) for item in fitted.convert().coef])
    return found


def split(value):
    upper = value.astype(jnp.bfloat16)
    lower = (value - upper.astype(jnp.float32)).astype(jnp.bfloat16)
    return upper, lower


def dot(first, second):
    return jnp.dot(first, second, preferred_element_type=jnp.float32)


def right_dot(value, table):
    upper, lower = split(value)
    return dot(upper, table[0]) + dot(lower, table[0]) + dot(upper, table[1])


def left_dot(table, value):
    upper, lower = split(value)
    return dot(table[0], upper) + dot(table[0], lower) + dot(table[1], upper)


def times(first, second):
    return (
        first[0] * second[0] - first[1] * second[1],
        first[0] * second[1] + first[1] * second[0],
    )


def conj_times(first, second):
    return (
        first[0] * second[0] + first[1] * second[1],
        first[0] * second[1] - first[1] * second[0],
    )


def plus(first, second):
    return (first[0] + second[0], first[1] + second[1])


def minus(first, second):
    return (first[0] - second[0], first[1] - second[1])


def turned(value):
    return (-value[1], value[0])


def scatter4(parts):
    sum02, dif02 = plus(parts[0], parts[2]), minus(parts[0], parts[2])
    sum13, dif13 = plus(parts[1], parts[3]), turned(minus(parts[1], parts[3]))
    return [plus(sum02, sum13), minus(dif02, dif13), minus(sum02, sum13), plus(dif02, dif13)]


def gather4(parts):
    sum02, dif02 = plus(parts[0], parts[2]), minus(parts[0], parts[2])
    sum13, dif13 = plus(parts[1], parts[3]), turned(minus(parts[1], parts[3]))
    return [plus(sum02, sum13), plus(dif02, dif13), minus(sum02, sum13), minus(dif02, dif13)]


def lane_twiddle(reference, index):
    return (reference[2 * index : 2 * index + 1, :], reference[2 * index + 1 : 2 * index + 2, :])


def forward_lanes(quarters, table, twiddle):
    rows = quarters[0][0].shape[0]
    classes = scatter4(quarters)
    packed = []
    for index, value in enumerate(classes):
        if index > 0:
            value = conj_times(lane_twiddle(twiddle, index), value)
        packed.append(jnp.concatenate(value, axis=1))
    result = right_dot(jnp.concatenate(packed, axis=0), table)
    half = result.shape[1] // 2
    return [
        (result[rows * index : rows * (index + 1), :half], result[rows * index : rows * (index + 1), half:])
        for index in range(4)
    ]


def inverse_lanes(classes, table, twiddle):
    rows = classes[0][0].shape[0]
    packed = jnp.concatenate([jnp.concatenate(value, axis=1) for value in classes], axis=0)
    result = right_dot(packed, table)
    half = result.shape[1] // 2
    parts = []
    for index in range(4):
        value = (result[rows * index : rows * (index + 1), :half], result[rows * index : rows * (index + 1), half:])
        if index > 0:
            value = times(lane_twiddle(twiddle, index), value)
        parts.append(value)
    return gather4(parts)


def forward_rows(quarters, table, twiddle):
    lanes = quarters[0][0].shape[1]
    packed = []
    for index, value in enumerate(scatter4(quarters)):
        if index > 0:
            value = conj_times((twiddle[index, 0], twiddle[index, 1]), value)
        packed.append(jnp.concatenate(value, axis=0))
    result = left_dot(table, jnp.concatenate(packed, axis=1))
    half = result.shape[0] // 2
    return [
        (result[:half, lanes * index : lanes * (index + 1)], result[half:, lanes * index : lanes * (index + 1)])
        for index in range(4)
    ]


def inverse_rows(classes, table, twiddle):
    lanes = classes[0][0].shape[1]
    packed = jnp.concatenate([jnp.concatenate(value, axis=0) for value in classes], axis=1)
    result = left_dot(table, packed)
    half = result.shape[0] // 2
    parts = []
    for index in range(4):
        value = (result[:half, lanes * index : lanes * (index + 1)], result[half:, lanes * index : lanes * (index + 1)])
        if index > 0:
            value = times((twiddle[index, 0], twiddle[index, 1]), value)
        parts.append(value)
    return gather4(parts)


def joined(parts, axis):
    return parts[0] if len(parts) == 1 else jnp.concatenate(parts, axis=axis)


class Plan:
    def __init__(self, number, sections, cores, own_probes, spans, breadth):
        assert own_probes == sections and spans > 1
        self.number, self.sections, self.cores = number, sections, cores
        self.own_probes, self.spans, self.breadth = own_probes, spans, breadth
        self.stride = number // sections
        assert self.stride >= cores
        self.top = (number - cores) // 2
        self.total = cores * own_probes
        self.order = [j for pair in zip(range(number // 2), range(number // 2, number)) for j in pair]

    def home(self, q):
        return self.top + q // self.sections, q % self.sections

    def base(self, q):
        z, x = self.home(q)
        return (z + self.stride * x) % self.number

    def own_base(self, info):
        return lax.rem(info[1] + self.stride * info[2], self.number)

    def served(self, info, j):
        step = lax.rem(info[1] - j - self.top + 2 * self.number, self.number)
        return jnp.minimum(lax.rem(step, self.stride), self.cores - 1), lax.div(step, self.stride)

    def offsets(self, info, j):
        batch, probe = self.served(info, j)
        spot = 3 + probe + jnp.where(batch == info[0], 0, 2 * self.own_probes)
        return info[spot], info[spot + self.own_probes]

    def blocks(self, info, j):
        column = self.offsets(info, j)[1]
        near = lax.div(column, self.breadth)
        far = jnp.where(near + 1 < self.spans, near + 1, near - 1)
        return near, far, lax.rem(column, self.breadth)


def prepare_kernel(info, phase_hbm, measured_hbm, phase_piece, own_pieces, other_pieces, phase, measured, scratch, sems):
    rows = phase.shape[0] // 4
    width = scratch.shape[2]
    tasks = [(pltpu.make_async_copy(phase_hbm, phase, sems.at[0]), phase, (phase_piece,))]
    for probe in range(measured.shape[0]):
        copy = pltpu.make_async_copy(measured_hbm.at[0, probe], measured.at[probe], sems.at[1 + probe])
        tasks.append((copy, measured.at[probe], (own_pieces.at[probe], other_pieces.at[probe])))
    for copy, _, _ in tasks:
        copy.start()
    for copy, source, targets in tasks:
        copy.wait()
        for tile in range(phase.shape[1] // width):
            columns = slice(width * tile, width * (tile + 1))
            scratch[tile] = source[:, columns]
            for index in range(2):
                part = slice(rows * index, rows * (index + 1))
                for flip, target in enumerate(targets):
                    low = scratch[tile, pl.ds(2 * flip + index, rows, stride=4), :]
                    high = scratch[tile, pl.ds(2 - 2 * flip + index, rows, stride=4), :]
                    target[part, columns] = jnp.where(info[0] == 0, low, high)


def exact_turn(value):
    length = value.shape[1]
    quarter = length // 4
    row = lax.broadcasted_iota(jnp.int32, (length, length), 0)
    column = lax.broadcasted_iota(jnp.int32, (length, length), 1)
    wanted = 4 * lax.rem(row, quarter) + lax.div(row, quarter)
    order = (wanted == column).astype(jnp.float32).astype(jnp.bfloat16)
    first = value.astype(jnp.bfloat16)
    rest = value - first.astype(jnp.float32)
    second = rest.astype(jnp.bfloat16)
    third = (rest - second.astype(jnp.float32)).astype(jnp.bfloat16)
    dims = (((1,), (1,)), ((), ()))
    parts = [
        lax.dot_general(order, item, dims, preferred_element_type=jnp.float32) for item in (first, second, third)
    ]
    return (parts[0] + parts[1]) + parts[2]


def class_rows(pieces, index):
    rows = pieces[0].shape[0] // 2
    return joined([piece[rows * index : rows * (index + 1), :] for piece in pieces], 0)


def polynomial(coefficients, value):
    result = jnp.full_like(value, coefficients[-1])
    for item in coefficients[-2::-1]:
        result = result * value + item
    return result


def filter_kernel(info, *refs):
    pieces, field = refs[:-1], refs[-1]
    cosine, sine = circle_polynomials(3.1416)
    quarter = field.shape[2] // 2
    rows = pieces[0].shape[0] // 2
    shift = lax.rem((info[1] + 1) * rows, quarter)
    for index in range(2):
        columns = slice(quarter * index, quarter * (index + 1))
        phase = pltpu.roll(exact_turn(class_rows(pieces, index)), shift, 1)
        square = phase * phase
        field[0, :, columns] = polynomial(cosine, square)
        field[1, :, columns] = polynomial(sine, square) * phase


def target_kernel(plan, info, *refs):
    pieces, target = refs[:-1], refs[-1]
    quarter = target.shape[1] // 2
    shift = plan.own_base(info) * (pieces[0].shape[1] // 2)
    for index in range(2):
        columns = slice(quarter * index, quarter * (index + 1))
        lines = class_rows([piece.at[2] for piece in pieces], index)
        target[:, columns] = pltpu.roll(exact_turn(lines), shift, 1)


def window_delta(info, plan, j, near, far):
    height, breadth = near.shape[1], near.shape[2]
    offset_y = plan.offsets(info, j)[0]
    column = plan.blocks(info, j)[2]
    lane = lax.broadcasted_iota(jnp.int32, (height, breadth), 1)
    line = lax.broadcasted_iota(jnp.int32, (height, breadth), 0)
    vacuum = (line < offset_y) & (info[1] == 0)
    use_near = lane >= column
    return [jnp.where(vacuum, 0.0, jnp.where(use_near, near[part], far[part])) for part in range(2)]


def patch_kernel(plan, j, info, delta, own_pieces, other_pieces, patch, near, far, scratch, sems):
    height, breadth = near.shape[1], near.shape[2]
    copies = []
    for index, target in enumerate((near, far)):
        first = pl.multiple_of(plan.blocks(info, j)[index] * breadth, breadth)
        copies.append(pltpu.make_async_copy(delta.at[0, :, :, pl.ds(first, breadth)], target, sems.at[index]))
        copies[-1].start()
    for copy in copies:
        copy.wait()
    real, imag = window_delta(info, plan, j, near, far)
    scratch[0] = real + 1.0
    scratch[1] = imag
    first = pl.multiple_of(info[0] * (height // 2), height // 2)
    patch[:2] = scratch[:, pl.ds(first, height // 2), :]
    batch, probe = plan.served(info, j)
    patch[2] = jnp.where(batch == info[0], own_pieces[probe], other_pieces[probe])


def launch_kernel(
    plan, j, info, near, far, above, above_other, probe, table, twiddle, message, rolled
):
    height, breadth = near.shape[2], near.shape[3]
    quarter = breadth // 4
    real, imag = window_delta(info, plan, j, near.at[0], far.at[0])
    transmit = (real + 1.0, imag)
    offset_y = plan.offsets(info, j)[0]
    column = plan.blocks(info, j)[2]
    lower = info[0] == 0
    entering = []
    for part in range(2):
        first, second = above[part], above_other[part]
        pieces = [jnp.where(lower, first, second), jnp.where(lower, second, first), probe[part]]
        lines = pltpu.roll(jnp.concatenate(pieces, axis=0), offset_y, 0)[height:]
        entering.append(pltpu.roll(lines, column, 1))
        rolled[part] = entering[part]
    value = times(entering, transmit)
    quarters = [tuple(item[:, quarter * m : quarter * (m + 1)] for item in value) for m in range(4)]
    classes = scatter4(quarters)
    packed = []
    for index in range(2):
        chosen = tuple(jnp.where(lower, classes[index][i], classes[index + 2][i]) for i in range(2))
        low, high = lane_twiddle(twiddle, index), lane_twiddle(twiddle, index + 2)
        factor = tuple(jnp.where(lower, low[i], high[i]) for i in range(2))
        packed.append(jnp.concatenate(conj_times(factor, chosen), axis=1))
    result = right_dot(jnp.concatenate(packed, axis=0), table)
    for index in range(2):
        block = result[height * index : height * (index + 1)]
        message[0, :, quarter * index : quarter * (index + 1)] = block[:, :quarter]
        message[1, :, quarter * index : quarter * (index + 1)] = block[:, quarter:]


def settle_kernel(plan, info, table, twiddle, *refs):
    number = plan.number
    own_spectra, other_spectra = refs[:number], refs[number : 2 * number]
    own_terms, other_terms = refs[2 * number : 3 * number], refs[3 * number : 4 * number]
    rolled = refs[4 * number : 5 * number]
    out, scratch = refs[5 * number :]
    height, breadth = scratch.shape[1], scratch.shape[2]
    quarter = breadth // 4
    lower = info[0] == 0
    lane = lax.broadcasted_iota(jnp.int32, (height, breadth), 1)
    line = lax.broadcasted_iota(jnp.int32, (height, breadth), 0)
    out[...] = jnp.zeros_like(out)
    for j in range(number):

        @pl.when(info[2] == 0)
        def _():
            classes = []
            for index in range(4):
                first = quarter * (index % 2)
                pair = []
                for part in range(2):
                    own = own_spectra[j][part, :, first : first + quarter]
                    other = other_spectra[j][part, :, first : first + quarter]
                    pair.append(jnp.where(lower, own, other) if index < 2 else jnp.where(lower, other, own))
                classes.append(tuple(pair))
            inner = inverse_lanes(classes, table, twiddle)
            for m in range(4):
                columns = slice(quarter * m, quarter * (m + 1))
                entering = (rolled[j][0, :, columns], rolled[j][1, :, columns])
                term = conj_times(entering, inner[m])
                scratch[0, :, columns] = term[0]
                scratch[1, :, columns] = term[1]

        @pl.when(info[2] != 0)
        def _():
            own, other = own_terms[j][...], other_terms[j][...]
            scratch[:, : height // 2, :] = jnp.where(lower, own, other)
            scratch[:, height // 2 :, :] = jnp.where(lower, other, own)

        near_block, far_block, column = plan.blocks(info, j)
        present = (line >= plan.offsets(info, j)[0]) | (info[1] != 0)
        near = pl.ds(pl.multiple_of(near_block * breadth, breadth), breadth)
        far = pl.ds(pl.multiple_of(far_block * breadth, breadth), breadth)
        use_near = lane >= column
        for part in range(2):
            term = jnp.where(present, scratch[part], 0.0)
            out[0, part, :, near] += jnp.where(use_near, term, 0.0)
            out[0, part, :, far] += jnp.where(use_near, 0.0, term)


def split_lines(value, lower, count):
    height = value.shape[0] // count
    firsts, seconds = [], []
    for index in range(count):
        first = value[height * index : height * index + height // 2]
        second = value[height * index + height // 2 : height * (index + 1)]
        firsts.append(jnp.where(lower, first, second))
        seconds.append(jnp.where(lower, second, first))
    return joined(firsts, 0), joined(seconds, 0)


def merge_lines(own, other, lower, count):
    height = own.shape[0] // count
    parts = []
    for index in range(count):
        first = own[height * index : height * (index + 1)]
        second = other[height * index : height * (index + 1)]
        parts.append(jnp.where(lower, first, second))
        parts.append(jnp.where(lower, second, first))
    return jnp.concatenate(parts, axis=0)


def tiles(width):
    quarter = width // 2
    return [slice(quarter * index, quarter * (index + 1)) for index in range(2)]


def merged_quarters(own, other, lower, count, columns):
    lines = own.shape[1] // 4
    quarters = []
    for m in range(4):
        rows = slice(lines * m, lines * (m + 1))
        quarters.append(
            tuple(merge_lines(own[part, rows, columns], other[part, rows, columns], lower, count) for part in range(2))
        )
    return quarters


def hand_over(quarters, lower, count, columns, keep, send):
    lines = keep.shape[1] // 4
    for m in range(4):
        rows = slice(lines * m, lines * (m + 1))
        for part in range(2):
            keep[part, rows, columns], send[part, rows, columns] = split_lines(quarters[m][part], lower, count)


def filtered(classes, field, conjugate, columns):
    quarter = classes[0][0].shape[0]
    result = []
    for index in range(4):
        rows = slice(quarter * index, quarter * (index + 1))
        factor = (field[0, rows, columns], field[1, rows, columns])
        result.append((conj_times if conjugate else times)(factor, classes[index]))
    return result


def enter_kernel(number, info, forward, inverse, twiddle, field, *refs):
    blocks, (keep, send) = refs[:number], refs[number:]
    lower = info[0] == 0
    count = number // 4
    for columns in tiles(keep.shape[2]):
        quarters = [
            tuple(
                joined([blocks[count * m + i][part, :, columns] for i in range(count)], 0) for part in range(2)
            )
            for m in range(4)
        ]
        far = filtered(forward_rows(quarters, forward, twiddle), field, False, columns)
        hand_over(inverse_rows(far, inverse, twiddle), lower, count, columns, keep, send)


def through_kernel(number, conjugate, info, forward, inverse, twiddle, field, own, other, keep, send):
    lower = info[0] == 0
    count = number // 4
    for columns in tiles(keep.shape[2]):
        far = forward_rows(merged_quarters(own, other, lower, count, columns), forward, twiddle)
        far = filtered(far, field, conjugate, columns)
        hand_over(inverse_rows(far, inverse, twiddle), lower, count, columns, keep, send)


def residual_kernel(number, info, forward, inverse, twiddle, target, own, other, keep, send):
    lower = info[0] == 0
    count = number // 4
    for columns in tiles(keep.shape[2]):
        far = forward_rows(merged_quarters(own, other, lower, count, columns), forward, twiddle)
        quarter = far[0][0].shape[0]
        seeded = []
        for index in range(4):
            real, imag = far[index]
            residual = real * real + imag * imag - target[quarter * index : quarter * (index + 1), columns]
            seeded.append((residual * real, residual * imag))
        hand_over(inverse_rows(seeded, inverse, twiddle), lower, count, columns, keep, send)


def leave_kernel(number, info, forward, inverse, twiddle, field, own, other, *blocks):
    lower = info[0] == 0
    count = number // 4
    height = blocks[0].shape[1]
    for columns in tiles(own.shape[2]):
        far = forward_rows(merged_quarters(own, other, lower, count, columns), forward, twiddle)
        quarters = inverse_rows(filtered(far, field, True, columns), inverse, twiddle)
        for m in range(4):
            for i in range(count):
                for part in range(2):
                    blocks[count * m + i][part, :, columns] = quarters[m][part][height * i : height * (i + 1)]


def lane_classes(own, other, lower, rows):
    quarter = own.shape[2] // 2
    classes = []
    for index in range(4):
        columns = slice(quarter * (index % 2), quarter * (index % 2) + quarter)
        pair = []
        for part in range(2):
            first, second = own[part, rows, columns], other[part, rows, columns]
            pair.append(jnp.where(lower, first, second) if index < 2 else jnp.where(lower, second, first))
        classes.append(tuple(pair))
    return classes


def lanes_out(classes, lower, rows, keep, send):
    quarter = keep.shape[2] // 2
    for index in range(2):
        columns = slice(quarter * index, quarter * (index + 1))
        for part in range(2):
            low, high = classes[index][part], classes[index + 2][part]
            keep[part, rows, columns] = jnp.where(lower, low, high)
            send[part, rows, columns] = jnp.where(lower, high, low)


def meet_kernel(plan, info, forward, inverse, twiddle, own, other, *refs):
    number = plan.number
    patches, (entering, keep, send) = refs[:number], refs[number:]
    lower = info[0] == 0
    count = number // 4
    lines = own.shape[1] // 4
    quarter = own.shape[2] // 2
    for m in range(4):
        rows = slice(lines * m, lines * (m + 1))
        group = patches[count * m : count * (m + 1)]
        wave = inverse_lanes(lane_classes(own, other, lower, rows), inverse, twiddle)
        quarters = []
        for piece in range(4):
            columns = slice(quarter * piece, quarter * (piece + 1))
            transmit = tuple(joined([patch[part, :, columns] for patch in group], 0) for part in range(2))
            entering[0, rows, columns] = wave[piece][0]
            entering[1, rows, columns] = wave[piece][1]
            quarters.append(times(wave[piece], transmit))
        lanes_out(forward_lanes(quarters, forward, twiddle), lower, rows, keep, send)


def grade_kernel(plan, info, inverse, twiddle, own, other, entering, *refs):
    number = plan.number
    patches, terms, leaving = refs[:number], refs[number : 2 * number], refs[2 * number]
    lower = info[0] == 0
    count = number // 4
    lines = own.shape[1] // 4
    height = lines // count
    quarter = own.shape[2] // 2
    for m in range(4):
        rows = slice(lines * m, lines * (m + 1))
        group = patches[count * m : count * (m + 1)]
        inner = inverse_lanes(lane_classes(own, other, lower, rows), inverse, twiddle)
        for piece in range(4):
            columns = slice(quarter * piece, quarter * (piece + 1))
            transmit = tuple(joined([patch[part, :, columns] for patch in group], 0) for part in range(2))
            wave = (entering[0, rows, columns], entering[1, rows, columns])
            term = conj_times(wave, inner[piece])
            for i in range(count):
                for part in range(2):
                    terms[count * m + i][part, :, columns] = term[part][height * i : height * (i + 1)]
            behind = conj_times(transmit, inner[piece])
            leaving[0, rows, columns] = behind[0]
            leaving[1, rows, columns] = behind[1]


def onward_kernel(info, forward, twiddle, leaving, keep, send):
    lower = info[0] == 0
    lines = leaving.shape[1] // 4
    quarter = leaving.shape[2] // 4
    for m in range(4):
        rows = slice(lines * m, lines * (m + 1))
        quarters = [
            tuple(leaving[part, rows, quarter * piece : quarter * (piece + 1)] for part in range(2))
            for piece in range(4)
        ]
        lanes_out(forward_lanes(quarters, forward, twiddle), lower, rows, keep, send)


def after(value, *others):
    return lax.optimization_barrier((value, *others))[0]


def on_device(probe, object_delta, measured, pos_y, pos_x, prop_phase):
    number = lax.axis_size("row")
    sections = lax.axis_size("sect")
    cores = lax.axis_size("batch")
    place, section, core = (lax.axis_index(axis) for axis in line_axes)
    height, breadth = probe.shape[1], probe.shape[2]
    spans = object_delta.shape[3] // breadth
    half, wide = height // 2, breadth // 2
    plan = Plan(number, sections, cores, measured.shape[1], spans, breadth)
    total = plan.total
    home_z = [plan.home(q)[0] for q in range(total)]
    home_x = [plan.home(q)[1] for q in range(total)]
    base = [plan.base(q) for q in range(total)]
    assert len(set(base)) == total

    def spot(z, x, c):
        return (z * sections + x) * cores + c

    every = [(q, c) for q in range(total) for c in range(cores)]

    def inward(j, layer):
        return [
            (spot((base[q] + j) % number, layer, c), spot(home_z[q], home_x[q], c)) for q, c in every
        ]

    def outward(j, layer):
        return [(target, source) for source, target in inward(j, layer)]

    def move(value, pairs):
        return lax.ppermute(value, line_axes, pairs)

    def swap(value):
        return lax.ppermute(value, "batch", [(i, (i + 1) % cores) for i in range(cores)])

    column_forward, column_inverse = (jnp.asarray(table) for table in column_tables(breadth))
    row_forward, row_inverse = (jnp.asarray(table) for table in row_tables(breadth))
    lane_factors, line_factors = (jnp.asarray(table) for table in twiddles(breadth))

    params = pltpu.CompilerParams(vmem_limit_bytes=vmem_bytes)
    def beside(*vectors):
        sizes = [value.shape[0] for value in vectors]
        return sum(
            jnp.pad(value, (sum(sizes[:i]), sum(sizes[i + 1 :]))) for i, value in enumerate(vectors)
        ).astype(jnp.int32)

    own_positions = beside(pos_y[0], pos_x[0])
    about = jnp.stack([core, place, section]).astype(jnp.int32)
    info = beside(about, own_positions, swap(own_positions))
    part = jnp.where(after(core, own_positions) == 0, probe[:, :half], probe[:, half:])
    above = lax.ppermute(part, "row", [(i, (i + 1) % number) for i in range(number)])

    def whole(shape):
        return pl.BlockSpec(tuple(shape), lambda i, *_: (0,) * len(shape))

    def floats(*shape):
        return jax.ShapeDtypeStruct(shape, jnp.float32)

    pieces_shape = (plan.own_probes, half, breadth)
    hbm = pl.BlockSpec(memory_space=pltpu.MemorySpace.HBM)
    phase_piece, own_pieces, other_pieces = pl.pallas_call(
        prepare_kernel,
        out_shape=[floats(half, breadth), floats(*pieces_shape), floats(*pieces_shape)],
        in_specs=[pl.BlockSpec(memory_space=smem), hbm, hbm],
        out_specs=[pl.BlockSpec(memory_space=pltpu.VMEM)] * 3,
        scratch_shapes=[
            pltpu.VMEM((height, breadth), jnp.float32),
            pltpu.VMEM((plan.own_probes, height, breadth), jnp.float32),
            pltpu.VMEM((breadth // 128, height, 128), jnp.float32),
            pltpu.SemaphoreType.DMA((1 + plan.own_probes,)),
        ],
        cost_estimate=light,
        compiler_params=params,
    )(after(about, part), prop_phase, measured)
    other_pieces = swap(other_pieces)

    phases = [phase_piece]
    while len(phases) < number:
        step = len(phases)
        if step > 1:
            moved = jnp.stack(phases)
        else:
            moved = phases[0][None]
        if 2 * step < number:
            moved = lax.ppermute(moved, "row", [(i, (i + step) % number) for i in range(number)])
        else:
            moved = move(moved, [(spot((home_z[q] - step) % number, home_x[q], c), spot(home_z[q], home_x[q], c)) for q, c in every])
        phases = phases + [moved[i] for i in range(step)]
    phases = phases[::-1]

    def near_spec(j, far):
        return pl.BlockSpec(
            (1, 2, height, breadth), lambda i, info: (0, 0, 0, plan.blocks(info, j)[1 if far else 0])
        )

    def patch_of(j, info):
        return pl.pallas_call(
            functools.partial(patch_kernel, plan, j),
            out_shape=floats(3, half, breadth),
            in_specs=[pl.BlockSpec(memory_space=smem), hbm] + [pl.BlockSpec(memory_space=pltpu.VMEM)] * 2,
            out_specs=pl.BlockSpec(memory_space=pltpu.VMEM),
            scratch_shapes=[pltpu.VMEM((2, height, breadth), jnp.float32)] * 3 + [pltpu.SemaphoreType.DMA((2,))],
            cost_estimate=light,
            compiler_params=params,
        )(info, object_delta, own_pieces, other_pieces)

    def launch_of(j, info):
        return pl.pallas_call(
            functools.partial(launch_kernel, plan, j),
            out_shape=[floats(2, height, wide), floats(2, height, breadth)],
            grid_spec=pltpu.PrefetchScalarGridSpec(
                num_scalar_prefetch=1,
                grid=(1,),
                in_specs=[
                    near_spec(j, False),
                    near_spec(j, True),
                    whole(above.shape),
                    whole(above.shape),
                    whole(probe.shape),
                    whole(row_forward.shape),
                    whole(lane_factors.shape),
                ],
                out_specs=[whole((2, height, wide)), whole((2, height, breadth))],
            ),
            cost_estimate=light,
            compiler_params=params,
        )(
            info,
            object_delta,
            object_delta,
            above,
            above_other,
            probe,
            row_forward,
            lane_factors,
        )

    later = range(1, sections)
    own_patches = []
    for j in range(number):
        own_patches.append(patch_of(j, info if j == 0 else after(info, own_patches[-1])))
    above_other = swap(above)
    launched = []
    for j in range(number):
        ready = [launched[j - 1][0]] if j else []
        if j == number - 1:
            ready.append(phases[0])
        launched.append(launch_of(j, after(info, *ready) if ready else info))
    patches = {layer: [] for layer in later}
    blocks = []
    for j in range(number):
        value, message = own_patches[j], launched[j][0]
        if j == 0:
            value = after(value, message)
        if j >= 2:
            value = after(value, launched[-1][0], *(patches[layer][j - 2] for layer in later))
            message = after(message, blocks[j - 2])
        for layer in later:
            patches[layer].append(move(value, inward(j, layer)))
        blocks.append(move(message, inward(j, 0)))
    rolled = [launched[j][1] for j in range(number)]
    arrived = (*blocks, *(patches[layer][j] for layer in later for j in range(number)))
    blocks = lax.optimization_barrier(arrived)[:number]

    traded = (2, wide, wide)
    column_set = (column_forward, column_inverse, line_factors)
    row_set = (row_forward, row_inverse, lane_factors)

    def at_home(kernel, outs, *operands):
        return pl.pallas_call(
            kernel,
            out_shape=[floats(*shape) for shape in outs],
            in_specs=[pl.BlockSpec(memory_space=smem)] + [pl.BlockSpec(memory_space=pltpu.VMEM)] * len(operands),
            out_specs=[pl.BlockSpec(memory_space=pltpu.VMEM)] * len(outs),
            cost_estimate=light,
            compiler_params=params,
        )(about, *operands)

    def through(conjugate, own, other):
        kernel = functools.partial(through_kernel, number, conjugate)
        return at_home(kernel, [traded, traded], *column_set, field, own, other)

    entries = {}
    field = at_home(filter_kernel, [(2, breadth, wide)], after(phases[0], launched[-1][0]), *phases[1:])[0]
    keep, send = at_home(
        functools.partial(enter_kernel, number), [traded, traded], *column_set, field, *blocks
    )
    target = at_home(functools.partial(target_kernel, plan), [(breadth, wide)], *patches[1])[0]
    for layer in later:
        other = swap(send)
        entries[layer], keep, send = at_home(
            functools.partial(meet_kernel, plan),
            [(2, wide, breadth), traded, traded],
            *row_set,
            keep,
            other,
            *patches[layer],
        )
        other = swap(send)
        if layer < sections - 1:
            keep, send = through(False, keep, other)
    keep, send = at_home(
        functools.partial(residual_kernel, number), [traded, traded], *column_set, target, keep, other
    )

    terms = None
    for layer in reversed(later):
        other = swap(send)
        found = at_home(
            functools.partial(grade_kernel, plan),
            [(2, half, breadth)] * number + [(2, wide, breadth)],
            row_inverse,
            lane_factors,
            keep,
            other,
            entries[layer],
            *patches[layer],
        )
        keep, send = at_home(onward_kernel, [traded, traded], row_forward, lane_factors, found[number])
        other = swap(send)
        if layer > 1:
            came = [move(found[j], outward(j, layer)) for j in range(number)]
            terms = came if terms is None else [first + second for first, second in zip(terms, came)]
            keep, send = through(True, keep, other)
    leaving = at_home(
        functools.partial(leave_kernel, number), [(2, height, wide)] * number, *column_set, field, keep, other
    )
    came, spectra = [None] * number, [None] * number
    for j in plan.order:
        came[j] = move(after(found[j], other), outward(j, 1))
    for j in plan.order:
        spectra[j] = move(leaving[j], outward(j, 0))
    terms = came if terms is None else [first + second for first, second in zip(terms, came)]

    operands = [
        row_inverse,
        lane_factors,
        *spectra,
        *(swap(value) for value in spectra),
        *terms,
        *(swap(value) for value in terms),
        *rolled,
    ]
    return pl.pallas_call(
        functools.partial(settle_kernel, plan),
        out_shape=jax.ShapeDtypeStruct(object_delta.shape, jnp.float32),
        in_specs=[pl.BlockSpec(memory_space=smem)] + [pl.BlockSpec(memory_space=pltpu.VMEM)] * len(operands),
        out_specs=pl.BlockSpec(memory_space=pltpu.VMEM),
        scratch_shapes=[pltpu.VMEM((2, height, breadth), jnp.float32)],
        cost_estimate=light,
        compiler_params=params,
    )(info, *operands)


def solution(mesh):
    in_specs = (
        P(None, "row", None),
        P(("groups", "sect"), None, "row", None),
        P(("groups", "batch"), None, "row", None),
        P(("groups", "batch"), None),
        P(("groups", "batch"), None),
        P("row", None),
    )
    out_specs = P(("groups", "sect"), None, "row", None)
    return jax.shard_map(
        on_device, mesh=mesh, in_specs=in_specs, out_specs=out_specs, check_vma=False
    )
```

```python
import functools
import math

import jax
import jax.numpy as jnp
import ml_dtypes
import numpy as np
from jax import lax
from jax.experimental import pallas as pl
from jax.experimental.pallas import tpu as pltpu
from jax.sharding import PartitionSpec as P

highest = lax.Precision.HIGHEST
line_axes = ("row", "sect", "batch")
vmem_bytes = 20 * 1024 * 1024
light = pl.CostEstimate(flops=0, transcendentals=0, bytes_accessed=0)
smem = pltpu.MemorySpace.SMEM


def halves(table, axis):
    table = table.astype(np.float64)
    upper = table.astype(ml_dtypes.bfloat16)
    lower = (table - upper.astype(np.float64)).astype(ml_dtypes.bfloat16)
    return np.concatenate([upper, upper, lower], axis=axis)


def circle(length):
    quarter = length // 4
    index = np.arange(quarter)
    angles = (index[:, None] * index[None, :] % quarter) * (2.0 * math.pi / quarter)
    scale = 1.0 / math.sqrt(length)
    return np.cos(angles) * scale, np.sin(angles) * scale


def column_tables(length):
    cosine, sine = circle(length)
    forward = np.block([[cosine, sine], [-sine, cosine]])
    inverse = np.block([[cosine, -sine], [sine, cosine]])
    return halves(forward, 1), halves(inverse, 1)


def row_tables(length):
    cosine, sine = circle(length)
    forward = np.block([[cosine, -sine], [sine, cosine]])
    inverse = np.block([[cosine.T, sine.T], [-sine.T, cosine.T]])
    return halves(forward, 0), halves(inverse, 0)


def twiddles(length):
    quarter = length // 4
    angles = np.arange(4)[:, None] * np.arange(quarter)[None, :] * (2.0 * math.pi / length)
    pairs = np.stack([np.cos(angles), np.sin(angles)], axis=1).astype(np.float32)
    along_lanes = pairs.reshape(8, quarter)
    along_rows = np.broadcast_to(pairs[..., None], (4, 2, quarter, 128)).copy()
    return along_lanes, along_rows


def circle_polynomials(reach):
    grid = np.cos((np.arange(64) + 0.5) * math.pi / 64.0)
    square = (grid + 1.0) * 0.5 * reach * reach
    root = np.sqrt(square)
    found = []
    for values in (np.cos(root), np.sinc(root / math.pi)):
        fitted = np.polynomial.Polynomial.fit(square, values, 9, domain=[0.0, reach * reach])
        found.append([float(item) for item in fitted.convert().coef])
    return found


def split(value):
    upper = value.astype(jnp.bfloat16)
    lower = (value - upper.astype(jnp.float32)).astype(jnp.bfloat16)
    return upper, lower


def dot(first, second):
    return jnp.dot(first, second, preferred_element_type=jnp.float32)


def right_dot(value, table):
    upper, lower = split(value)
    return dot(jnp.concatenate([upper, lower, upper], axis=1), table[...])


def left_dot(table, value):
    upper, lower = split(value)
    return dot(table[...], jnp.concatenate([upper, lower, upper], axis=0))


def times(first, second):
    return (
        first[0] * second[0] - first[1] * second[1],
        first[0] * second[1] + first[1] * second[0],
    )


def conj_times(first, second):
    return (
        first[0] * second[0] + first[1] * second[1],
        first[0] * second[1] - first[1] * second[0],
    )


def plus(first, second):
    return (first[0] + second[0], first[1] + second[1])


def minus(first, second):
    return (first[0] - second[0], first[1] - second[1])


def turned(value):
    return (-value[1], value[0])


def scatter4(parts):
    sum02, dif02 = plus(parts[0], parts[2]), minus(parts[0], parts[2])
    sum13, dif13 = plus(parts[1], parts[3]), turned(minus(parts[1], parts[3]))
    return [plus(sum02, sum13), minus(dif02, dif13), minus(sum02, sum13), plus(dif02, dif13)]


def gather4(parts):
    sum02, dif02 = plus(parts[0], parts[2]), minus(parts[0], parts[2])
    sum13, dif13 = plus(parts[1], parts[3]), turned(minus(parts[1], parts[3]))
    return [plus(sum02, sum13), plus(dif02, dif13), minus(sum02, sum13), minus(dif02, dif13)]


def lane_twiddle(reference, index):
    return (reference[2 * index : 2 * index + 1, :], reference[2 * index + 1 : 2 * index + 2, :])


def forward_lanes(quarters, table, twiddle):
    rows = quarters[0][0].shape[0]
    classes = scatter4(quarters)
    packed = []
    for index, value in enumerate(classes):
        if index > 0:
            value = conj_times(lane_twiddle(twiddle, index), value)
        packed.append(jnp.concatenate(value, axis=1))
    result = right_dot(jnp.concatenate(packed, axis=0), table)
    half = result.shape[1] // 2
    return [
        (result[rows * index : rows * (index + 1), :half], result[rows * index : rows * (index + 1), half:])
        for index in range(4)
    ]


def inverse_lanes(classes, table, twiddle):
    rows = classes[0][0].shape[0]
    packed = jnp.concatenate([jnp.concatenate(value, axis=1) for value in classes], axis=0)
    result = right_dot(packed, table)
    half = result.shape[1] // 2
    parts = []
    for index in range(4):
        value = (result[rows * index : rows * (index + 1), :half], result[rows * index : rows * (index + 1), half:])
        if index > 0:
            value = times(lane_twiddle(twiddle, index), value)
        parts.append(value)
    return gather4(parts)


def forward_rows(quarters, table, twiddle):
    lanes = quarters[0][0].shape[1]
    packed = []
    for index, value in enumerate(scatter4(quarters)):
        if index > 0:
            value = conj_times((twiddle[index, 0], twiddle[index, 1]), value)
        packed.append(jnp.concatenate(value, axis=0))
    result = left_dot(table, jnp.concatenate(packed, axis=1))
    half = result.shape[0] // 2
    return [
        (result[:half, lanes * index : lanes * (index + 1)], result[half:, lanes * index : lanes * (index + 1)])
        for index in range(4)
    ]


def inverse_rows(classes, table, twiddle):
    lanes = classes[0][0].shape[1]
    packed = jnp.concatenate([jnp.concatenate(value, axis=0) for value in classes], axis=1)
    result = left_dot(table, packed)
    half = result.shape[0] // 2
    parts = []
    for index in range(4):
        value = (result[:half, lanes * index : lanes * (index + 1)], result[half:, lanes * index : lanes * (index + 1)])
        if index > 0:
            value = times((twiddle[index, 0], twiddle[index, 1]), value)
        parts.append(value)
    return gather4(parts)


def joined(parts, axis):
    return parts[0] if len(parts) == 1 else jnp.concatenate(parts, axis=axis)


class Plan:
    def __init__(self, number, sections, cores, own_probes, spans, breadth):
        assert own_probes == sections and spans > 1
        self.number, self.sections, self.cores = number, sections, cores
        self.own_probes, self.spans, self.breadth = own_probes, spans, breadth
        self.stride = number // sections
        assert self.stride >= cores
        self.top = (number - cores) // 2
        self.total = cores * own_probes
        self.order = [j for pair in zip(range(number // 2), range(number // 2, number)) for j in pair]

    def home(self, q):
        return self.top + q // self.sections, q % self.sections

    def base(self, q):
        z, x = self.home(q)
        return (z + self.stride * x) % self.number

    def own_base(self, info):
        return lax.rem(info[1] + self.stride * info[2], self.number)

    def served(self, info, j):
        step = lax.rem(info[1] - j - self.top + 2 * self.number, self.number)
        return jnp.minimum(lax.rem(step, self.stride), self.cores - 1), lax.div(step, self.stride)

    def offsets(self, info, j):
        batch, probe = self.served(info, j)
        spot = 3 + probe + jnp.where(batch == info[0], 0, 2 * self.own_probes)
        return info[spot], info[spot + self.own_probes]

    def blocks(self, info, j):
        column = self.offsets(info, j)[1]
        near = lax.div(column, self.breadth)
        far = jnp.where(near + 1 < self.spans, near + 1, near - 1)
        return near, far, lax.rem(column, self.breadth)


def prepare_kernel(info, phase_hbm, measured_hbm, phase_piece, own_pieces, other_pieces, phase, measured, scratch, sems):
    rows = phase.shape[0] // 4
    width = scratch.shape[2]
    tasks = [(pltpu.make_async_copy(phase_hbm, phase, sems.at[0]), phase, (phase_piece,))]
    for probe in range(measured.shape[0]):
        copy = pltpu.make_async_copy(measured_hbm.at[0, probe], measured.at[probe], sems.at[1 + probe])
        tasks.append((copy, measured.at[probe], (own_pieces.at[probe], other_pieces.at[probe])))
    for copy, _, _ in tasks:
        copy.start()
    for copy, source, targets in tasks:
        copy.wait()
        for tile in range(phase.shape[1] // width):
            columns = slice(width * tile, width * (tile + 1))
            scratch[tile] = source[:, columns]
            for index in range(2):
                part = slice(rows * index, rows * (index + 1))
                for flip, target in enumerate(targets):
                    low = scratch[tile, pl.ds(2 * flip + index, rows, stride=4), :]
                    high = scratch[tile, pl.ds(2 - 2 * flip + index, rows, stride=4), :]
                    target[part, columns] = jnp.where(info[0] == 0, low, high)


def exact_turn(value):
    length = value.shape[1]
    quarter = length // 4
    row = lax.broadcasted_iota(jnp.int32, (length, length), 0)
    column = lax.broadcasted_iota(jnp.int32, (length, length), 1)
    wanted = 4 * lax.rem(row, quarter) + lax.div(row, quarter)
    order = (wanted == column).astype(jnp.float32).astype(jnp.bfloat16)
    first = value.astype(jnp.bfloat16)
    rest = value - first.astype(jnp.float32)
    second = rest.astype(jnp.bfloat16)
    third = (rest - second.astype(jnp.float32)).astype(jnp.bfloat16)
    dims = (((1,), (1,)), ((), ()))
    parts = [
        lax.dot_general(order, item, dims, preferred_element_type=jnp.float32) for item in (first, second, third)
    ]
    return (parts[0] + parts[1]) + parts[2]


def class_rows(pieces, index):
    rows = pieces[0].shape[0] // 2
    return joined([piece[rows * index : rows * (index + 1), :] for piece in pieces], 0)


def polynomial(coefficients, value):
    result = jnp.full_like(value, coefficients[-1])
    for item in coefficients[-2::-1]:
        result = result * value + item
    return result


def filter_kernel(info, *refs):
    pieces, field = refs[:-1], refs[-1]
    cosine, sine = circle_polynomials(3.1416)
    quarter = field.shape[2] // 2
    rows = pieces[0].shape[0] // 2
    shift = lax.rem((info[1] + 1) * rows, quarter)
    for index in range(2):
        columns = slice(quarter * index, quarter * (index + 1))
        phase = pltpu.roll(exact_turn(class_rows(pieces, index)), shift, 1)
        square = phase * phase
        field[0, :, columns] = polynomial(cosine, square)
        field[1, :, columns] = polynomial(sine, square) * phase


def target_kernel(plan, info, *refs):
    pieces, target = refs[:-1], refs[-1]
    quarter = target.shape[1] // 2
    shift = plan.own_base(info) * (pieces[0].shape[1] // 2)
    for index in range(2):
        columns = slice(quarter * index, quarter * (index + 1))
        lines = class_rows([piece.at[2] for piece in pieces], index)
        target[:, columns] = pltpu.roll(exact_turn(lines), shift, 1)


def window_delta(info, plan, j, near, far):
    height, breadth = near.shape[1], near.shape[2]
    offset_y = plan.offsets(info, j)[0]
    column = plan.blocks(info, j)[2]
    lane = lax.broadcasted_iota(jnp.int32, (height, breadth), 1)
    line = lax.broadcasted_iota(jnp.int32, (height, breadth), 0)
    vacuum = (line < offset_y) & (info[1] == 0)
    use_near = lane >= column
    return [jnp.where(vacuum, 0.0, jnp.where(use_near, near[part], far[part])) for part in range(2)]


def patch_kernel(plan, j, info, delta, own_pieces, other_pieces, patch, near, far, scratch, sems):
    height, breadth = near.shape[1], near.shape[2]
    copies = []
    for index, target in enumerate((near, far)):
        first = pl.multiple_of(plan.blocks(info, j)[index] * breadth, breadth)
        copies.append(pltpu.make_async_copy(delta.at[0, :, :, pl.ds(first, breadth)], target, sems.at[index]))
        copies[-1].start()
    for copy in copies:
        copy.wait()
    real, imag = window_delta(info, plan, j, near, far)
    scratch[0] = real + 1.0
    scratch[1] = imag
    first = pl.multiple_of(info[0] * (height // 2), height // 2)
    patch[:2] = scratch[:, pl.ds(first, height // 2), :]
    batch, probe = plan.served(info, j)
    patch[2] = jnp.where(batch == info[0], own_pieces[probe], other_pieces[probe])


def launch_kernel(
    plan, j, info, near, far, above, above_other, probe, table, twiddle, message, rolled
):
    height, breadth = near.shape[2], near.shape[3]
    quarter = breadth // 4
    real, imag = window_delta(info, plan, j, near.at[0], far.at[0])
    transmit = (real + 1.0, imag)
    offset_y = plan.offsets(info, j)[0]
    column = plan.blocks(info, j)[2]
    lower = info[0] == 0
    entering = []
    for part in range(2):
        first, second = above[part], above_other[part]
        pieces = [jnp.where(lower, first, second), jnp.where(lower, second, first), probe[part]]
        lines = pltpu.roll(jnp.concatenate(pieces, axis=0), offset_y, 0)[height:]
        entering.append(pltpu.roll(lines, column, 1))
        rolled[part] = entering[part]
    value = times(entering, transmit)
    quarters = [tuple(item[:, quarter * m : quarter * (m + 1)] for item in value) for m in range(4)]
    classes = scatter4(quarters)
    packed = []
    for index in range(2):
        chosen = tuple(jnp.where(lower, classes[index][i], classes[index + 2][i]) for i in range(2))
        low, high = lane_twiddle(twiddle, index), lane_twiddle(twiddle, index + 2)
        factor = tuple(jnp.where(lower, low[i], high[i]) for i in range(2))
        packed.append(jnp.concatenate(conj_times(factor, chosen), axis=1))
    result = right_dot(jnp.concatenate(packed, axis=0), table)
    for index in range(2):
        block = result[height * index : height * (index + 1)]
        message[0, :, quarter * index : quarter * (index + 1)] = block[:, :quarter]
        message[1, :, quarter * index : quarter * (index + 1)] = block[:, quarter:]


def settle_kernel(plan, info, table, twiddle, *refs):
    number = plan.number
    own_spectra, other_spectra = refs[:number], refs[number : 2 * number]
    own_terms, other_terms = refs[2 * number : 3 * number], refs[3 * number : 4 * number]
    rolled = refs[4 * number : 5 * number]
    out, scratch = refs[5 * number :]
    height, breadth = scratch.shape[1], scratch.shape[2]
    quarter = breadth // 4
    lower = info[0] == 0
    lane = lax.broadcasted_iota(jnp.int32, (height, breadth), 1)
    line = lax.broadcasted_iota(jnp.int32, (height, breadth), 0)
    out[...] = jnp.zeros_like(out)
    for j in range(number):

        @pl.when(info[2] == 0)
        def _():
            classes = []
            for index in range(4):
                first = quarter * (index % 2)
                pair = []
                for part in range(2):
                    own = own_spectra[j][part, :, first : first + quarter]
                    other = other_spectra[j][part, :, first : first + quarter]
                    pair.append(jnp.where(lower, own, other) if index < 2 else jnp.where(lower, other, own))
                classes.append(tuple(pair))
            inner = inverse_lanes(classes, table, twiddle)
            for m in range(4):
                columns = slice(quarter * m, quarter * (m + 1))
                entering = (rolled[j][0, :, columns], rolled[j][1, :, columns])
                term = conj_times(entering, inner[m])
                scratch[0, :, columns] = term[0]
                scratch[1, :, columns] = term[1]

        @pl.when(info[2] != 0)
        def _():
            own, other = own_terms[j][...], other_terms[j][...]
            scratch[:, : height // 2, :] = jnp.where(lower, own, other)
            scratch[:, height // 2 :, :] = jnp.where(lower, other, own)

        near_block, far_block, column = plan.blocks(info, j)
        present = (line >= plan.offsets(info, j)[0]) | (info[1] != 0)
        near = pl.ds(pl.multiple_of(near_block * breadth, breadth), breadth)
        far = pl.ds(pl.multiple_of(far_block * breadth, breadth), breadth)
        use_near = lane >= column
        for part in range(2):
            term = jnp.where(present, scratch[part], 0.0)
            out[0, part, :, near] += jnp.where(use_near, term, 0.0)
            out[0, part, :, far] += jnp.where(use_near, 0.0, term)


def split_lines(value, lower, count):
    height = value.shape[0] // count
    firsts, seconds = [], []
    for index in range(count):
        first = value[height * index : height * index + height // 2]
        second = value[height * index + height // 2 : height * (index + 1)]
        firsts.append(jnp.where(lower, first, second))
        seconds.append(jnp.where(lower, second, first))
    return joined(firsts, 0), joined(seconds, 0)


def merge_lines(own, other, lower, count):
    height = own.shape[0] // count
    parts = []
    for index in range(count):
        first = own[height * index : height * (index + 1)]
        second = other[height * index : height * (index + 1)]
        parts.append(jnp.where(lower, first, second))
        parts.append(jnp.where(lower, second, first))
    return jnp.concatenate(parts, axis=0)


def tiles(width):
    quarter = width // 2
    return [slice(quarter * index, quarter * (index + 1)) for index in range(2)]


def merged_quarters(own, other, lower, count, columns):
    lines = own.shape[1] // 4
    quarters = []
    for m in range(4):
        rows = slice(lines * m, lines * (m + 1))
        quarters.append(
            tuple(merge_lines(own[part, rows, columns], other[part, rows, columns], lower, count) for part in range(2))
        )
    return quarters


def hand_over(quarters, lower, count, columns, keep, send):
    lines = keep.shape[1] // 4
    for m in range(4):
        rows = slice(lines * m, lines * (m + 1))
        for part in range(2):
            keep[part, rows, columns], send[part, rows, columns] = split_lines(quarters[m][part], lower, count)


def filtered(classes, field, conjugate, columns):
    quarter = classes[0][0].shape[0]
    result = []
    for index in range(4):
        rows = slice(quarter * index, quarter * (index + 1))
        factor = (field[0, rows, columns], field[1, rows, columns])
        result.append((conj_times if conjugate else times)(factor, classes[index]))
    return result


def enter_kernel(number, info, forward, inverse, twiddle, field, *refs):
    blocks, (keep, send) = refs[:number], refs[number:]
    lower = info[0] == 0
    count = number // 4
    for columns in tiles(keep.shape[2]):
        quarters = [
            tuple(
                joined([blocks[count * m + i][part, :, columns] for i in range(count)], 0) for part in range(2)
            )
            for m in range(4)
        ]
        far = filtered(forward_rows(quarters, forward, twiddle), field, False, columns)
        hand_over(inverse_rows(far, inverse, twiddle), lower, count, columns, keep, send)


def through_kernel(number, conjugate, info, forward, inverse, twiddle, field, own, other, keep, send):
    lower = info[0] == 0
    count = number // 4
    for columns in tiles(keep.shape[2]):
        far = forward_rows(merged_quarters(own, other, lower, count, columns), forward, twiddle)
        far = filtered(far, field, conjugate, columns)
        hand_over(inverse_rows(far, inverse, twiddle), lower, count, columns, keep, send)


def residual_kernel(number, info, forward, inverse, twiddle, target, own, other, keep, send):
    lower = info[0] == 0
    count = number // 4
    for columns in tiles(keep.shape[2]):
        far = forward_rows(merged_quarters(own, other, lower, count, columns), forward, twiddle)
        quarter = far[0][0].shape[0]
        seeded = []
        for index in range(4):
            real, imag = far[index]
            residual = real * real + imag * imag - target[quarter * index : quarter * (index + 1), columns]
            seeded.append((residual * real, residual * imag))
        hand_over(inverse_rows(seeded, inverse, twiddle), lower, count, columns, keep, send)


def leave_kernel(number, info, forward, inverse, twiddle, field, own, other, *blocks):
    lower = info[0] == 0
    count = number // 4
    height = blocks[0].shape[1]
    for columns in tiles(own.shape[2]):
        far = forward_rows(merged_quarters(own, other, lower, count, columns), forward, twiddle)
        quarters = inverse_rows(filtered(far, field, True, columns), inverse, twiddle)
        for m in range(4):
            for i in range(count):
                for part in range(2):
                    blocks[count * m + i][part, :, columns] = quarters[m][part][height * i : height * (i + 1)]


def lane_classes(own, other, lower, rows):
    quarter = own.shape[2] // 2
    classes = []
    for index in range(4):
        columns = slice(quarter * (index % 2), quarter * (index % 2) + quarter)
        pair = []
        for part in range(2):
            first, second = own[part, rows, columns], other[part, rows, columns]
            pair.append(jnp.where(lower, first, second) if index < 2 else jnp.where(lower, second, first))
        classes.append(tuple(pair))
    return classes


def lanes_out(classes, lower, rows, keep, send):
    quarter = keep.shape[2] // 2
    for index in range(2):
        columns = slice(quarter * index, quarter * (index + 1))
        for part in range(2):
            low, high = classes[index][part], classes[index + 2][part]
            keep[part, rows, columns] = jnp.where(lower, low, high)
            send[part, rows, columns] = jnp.where(lower, high, low)


def meet_kernel(plan, info, forward, inverse, twiddle, own, other, *refs):
    number = plan.number
    patches, (entering, keep, send) = refs[:number], refs[number:]
    lower = info[0] == 0
    count = number // 4
    lines = own.shape[1] // 4
    quarter = own.shape[2] // 2
    for m in range(4):
        rows = slice(lines * m, lines * (m + 1))
        group = patches[count * m : count * (m + 1)]
        wave = inverse_lanes(lane_classes(own, other, lower, rows), inverse, twiddle)
        quarters = []
        for piece in range(4):
            columns = slice(quarter * piece, quarter * (piece + 1))
            transmit = tuple(joined([patch[part, :, columns] for patch in group], 0) for part in range(2))
            entering[0, rows, columns] = wave[piece][0]
            entering[1, rows, columns] = wave[piece][1]
            quarters.append(times(wave[piece], transmit))
        lanes_out(forward_lanes(quarters, forward, twiddle), lower, rows, keep, send)


def grade_kernel(plan, info, inverse, twiddle, own, other, entering, *refs):
    number = plan.number
    patches, terms, leaving = refs[:number], refs[number : 2 * number], refs[2 * number]
    lower = info[0] == 0
    count = number // 4
    lines = own.shape[1] // 4
    height = lines // count
    quarter = own.shape[2] // 2
    for m in range(4):
        rows = slice(lines * m, lines * (m + 1))
        group = patches[count * m : count * (m + 1)]
        inner = inverse_lanes(lane_classes(own, other, lower, rows), inverse, twiddle)
        for piece in range(4):
            columns = slice(quarter * piece, quarter * (piece + 1))
            transmit = tuple(joined([patch[part, :, columns] for patch in group], 0) for part in range(2))
            wave = (entering[0, rows, columns], entering[1, rows, columns])
            term = conj_times(wave, inner[piece])
            for i in range(count):
                for part in range(2):
                    terms[count * m + i][part, :, columns] = term[part][height * i : height * (i + 1)]
            behind = conj_times(transmit, inner[piece])
            leaving[0, rows, columns] = behind[0]
            leaving[1, rows, columns] = behind[1]


def onward_kernel(info, forward, twiddle, leaving, keep, send):
    lower = info[0] == 0
    lines = leaving.shape[1] // 4
    quarter = leaving.shape[2] // 4
    for m in range(4):
        rows = slice(lines * m, lines * (m + 1))
        quarters = [
            tuple(leaving[part, rows, quarter * piece : quarter * (piece + 1)] for part in range(2))
            for piece in range(4)
        ]
        lanes_out(forward_lanes(quarters, forward, twiddle), lower, rows, keep, send)


def after(value, *others):
    return lax.optimization_barrier((value, *others))[0]


def on_device(probe, object_delta, measured, pos_y, pos_x, prop_phase):
    number = lax.axis_size("row")
    sections = lax.axis_size("sect")
    cores = lax.axis_size("batch")
    place, section, core = (lax.axis_index(axis) for axis in line_axes)
    height, breadth = probe.shape[1], probe.shape[2]
    spans = object_delta.shape[3] // breadth
    half, wide = height // 2, breadth // 2
    plan = Plan(number, sections, cores, measured.shape[1], spans, breadth)
    total = plan.total
    home_z = [plan.home(q)[0] for q in range(total)]
    home_x = [plan.home(q)[1] for q in range(total)]
    base = [plan.base(q) for q in range(total)]
    assert len(set(base)) == total

    def spot(z, x, c):
        return (z * sections + x) * cores + c

    every = [(q, c) for q in range(total) for c in range(cores)]

    def inward(j, layer):
        return [
            (spot((base[q] + j) % number, layer, c), spot(home_z[q], home_x[q], c)) for q, c in every
        ]

    def outward(j, layer):
        return [(target, source) for source, target in inward(j, layer)]

    def move(value, pairs):
        return lax.ppermute(value, line_axes, pairs)

    def swap(value):
        return lax.ppermute(value, "batch", [(i, (i + 1) % cores) for i in range(cores)])

    column_forward, column_inverse = (jnp.asarray(table) for table in column_tables(breadth))
    row_forward, row_inverse = (jnp.asarray(table) for table in row_tables(breadth))
    lane_factors, line_factors = (jnp.asarray(table) for table in twiddles(breadth))

    params = pltpu.CompilerParams(vmem_limit_bytes=vmem_bytes)
    def beside(*vectors):
        sizes = [value.shape[0] for value in vectors]
        return sum(
            jnp.pad(value, (sum(sizes[:i]), sum(sizes[i + 1 :]))) for i, value in enumerate(vectors)
        ).astype(jnp.int32)

    own_positions = beside(pos_y[0], pos_x[0])
    about = jnp.stack([core, place, section]).astype(jnp.int32)
    info = beside(about, own_positions, swap(own_positions))
    part = jnp.where(after(core, own_positions) == 0, probe[:, :half], probe[:, half:])
    above = lax.ppermute(part, "row", [(i, (i + 1) % number) for i in range(number)])

    def whole(shape):
        return pl.BlockSpec(tuple(shape), lambda i, *_: (0,) * len(shape))

    def floats(*shape):
        return jax.ShapeDtypeStruct(shape, jnp.float32)

    pieces_shape = (plan.own_probes, half, breadth)
    hbm = pl.BlockSpec(memory_space=pltpu.MemorySpace.HBM)
    phase_piece, own_pieces, other_pieces = pl.pallas_call(
        prepare_kernel,
        out_shape=[floats(half, breadth), floats(*pieces_shape), floats(*pieces_shape)],
        in_specs=[pl.BlockSpec(memory_space=smem), hbm, hbm],
        out_specs=[pl.BlockSpec(memory_space=pltpu.VMEM)] * 3,
        scratch_shapes=[
            pltpu.VMEM((height, breadth), jnp.float32),
            pltpu.VMEM((plan.own_probes, height, breadth), jnp.float32),
            pltpu.VMEM((breadth // 128, height, 128), jnp.float32),
            pltpu.SemaphoreType.DMA((1 + plan.own_probes,)),
        ],
        cost_estimate=light,
        compiler_params=params,
    )(after(about, part), prop_phase, measured)
    other_pieces = swap(other_pieces)

    phases = [phase_piece]
    while len(phases) < number:
        step = len(phases)
        if step > 1:
            moved = jnp.stack(phases)
        else:
            moved = phases[0][None]
        if 2 * step < number:
            moved = lax.ppermute(moved, "row", [(i, (i + step) % number) for i in range(number)])
        else:
            moved = move(moved, [(spot((home_z[q] - step) % number, home_x[q], c), spot(home_z[q], home_x[q], c)) for q, c in every])
        phases = phases + [moved[i] for i in range(step)]
    phases = phases[::-1]

    def near_spec(j, far):
        return pl.BlockSpec(
            (1, 2, height, breadth), lambda i, info: (0, 0, 0, plan.blocks(info, j)[1 if far else 0])
        )

    def patch_of(j, info):
        return pl.pallas_call(
            functools.partial(patch_kernel, plan, j),
            out_shape=floats(3, half, breadth),
            in_specs=[pl.BlockSpec(memory_space=smem), hbm] + [pl.BlockSpec(memory_space=pltpu.VMEM)] * 2,
            out_specs=pl.BlockSpec(memory_space=pltpu.VMEM),
            scratch_shapes=[pltpu.VMEM((2, height, breadth), jnp.float32)] * 3 + [pltpu.SemaphoreType.DMA((2,))],
            cost_estimate=light,
            compiler_params=params,
        )(info, object_delta, own_pieces, other_pieces)

    def launch_of(j, info):
        return pl.pallas_call(
            functools.partial(launch_kernel, plan, j),
            out_shape=[floats(2, height, wide), floats(2, height, breadth)],
            grid_spec=pltpu.PrefetchScalarGridSpec(
                num_scalar_prefetch=1,
                grid=(1,),
                in_specs=[
                    near_spec(j, False),
                    near_spec(j, True),
                    whole(above.shape),
                    whole(above.shape),
                    whole(probe.shape),
                    whole(row_forward.shape),
                    whole(lane_factors.shape),
                ],
                out_specs=[whole((2, height, wide)), whole((2, height, breadth))],
            ),
            cost_estimate=light,
            compiler_params=params,
        )(
            info,
            object_delta,
            object_delta,
            above,
            above_other,
            probe,
            row_forward,
            lane_factors,
        )

    later = range(1, sections)
    own_patches = []
    for j in range(number):
        own_patches.append(patch_of(j, info if j == 0 else after(info, own_patches[-1])))
    above_other = swap(above)
    launched = []
    for j in range(number):
        ready = [launched[j - 1][0]] if j else []
        if j == number - 1:
            ready.append(phases[0])
        launched.append(launch_of(j, after(info, *ready) if ready else info))
    patches = {layer: [] for layer in later}
    blocks = []
    for j in range(number):
        value, message = own_patches[j], launched[j][0]
        if j == 0:
            value = after(value, message)
        if j >= 2:
            value = after(value, launched[-1][0], *(patches[layer][j - 2] for layer in later))
            message = after(message, blocks[j - 2])
        for layer in later:
            patches[layer].append(move(value, inward(j, layer)))
        blocks.append(move(message, inward(j, 0)))
    rolled = [launched[j][1] for j in range(number)]
    arrived = (*blocks, *(patches[layer][j] for layer in later for j in range(number)))
    blocks = lax.optimization_barrier(arrived)[:number]

    traded = (2, wide, wide)
    column_set = (column_forward, column_inverse, line_factors)
    row_set = (row_forward, row_inverse, lane_factors)

    def at_home(kernel, outs, *operands):
        return pl.pallas_call(
            kernel,
            out_shape=[floats(*shape) for shape in outs],
            in_specs=[pl.BlockSpec(memory_space=smem)] + [pl.BlockSpec(memory_space=pltpu.VMEM)] * len(operands),
            out_specs=[pl.BlockSpec(memory_space=pltpu.VMEM)] * len(outs),
            cost_estimate=light,
            compiler_params=params,
        )(about, *operands)

    def through(conjugate, own, other):
        kernel = functools.partial(through_kernel, number, conjugate)
        return at_home(kernel, [traded, traded], *column_set, field, own, other)

    entries = {}
    field = at_home(filter_kernel, [(2, breadth, wide)], after(phases[0], launched[-1][0]), *phases[1:])[0]
    keep, send = at_home(
        functools.partial(enter_kernel, number), [traded, traded], *column_set, field, *blocks
    )
    target = at_home(functools.partial(target_kernel, plan), [(breadth, wide)], *patches[1])[0]
    for layer in later:
        other = swap(send)
        entries[layer], keep, send = at_home(
            functools.partial(meet_kernel, plan),
            [(2, wide, breadth), traded, traded],
            *row_set,
            keep,
            other,
            *patches[layer],
        )
        other = swap(send)
        if layer < sections - 1:
            keep, send = through(False, keep, other)
    keep, send = at_home(
        functools.partial(residual_kernel, number), [traded, traded], *column_set, target, keep, other
    )

    terms = None
    for layer in reversed(later):
        other = swap(send)
        found = at_home(
            functools.partial(grade_kernel, plan),
            [(2, half, breadth)] * number + [(2, wide, breadth)],
            row_inverse,
            lane_factors,
            keep,
            other,
            entries[layer],
            *patches[layer],
        )
        keep, send = at_home(onward_kernel, [traded, traded], row_forward, lane_factors, found[number])
        other = swap(send)
        if layer > 1:
            came = [move(found[j], outward(j, layer)) for j in range(number)]
            terms = came if terms is None else [first + second for first, second in zip(terms, came)]
            keep, send = through(True, keep, other)
    leaving = at_home(
        functools.partial(leave_kernel, number), [(2, height, wide)] * number, *column_set, field, keep, other
    )
    came, spectra = [None] * number, [None] * number
    for j in plan.order:
        came[j] = move(after(found[j], other), outward(j, 1))
    for j in plan.order:
        spectra[j] = move(leaving[j], outward(j, 0))
    terms = came if terms is None else [first + second for first, second in zip(terms, came)]

    operands = [
        row_inverse,
        lane_factors,
        *spectra,
        *(swap(value) for value in spectra),
        *terms,
        *(swap(value) for value in terms),
        *rolled,
    ]
    return pl.pallas_call(
        functools.partial(settle_kernel, plan),
        out_shape=jax.ShapeDtypeStruct(object_delta.shape, jnp.float32),
        in_specs=[pl.BlockSpec(memory_space=smem)] + [pl.BlockSpec(memory_space=pltpu.VMEM)] * len(operands),
        out_specs=pl.BlockSpec(memory_space=pltpu.VMEM),
        scratch_shapes=[pltpu.VMEM((2, height, breadth), jnp.float32)],
        cost_estimate=light,
        compiler_params=params,
    )(info, *operands)


def solution(mesh):
    in_specs = (
        P(None, "row", None),
        P(("groups", "sect"), None, "row", None),
        P(("groups", "batch"), None, "row", None),
        P(("groups", "batch"), None),
        P(("groups", "batch"), None),
        P("row", None),
    )
    out_specs = P(("groups", "sect"), None, "row", None)
    return jax.shard_map(
        on_device, mesh=mesh, in_specs=in_specs, out_specs=out_specs, check_vma=False
    )
```

```python
import functools
import math

import jax
import jax.numpy as jnp
import ml_dtypes
import numpy as np
from jax import lax
from jax.experimental import pallas as pl
from jax.experimental.pallas import tpu as pltpu
from jax.sharding import PartitionSpec as P

highest = lax.Precision.HIGHEST
line_axes = ("row", "sect", "batch")
vmem_bytes = 20 * 1024 * 1024
light = pl.CostEstimate(flops=0, transcendentals=0, bytes_accessed=0)
smem = pltpu.MemorySpace.SMEM


def halves(table, axis):
    table = table.astype(np.float64)
    upper = table.astype(ml_dtypes.bfloat16)
    lower = (table - upper.astype(np.float64)).astype(ml_dtypes.bfloat16)
    return np.concatenate([upper, upper, lower], axis=axis)


def circle(length):
    quarter = length // 4
    index = np.arange(quarter)
    angles = (index[:, None] * index[None, :] % quarter) * (2.0 * math.pi / quarter)
    scale = 1.0 / math.sqrt(length)
    return np.cos(angles) * scale, np.sin(angles) * scale


def column_tables(length):
    cosine, sine = circle(length)
    forward = np.block([[cosine, sine], [-sine, cosine]])
    inverse = np.block([[cosine, -sine], [sine, cosine]])
    return halves(forward, 1), halves(inverse, 1)


def row_tables(length):
    cosine, sine = circle(length)
    forward = np.block([[cosine, -sine], [sine, cosine]])
    inverse = np.block([[cosine.T, sine.T], [-sine.T, cosine.T]])
    return halves(forward, 0), halves(inverse, 0)


def twiddles(length):
    quarter = length // 4
    angles = np.arange(4)[:, None] * np.arange(quarter)[None, :] * (2.0 * math.pi / length)
    pairs = np.stack([np.cos(angles), np.sin(angles)], axis=1).astype(np.float32)
    along_lanes = pairs.reshape(8, quarter)
    along_rows = np.broadcast_to(pairs[..., None], (4, 2, quarter, 128)).copy()
    return along_lanes, along_rows


def circle_polynomials(reach):
    grid = np.cos((np.arange(64) + 0.5) * math.pi / 64.0)
    square = (grid + 1.0) * 0.5 * reach * reach
    root = np.sqrt(square)
    found = []
    for values in (np.cos(root), np.sinc(root / math.pi)):
        fitted = np.polynomial.Polynomial.fit(square, values, 9, domain=[0.0, reach * reach])
        found.append([float(item) for item in fitted.convert().coef])
    return found


def split(value):
    upper = value.astype(jnp.bfloat16)
    lower = (value - upper.astype(jnp.float32)).astype(jnp.bfloat16)
    return upper, lower


def dot(first, second):
    return jnp.dot(first, second, preferred_element_type=jnp.float32)


def right_dot(value, table):
    upper, lower = split(value)
    return dot(jnp.concatenate([upper, lower, upper], axis=1), table[...])


def left_dot(table, value):
    upper, lower = split(value)
    return dot(table[...], jnp.concatenate([upper, lower, upper], axis=0))


def times(first, second):
    return (
        first[0] * second[0] - first[1] * second[1],
        first[0] * second[1] + first[1] * second[0],
    )


def conj_times(first, second):
    return (
        first[0] * second[0] + first[1] * second[1],
        first[0] * second[1] - first[1] * second[0],
    )


def plus(first, second):
    return (first[0] + second[0], first[1] + second[1])


def minus(first, second):
    return (first[0] - second[0], first[1] - second[1])


def turned(value):
    return (-value[1], value[0])


def scatter4(parts):
    sum02, dif02 = plus(parts[0], parts[2]), minus(parts[0], parts[2])
    sum13, dif13 = plus(parts[1], parts[3]), turned(minus(parts[1], parts[3]))
    return [plus(sum02, sum13), minus(dif02, dif13), minus(sum02, sum13), plus(dif02, dif13)]


def gather4(parts):
    sum02, dif02 = plus(parts[0], parts[2]), minus(parts[0], parts[2])
    sum13, dif13 = plus(parts[1], parts[3]), turned(minus(parts[1], parts[3]))
    return [plus(sum02, sum13), plus(dif02, dif13), minus(sum02, sum13), minus(dif02, dif13)]


def lane_twiddle(reference, index):
    return (reference[2 * index : 2 * index + 1, :], reference[2 * index + 1 : 2 * index + 2, :])


def forward_lanes(quarters, table, twiddle):
    rows = quarters[0][0].shape[0]
    classes = scatter4(quarters)
    packed = []
    for index, value in enumerate(classes):
        if index > 0:
            value = conj_times(lane_twiddle(twiddle, index), value)
        packed.append(jnp.concatenate(value, axis=1))
    result = right_dot(jnp.concatenate(packed, axis=0), table)
    half = result.shape[1] // 2
    return [
        (result[rows * index : rows * (index + 1), :half], result[rows * index : rows * (index + 1), half:])
        for index in range(4)
    ]


def inverse_lanes(classes, table, twiddle):
    rows = classes[0][0].shape[0]
    packed = jnp.concatenate([jnp.concatenate(value, axis=1) for value in classes], axis=0)
    result = right_dot(packed, table)
    half = result.shape[1] // 2
    parts = []
    for index in range(4):
        value = (result[rows * index : rows * (index + 1), :half], result[rows * index : rows * (index + 1), half:])
        if index > 0:
            value = times(lane_twiddle(twiddle, index), value)
        parts.append(value)
    return gather4(parts)


def forward_rows(quarters, table, twiddle):
    lanes = quarters[0][0].shape[1]
    packed = []
    for index, value in enumerate(scatter4(quarters)):
        if index > 0:
            value = conj_times((twiddle[index, 0], twiddle[index, 1]), value)
        packed.append(jnp.concatenate(value, axis=0))
    result = left_dot(table, jnp.concatenate(packed, axis=1))
    half = result.shape[0] // 2
    return [
        (result[:half, lanes * index : lanes * (index + 1)], result[half:, lanes * index : lanes * (index + 1)])
        for index in range(4)
    ]


def inverse_rows(classes, table, twiddle):
    lanes = classes[0][0].shape[1]
    packed = jnp.concatenate([jnp.concatenate(value, axis=0) for value in classes], axis=1)
    result = left_dot(table, packed)
    half = result.shape[0] // 2
    parts = []
    for index in range(4):
        value = (result[:half, lanes * index : lanes * (index + 1)], result[half:, lanes * index : lanes * (index + 1)])
        if index > 0:
            value = times((twiddle[index, 0], twiddle[index, 1]), value)
        parts.append(value)
    return gather4(parts)


def joined(parts, axis):
    return parts[0] if len(parts) == 1 else jnp.concatenate(parts, axis=axis)


class Plan:
    def __init__(self, number, sections, cores, own_probes, spans, breadth):
        assert own_probes == sections and spans > 1
        self.number, self.sections, self.cores = number, sections, cores
        self.own_probes, self.spans, self.breadth = own_probes, spans, breadth
        self.stride = number // sections
        assert self.stride >= cores
        self.top = (number - cores) // 2
        self.total = cores * own_probes
        self.order = [j for pair in zip(range(number // 2), range(number // 2, number)) for j in pair]

    def home(self, q):
        return self.top + q // self.sections, q % self.sections

    def base(self, q):
        z, x = self.home(q)
        return (z + self.stride * x) % self.number

    def own_base(self, info):
        return lax.rem(info[1] + self.stride * info[2], self.number)

    def served(self, info, j):
        step = lax.rem(info[1] - j - self.top + 2 * self.number, self.number)
        return jnp.minimum(lax.rem(step, self.stride), self.cores - 1), lax.div(step, self.stride)

    def offsets(self, info, j):
        batch, probe = self.served(info, j)
        spot = 3 + probe + jnp.where(batch == info[0], 0, 2 * self.own_probes)
        return info[spot], info[spot + self.own_probes]

    def blocks(self, info, j):
        column = self.offsets(info, j)[1]
        near = lax.div(column, self.breadth)
        far = jnp.where(near + 1 < self.spans, near + 1, near - 1)
        return near, far, lax.rem(column, self.breadth)


def prepare_kernel(info, phase_hbm, measured_hbm, phase_piece, own_pieces, other_pieces, phase, measured, scratch, sems):
    rows = phase.shape[0] // 4
    width = scratch.shape[2]
    tasks = [(pltpu.make_async_copy(phase_hbm, phase, sems.at[0]), phase, (phase_piece,))]
    for probe in range(measured.shape[0]):
        copy = pltpu.make_async_copy(measured_hbm.at[0, probe], measured.at[probe], sems.at[1 + probe])
        tasks.append((copy, measured.at[probe], (own_pieces.at[probe], other_pieces.at[probe])))
    for copy, _, _ in tasks:
        copy.start()
    for copy, source, targets in tasks:
        copy.wait()
        for tile in range(phase.shape[1] // width):
            columns = slice(width * tile, width * (tile + 1))
            scratch[tile] = source[:, columns]
            for index in range(2):
                part = slice(rows * index, rows * (index + 1))
                for flip, target in enumerate(targets):
                    low = scratch[tile, pl.ds(2 * flip + index, rows, stride=4), :]
                    high = scratch[tile, pl.ds(2 - 2 * flip + index, rows, stride=4), :]
                    target[part, columns] = jnp.where(info[0] == 0, low, high)


def exact_turn(value):
    length = value.shape[1]
    quarter = length // 4
    row = lax.broadcasted_iota(jnp.int32, (length, length), 0)
    column = lax.broadcasted_iota(jnp.int32, (length, length), 1)
    wanted = 4 * lax.rem(row, quarter) + lax.div(row, quarter)
    order = (wanted == column).astype(jnp.float32).astype(jnp.bfloat16)
    first = value.astype(jnp.bfloat16)
    rest = value - first.astype(jnp.float32)
    second = rest.astype(jnp.bfloat16)
    third = (rest - second.astype(jnp.float32)).astype(jnp.bfloat16)
    dims = (((1,), (1,)), ((), ()))
    parts = [
        lax.dot_general(order, item, dims, preferred_element_type=jnp.float32) for item in (first, second, third)
    ]
    return (parts[0] + parts[1]) + parts[2]


def class_rows(pieces, index):
    rows = pieces[0].shape[0] // 2
    return joined([piece[rows * index : rows * (index + 1), :] for piece in pieces], 0)


def polynomial(coefficients, value):
    result = jnp.full_like(value, coefficients[-1])
    for item in coefficients[-2::-1]:
        result = result * value + item
    return result


def filter_kernel(info, *refs):
    pieces, field = refs[:-1], refs[-1]
    cosine, sine = circle_polynomials(3.1416)
    quarter = field.shape[2] // 2
    rows = pieces[0].shape[0] // 2
    shift = lax.rem((info[1] + 1) * rows, quarter)
    for index in range(2):
        columns = slice(quarter * index, quarter * (index + 1))
        phase = pltpu.roll(exact_turn(class_rows(pieces, index)), shift, 1)
        square = phase * phase
        field[0, :, columns] = polynomial(cosine, square)
        field[1, :, columns] = polynomial(sine, square) * phase


def target_kernel(plan, info, *refs):
    pieces, target = refs[:-1], refs[-1]
    quarter = target.shape[1] // 2
    shift = plan.own_base(info) * (pieces[0].shape[1] // 2)
    for index in range(2):
        columns = slice(quarter * index, quarter * (index + 1))
        lines = class_rows([piece.at[2] for piece in pieces], index)
        target[:, columns] = pltpu.roll(exact_turn(lines), shift, 1)


def window_delta(info, plan, j, near, far):
    height, breadth = near.shape[1], near.shape[2]
    offset_y = plan.offsets(info, j)[0]
    column = plan.blocks(info, j)[2]
    lane = lax.broadcasted_iota(jnp.int32, (height, breadth), 1)
    line = lax.broadcasted_iota(jnp.int32, (height, breadth), 0)
    vacuum = (line < offset_y) & (info[1] == 0)
    use_near = lane >= column
    return [jnp.where(vacuum, 0.0, jnp.where(use_near, near[part], far[part])) for part in range(2)]


def patch_kernel(plan, j, info, delta, own_pieces, other_pieces, patch, near, far, scratch, sems):
    height, breadth = near.shape[1], near.shape[2]
    copies = []
    for index, target in enumerate((near, far)):
        first = pl.multiple_of(plan.blocks(info, j)[index] * breadth, breadth)
        copies.append(pltpu.make_async_copy(delta.at[0, :, :, pl.ds(first, breadth)], target, sems.at[index]))
        copies[-1].start()
    for copy in copies:
        copy.wait()
    real, imag = window_delta(info, plan, j, near, far)
    scratch[0] = real + 1.0
    scratch[1] = imag
    first = pl.multiple_of(info[0] * (height // 2), height // 2)
    patch[:2] = scratch[:, pl.ds(first, height // 2), :]
    batch, probe = plan.served(info, j)
    patch[2] = jnp.where(batch == info[0], own_pieces[probe], other_pieces[probe])


def launch_kernel(
    plan, j, info, near, far, above, above_other, probe, table, twiddle, message, rolled
):
    height, breadth = near.shape[2], near.shape[3]
    quarter = breadth // 4
    real, imag = window_delta(info, plan, j, near.at[0], far.at[0])
    transmit = (real + 1.0, imag)
    offset_y = plan.offsets(info, j)[0]
    column = plan.blocks(info, j)[2]
    lower = info[0] == 0
    entering = []
    for part in range(2):
        first, second = above[part], above_other[part]
        pieces = [jnp.where(lower, first, second), jnp.where(lower, second, first), probe[part]]
        lines = pltpu.roll(jnp.concatenate(pieces, axis=0), offset_y, 0)[height:]
        entering.append(pltpu.roll(lines, column, 1))
        rolled[part] = entering[part]
    value = times(entering, transmit)
    quarters = [tuple(item[:, quarter * m : quarter * (m + 1)] for item in value) for m in range(4)]
    classes = scatter4(quarters)
    packed = []
    for index in range(2):
        chosen = tuple(jnp.where(lower, classes[index][i], classes[index + 2][i]) for i in range(2))
        low, high = lane_twiddle(twiddle, index), lane_twiddle(twiddle, index + 2)
        factor = tuple(jnp.where(lower, low[i], high[i]) for i in range(2))
        packed.append(jnp.concatenate(conj_times(factor, chosen), axis=1))
    result = right_dot(jnp.concatenate(packed, axis=0), table)
    for index in range(2):
        block = result[height * index : height * (index + 1)]
        message[0, :, quarter * index : quarter * (index + 1)] = block[:, :quarter]
        message[1, :, quarter * index : quarter * (index + 1)] = block[:, quarter:]


def settle_kernel(plan, info, table, twiddle, *refs):
    number = plan.number
    own_spectra, other_spectra = refs[:number], refs[number : 2 * number]
    own_terms, other_terms = refs[2 * number : 3 * number], refs[3 * number : 4 * number]
    rolled = refs[4 * number : 5 * number]
    out, scratch = refs[5 * number :]
    height, breadth = scratch.shape[1], scratch.shape[2]
    quarter = breadth // 4
    lower = info[0] == 0
    lane = lax.broadcasted_iota(jnp.int32, (height, breadth), 1)
    line = lax.broadcasted_iota(jnp.int32, (height, breadth), 0)
    out[...] = jnp.zeros_like(out)
    for i, j in enumerate(plan.order):

        @pl.when(info[2] == 0)
        def _():
            classes = []
            for index in range(4):
                first = quarter * (index % 2)
                pair = []
                for part in range(2):
                    own = own_spectra[i][part, :, first : first + quarter]
                    other = other_spectra[i][part, :, first : first + quarter]
                    pair.append(jnp.where(lower, own, other) if index < 2 else jnp.where(lower, other, own))
                classes.append(tuple(pair))
            inner = inverse_lanes(classes, table, twiddle)
            for m in range(4):
                columns = slice(quarter * m, quarter * (m + 1))
                entering = (rolled[i][0, :, columns], rolled[i][1, :, columns])
                term = conj_times(entering, inner[m])
                scratch[0, :, columns] = term[0]
                scratch[1, :, columns] = term[1]

        @pl.when(info[2] != 0)
        def _():
            own, other = own_terms[i][...], other_terms[i][...]
            scratch[:, : height // 2, :] = jnp.where(lower, own, other)
            scratch[:, height // 2 :, :] = jnp.where(lower, other, own)

        near_block, far_block, column = plan.blocks(info, j)
        present = (line >= plan.offsets(info, j)[0]) | (info[1] != 0)
        near = pl.ds(pl.multiple_of(near_block * breadth, breadth), breadth)
        far = pl.ds(pl.multiple_of(far_block * breadth, breadth), breadth)
        use_near = lane >= column
        for part in range(2):
            term = jnp.where(present, scratch[part], 0.0)
            out[0, part, :, near] += jnp.where(use_near, term, 0.0)
            out[0, part, :, far] += jnp.where(use_near, 0.0, term)


def split_lines(value, lower, count):
    height = value.shape[0] // count
    firsts, seconds = [], []
    for index in range(count):
        first = value[height * index : height * index + height // 2]
        second = value[height * index + height // 2 : height * (index + 1)]
        firsts.append(jnp.where(lower, first, second))
        seconds.append(jnp.where(lower, second, first))
    return joined(firsts, 0), joined(seconds, 0)


def merge_lines(own, other, lower, count):
    height = own.shape[0] // count
    parts = []
    for index in range(count):
        first = own[height * index : height * (index + 1)]
        second = other[height * index : height * (index + 1)]
        parts.append(jnp.where(lower, first, second))
        parts.append(jnp.where(lower, second, first))
    return jnp.concatenate(parts, axis=0)


def tiles(width):
    quarter = width // 2
    return [slice(quarter * index, quarter * (index + 1)) for index in range(2)]


def merged_quarters(own, other, lower, count, columns):
    lines = own.shape[1] // 4
    quarters = []
    for m in range(4):
        rows = slice(lines * m, lines * (m + 1))
        quarters.append(
            tuple(merge_lines(own[part, rows, columns], other[part, rows, columns], lower, count) for part in range(2))
        )
    return quarters


def hand_over(quarters, lower, count, columns, keep, send):
    lines = keep.shape[1] // 4
    for m in range(4):
        rows = slice(lines * m, lines * (m + 1))
        for part in range(2):
            keep[part, rows, columns], send[part, rows, columns] = split_lines(quarters[m][part], lower, count)


def filtered(classes, field, conjugate, columns):
    quarter = classes[0][0].shape[0]
    result = []
    for index in range(4):
        rows = slice(quarter * index, quarter * (index + 1))
        factor = (field[0, rows, columns], field[1, rows, columns])
        result.append((conj_times if conjugate else times)(factor, classes[index]))
    return result


def enter_kernel(number, info, forward, inverse, twiddle, field, *refs):
    blocks, (keep, send) = refs[:number], refs[number:]
    lower = info[0] == 0
    count = number // 4
    for columns in tiles(keep.shape[2]):
        quarters = [
            tuple(
                joined([blocks[count * m + i][part, :, columns] for i in range(count)], 0) for part in range(2)
            )
            for m in range(4)
        ]
        far = filtered(forward_rows(quarters, forward, twiddle), field, False, columns)
        hand_over(inverse_rows(far, inverse, twiddle), lower, count, columns, keep, send)


def through_kernel(number, conjugate, info, forward, inverse, twiddle, field, own, other, keep, send):
    lower = info[0] == 0
    count = number // 4
    for columns in tiles(keep.shape[2]):
        far = forward_rows(merged_quarters(own, other, lower, count, columns), forward, twiddle)
        far = filtered(far, field, conjugate, columns)
        hand_over(inverse_rows(far, inverse, twiddle), lower, count, columns, keep, send)


def residual_kernel(number, info, forward, inverse, twiddle, target, own, other, keep, send):
    lower = info[0] == 0
    count = number // 4
    for columns in tiles(keep.shape[2]):
        far = forward_rows(merged_quarters(own, other, lower, count, columns), forward, twiddle)
        quarter = far[0][0].shape[0]
        seeded = []
        for index in range(4):
            real, imag = far[index]
            residual = real * real + imag * imag - target[quarter * index : quarter * (index + 1), columns]
            seeded.append((residual * real, residual * imag))
        hand_over(inverse_rows(seeded, inverse, twiddle), lower, count, columns, keep, send)


def leave_kernel(number, info, forward, inverse, twiddle, field, own, other, *blocks):
    lower = info[0] == 0
    count = number // 4
    height = blocks[0].shape[1]
    for columns in tiles(own.shape[2]):
        far = forward_rows(merged_quarters(own, other, lower, count, columns), forward, twiddle)
        quarters = inverse_rows(filtered(far, field, True, columns), inverse, twiddle)
        for m in range(4):
            for i in range(count):
                for part in range(2):
                    blocks[count * m + i][part, :, columns] = quarters[m][part][height * i : height * (i + 1)]


def lane_classes(own, other, lower, rows):
    quarter = own.shape[2] // 2
    classes = []
    for index in range(4):
        columns = slice(quarter * (index % 2), quarter * (index % 2) + quarter)
        pair = []
        for part in range(2):
            first, second = own[part, rows, columns], other[part, rows, columns]
            pair.append(jnp.where(lower, first, second) if index < 2 else jnp.where(lower, second, first))
        classes.append(tuple(pair))
    return classes


def lanes_out(classes, lower, rows, keep, send):
    quarter = keep.shape[2] // 2
    for index in range(2):
        columns = slice(quarter * index, quarter * (index + 1))
        for part in range(2):
            low, high = classes[index][part], classes[index + 2][part]
            keep[part, rows, columns] = jnp.where(lower, low, high)
            send[part, rows, columns] = jnp.where(lower, high, low)


def meet_kernel(plan, info, forward, inverse, twiddle, own, other, *refs):
    number = plan.number
    patches, (entering, keep, send) = refs[:number], refs[number:]
    lower = info[0] == 0
    count = number // 4
    lines = own.shape[1] // 4
    quarter = own.shape[2] // 2
    for m in range(4):
        rows = slice(lines * m, lines * (m + 1))
        group = patches[count * m : count * (m + 1)]
        wave = inverse_lanes(lane_classes(own, other, lower, rows), inverse, twiddle)
        quarters = []
        for piece in range(4):
            columns = slice(quarter * piece, quarter * (piece + 1))
            transmit = tuple(joined([patch[part, :, columns] for patch in group], 0) for part in range(2))
            entering[0, rows, columns] = wave[piece][0]
            entering[1, rows, columns] = wave[piece][1]
            quarters.append(times(wave[piece], transmit))
        lanes_out(forward_lanes(quarters, forward, twiddle), lower, rows, keep, send)


def grade_kernel(plan, info, inverse, twiddle, own, other, entering, *refs):
    number = plan.number
    patches, terms, leaving = refs[:number], refs[number : 2 * number], refs[2 * number]
    lower = info[0] == 0
    count = number // 4
    lines = own.shape[1] // 4
    height = lines // count
    quarter = own.shape[2] // 2
    for m in range(4):
        rows = slice(lines * m, lines * (m + 1))
        group = patches[count * m : count * (m + 1)]
        inner = inverse_lanes(lane_classes(own, other, lower, rows), inverse, twiddle)
        for piece in range(4):
            columns = slice(quarter * piece, quarter * (piece + 1))
            transmit = tuple(joined([patch[part, :, columns] for patch in group], 0) for part in range(2))
            wave = (entering[0, rows, columns], entering[1, rows, columns])
            term = conj_times(wave, inner[piece])
            for i in range(count):
                for part in range(2):
                    terms[count * m + i][part, :, columns] = term[part][height * i : height * (i + 1)]
            behind = conj_times(transmit, inner[piece])
            leaving[0, rows, columns] = behind[0]
            leaving[1, rows, columns] = behind[1]


def onward_kernel(info, forward, twiddle, leaving, keep, send):
    lower = info[0] == 0
    lines = leaving.shape[1] // 4
    quarter = leaving.shape[2] // 4
    for m in range(4):
        rows = slice(lines * m, lines * (m + 1))
        quarters = [
            tuple(leaving[part, rows, quarter * piece : quarter * (piece + 1)] for part in range(2))
            for piece in range(4)
        ]
        lanes_out(forward_lanes(quarters, forward, twiddle), lower, rows, keep, send)


def after(value, *others):
    return lax.optimization_barrier((value, *others))[0]


def on_device(probe, object_delta, measured, pos_y, pos_x, prop_phase):
    number = lax.axis_size("row")
    sections = lax.axis_size("sect")
    cores = lax.axis_size("batch")
    place, section, core = (lax.axis_index(axis) for axis in line_axes)
    height, breadth = probe.shape[1], probe.shape[2]
    spans = object_delta.shape[3] // breadth
    half, wide = height // 2, breadth // 2
    plan = Plan(number, sections, cores, measured.shape[1], spans, breadth)
    total = plan.total
    home_z = [plan.home(q)[0] for q in range(total)]
    home_x = [plan.home(q)[1] for q in range(total)]
    base = [plan.base(q) for q in range(total)]
    assert len(set(base)) == total

    def spot(z, x, c):
        return (z * sections + x) * cores + c

    every = [(q, c) for q in range(total) for c in range(cores)]

    def inward(j, layer):
        return [
            (spot((base[q] + j) % number, layer, c), spot(home_z[q], home_x[q], c)) for q, c in every
        ]

    def outward(j, layer):
        return [(target, source) for source, target in inward(j, layer)]

    def move(value, pairs):
        return lax.ppermute(value, line_axes, pairs)

    def swap(value):
        return lax.ppermute(value, "batch", [(i, (i + 1) % cores) for i in range(cores)])

    column_forward, column_inverse = (jnp.asarray(table) for table in column_tables(breadth))
    row_forward, row_inverse = (jnp.asarray(table) for table in row_tables(breadth))
    lane_factors, line_factors = (jnp.asarray(table) for table in twiddles(breadth))

    params = pltpu.CompilerParams(vmem_limit_bytes=vmem_bytes)
    def beside(*vectors):
        sizes = [value.shape[0] for value in vectors]
        return sum(
            jnp.pad(value, (sum(sizes[:i]), sum(sizes[i + 1 :]))) for i, value in enumerate(vectors)
        ).astype(jnp.int32)

    own_positions = beside(pos_y[0], pos_x[0])
    about = jnp.stack([core, place, section]).astype(jnp.int32)
    info = beside(about, own_positions, swap(own_positions))
    part = jnp.where(after(core, own_positions) == 0, probe[:, :half], probe[:, half:])
    above = lax.ppermute(part, "row", [(i, (i + 1) % number) for i in range(number)])

    def whole(shape):
        return pl.BlockSpec(tuple(shape), lambda i, *_: (0,) * len(shape))

    def floats(*shape):
        return jax.ShapeDtypeStruct(shape, jnp.float32)

    pieces_shape = (plan.own_probes, half, breadth)
    hbm = pl.BlockSpec(memory_space=pltpu.MemorySpace.HBM)
    phase_piece, own_pieces, other_pieces = pl.pallas_call(
        prepare_kernel,
        out_shape=[floats(half, breadth), floats(*pieces_shape), floats(*pieces_shape)],
        in_specs=[pl.BlockSpec(memory_space=smem), hbm, hbm],
        out_specs=[pl.BlockSpec(memory_space=pltpu.VMEM)] * 3,
        scratch_shapes=[
            pltpu.VMEM((height, breadth), jnp.float32),
            pltpu.VMEM((plan.own_probes, height, breadth), jnp.float32),
            pltpu.VMEM((breadth // 128, height, 128), jnp.float32),
            pltpu.SemaphoreType.DMA((1 + plan.own_probes,)),
        ],
        cost_estimate=light,
        compiler_params=params,
    )(after(about, part), prop_phase, measured)
    other_pieces = swap(other_pieces)

    phases = [phase_piece]
    while len(phases) < number:
        step = len(phases)
        if step > 1:
            moved = jnp.stack(phases)
        else:
            moved = phases[0][None]
        if 2 * step < number:
            moved = lax.ppermute(moved, "row", [(i, (i + step) % number) for i in range(number)])
        else:
            moved = move(moved, [(spot((home_z[q] - step) % number, home_x[q], c), spot(home_z[q], home_x[q], c)) for q, c in every])
        phases = phases + [moved[i] for i in range(step)]
    phases = phases[::-1]

    def near_spec(j, far):
        return pl.BlockSpec(
            (1, 2, height, breadth), lambda i, info: (0, 0, 0, plan.blocks(info, j)[1 if far else 0])
        )

    def patch_of(j, info):
        return pl.pallas_call(
            functools.partial(patch_kernel, plan, j),
            out_shape=floats(3, half, breadth),
            in_specs=[pl.BlockSpec(memory_space=smem), hbm] + [pl.BlockSpec(memory_space=pltpu.VMEM)] * 2,
            out_specs=pl.BlockSpec(memory_space=pltpu.VMEM),
            scratch_shapes=[pltpu.VMEM((2, height, breadth), jnp.float32)] * 3 + [pltpu.SemaphoreType.DMA((2,))],
            cost_estimate=light,
            compiler_params=params,
        )(info, object_delta, own_pieces, other_pieces)

    def launch_of(j, info):
        return pl.pallas_call(
            functools.partial(launch_kernel, plan, j),
            out_shape=[floats(2, height, wide), floats(2, height, breadth)],
            grid_spec=pltpu.PrefetchScalarGridSpec(
                num_scalar_prefetch=1,
                grid=(1,),
                in_specs=[
                    near_spec(j, False),
                    near_spec(j, True),
                    whole(above.shape),
                    whole(above.shape),
                    whole(probe.shape),
                    whole(row_forward.shape),
                    whole(lane_factors.shape),
                ],
                out_specs=[whole((2, height, wide)), whole((2, height, breadth))],
            ),
            cost_estimate=light,
            compiler_params=params,
        )(
            info,
            object_delta,
            object_delta,
            above,
            above_other,
            probe,
            row_forward,
            lane_factors,
        )

    later = range(1, sections)
    own_patches = []
    for j in range(number):
        own_patches.append(patch_of(j, info if j == 0 else after(info, own_patches[-1])))
    above_other = swap(above)
    launched = []
    for j in range(number):
        ready = [launched[j - 1][0]] if j else []
        if j == number - 1:
            ready.append(phases[0])
        launched.append(launch_of(j, after(info, *ready) if ready else info))
    patches = {layer: [] for layer in later}
    blocks = []
    for j in range(number):
        value, message = own_patches[j], launched[j][0]
        if j == 0:
            value = after(value, message)
        if j >= 2:
            value = after(value, launched[-1][0], *(patches[layer][j - 2] for layer in later))
            message = after(message, blocks[j - 2])
        for layer in later:
            patches[layer].append(move(value, inward(j, layer)))
        blocks.append(move(message, inward(j, 0)))
    rolled = [launched[j][1] for j in range(number)]
    arrived = (*blocks, *(patches[layer][j] for layer in later for j in range(number)))
    blocks = lax.optimization_barrier(arrived)[:number]

    traded = (2, wide, wide)
    column_set = (column_forward, column_inverse, line_factors)
    row_set = (row_forward, row_inverse, lane_factors)

    def at_home(kernel, outs, *operands):
        return pl.pallas_call(
            kernel,
            out_shape=[floats(*shape) for shape in outs],
            in_specs=[pl.BlockSpec(memory_space=smem)] + [pl.BlockSpec(memory_space=pltpu.VMEM)] * len(operands),
            out_specs=[pl.BlockSpec(memory_space=pltpu.VMEM)] * len(outs),
            cost_estimate=light,
            compiler_params=params,
        )(about, *operands)

    def through(conjugate, own, other):
        kernel = functools.partial(through_kernel, number, conjugate)
        return at_home(kernel, [traded, traded], *column_set, field, own, other)

    entries = {}
    field = at_home(filter_kernel, [(2, breadth, wide)], after(phases[0], launched[-1][0]), *phases[1:])[0]
    keep, send = at_home(
        functools.partial(enter_kernel, number), [traded, traded], *column_set, field, *blocks
    )
    target = at_home(functools.partial(target_kernel, plan), [(breadth, wide)], *patches[1])[0]
    for layer in later:
        other = swap(send)
        entries[layer], keep, send = at_home(
            functools.partial(meet_kernel, plan),
            [(2, wide, breadth), traded, traded],
            *row_set,
            keep,
            other,
            *patches[layer],
        )
        other = swap(send)
        if layer < sections - 1:
            keep, send = through(False, keep, other)
    keep, send = at_home(
        functools.partial(residual_kernel, number), [traded, traded], *column_set, target, keep, other
    )

    terms = None
    for layer in reversed(later):
        other = swap(send)
        found = at_home(
            functools.partial(grade_kernel, plan),
            [(2, half, breadth)] * number + [(2, wide, breadth)],
            row_inverse,
            lane_factors,
            keep,
            other,
            entries[layer],
            *patches[layer],
        )
        keep, send = at_home(onward_kernel, [traded, traded], row_forward, lane_factors, found[number])
        other = swap(send)
        if layer > 1:
            came = [move(found[j], outward(j, layer)) for j in range(number)]
            terms = came if terms is None else [first + second for first, second in zip(terms, came)]
            keep, send = through(True, keep, other)
    leaving = at_home(
        functools.partial(leave_kernel, number), [(2, height, wide)] * number, *column_set, field, keep, other
    )
    came, spectra = [None] * number, [None] * number
    for j in plan.order:
        value = found[j] if j == plan.order[0] else after(found[j], other)
        came[j] = move(value, outward(j, 1))
    for j in plan.order:
        spectra[j] = move(leaving[j], outward(j, 0))
    terms = came if terms is None else [first + second for first, second in zip(terms, came)]

    operands = [
        row_inverse,
        lane_factors,
        *(spectra[j] for j in plan.order),
        *(swap(spectra[j]) for j in plan.order),
        *(terms[j] for j in plan.order),
        *(swap(after(terms[j], leaving[0])) for j in plan.order),
        *(rolled[j] for j in plan.order),
    ]
    return pl.pallas_call(
        functools.partial(settle_kernel, plan),
        out_shape=jax.ShapeDtypeStruct(object_delta.shape, jnp.float32),
        in_specs=[pl.BlockSpec(memory_space=smem)] + [pl.BlockSpec(memory_space=pltpu.VMEM)] * len(operands),
        out_specs=pl.BlockSpec(memory_space=pltpu.VMEM),
        scratch_shapes=[pltpu.VMEM((2, height, breadth), jnp.float32)],
        cost_estimate=light,
        compiler_params=params,
    )(info, *operands)


def solution(mesh):
    in_specs = (
        P(None, "row", None),
        P(("groups", "sect"), None, "row", None),
        P(("groups", "batch"), None, "row", None),
        P(("groups", "batch"), None),
        P(("groups", "batch"), None),
        P("row", None),
    )
    out_specs = P(("groups", "sect"), None, "row", None)
    return jax.shard_map(
        on_device, mesh=mesh, in_specs=in_specs, out_specs=out_specs, check_vma=False
    )
```

```python
import functools
import math

import jax
import jax.numpy as jnp
import ml_dtypes
import numpy as np
from jax import lax
from jax.experimental import pallas as pl
from jax.experimental.pallas import tpu as pltpu
from jax.sharding import PartitionSpec as P

highest = lax.Precision.HIGHEST
line_axes = ("row", "sect", "batch")
vmem_bytes = 20 * 1024 * 1024
light = pl.CostEstimate(flops=0, transcendentals=0, bytes_accessed=0)
smem = pltpu.MemorySpace.SMEM


def halves(table, axis):
    table = table.astype(np.float64)
    upper = table.astype(ml_dtypes.bfloat16)
    lower = (table - upper.astype(np.float64)).astype(ml_dtypes.bfloat16)
    return np.concatenate([upper, upper, lower], axis=axis)


def circle(length):
    quarter = length // 4
    index = np.arange(quarter)
    angles = (index[:, None] * index[None, :] % quarter) * (2.0 * math.pi / quarter)
    scale = 1.0 / math.sqrt(length)
    return np.cos(angles) * scale, np.sin(angles) * scale


def column_tables(length):
    cosine, sine = circle(length)
    forward = np.block([[cosine, sine], [-sine, cosine]])
    inverse = np.block([[cosine, -sine], [sine, cosine]])
    return halves(forward, 1), halves(inverse, 1)


def row_tables(length):
    cosine, sine = circle(length)
    forward = np.block([[cosine, -sine], [sine, cosine]])
    inverse = np.block([[cosine.T, sine.T], [-sine.T, cosine.T]])
    return halves(forward, 0), halves(inverse, 0)


def twiddles(length):
    quarter = length // 4
    angles = np.arange(4)[:, None] * np.arange(quarter)[None, :] * (2.0 * math.pi / length)
    pairs = np.stack([np.cos(angles), np.sin(angles)], axis=1).astype(np.float32)
    along_lanes = pairs.reshape(8, quarter)
    along_rows = np.broadcast_to(pairs[..., None], (4, 2, quarter, 128)).copy()
    return along_lanes, along_rows


def circle_polynomials(reach):
    grid = np.cos((np.arange(64) + 0.5) * math.pi / 64.0)
    square = (grid + 1.0) * 0.5 * reach * reach
    root = np.sqrt(square)
    found = []
    for values in (np.cos(root), np.sinc(root / math.pi)):
        fitted = np.polynomial.Polynomial.fit(square, values, 9, domain=[0.0, reach * reach])
        found.append([float(item) for item in fitted.convert().coef])
    return found


def split(value):
    upper = value.astype(jnp.bfloat16)
    lower = (value - upper.astype(jnp.float32)).astype(jnp.bfloat16)
    return upper, lower


def dot(first, second):
    return jnp.dot(first, second, preferred_element_type=jnp.float32)


def right_dot(value, table):
    upper, lower = split(value)
    return dot(jnp.concatenate([upper, lower, upper], axis=1), table[...])


def left_dot(table, value):
    upper, lower = split(value)
    return dot(table[...], jnp.concatenate([upper, lower, upper], axis=0))


def times(first, second):
    return (
        first[0] * second[0] - first[1] * second[1],
        first[0] * second[1] + first[1] * second[0],
    )


def conj_times(first, second):
    return (
        first[0] * second[0] + first[1] * second[1],
        first[0] * second[1] - first[1] * second[0],
    )


def plus(first, second):
    return (first[0] + second[0], first[1] + second[1])


def minus(first, second):
    return (first[0] - second[0], first[1] - second[1])


def turned(value):
    return (-value[1], value[0])


def scatter4(parts):
    sum02, dif02 = plus(parts[0], parts[2]), minus(parts[0], parts[2])
    sum13, dif13 = plus(parts[1], parts[3]), turned(minus(parts[1], parts[3]))
    return [plus(sum02, sum13), minus(dif02, dif13), minus(sum02, sum13), plus(dif02, dif13)]


def gather4(parts):
    sum02, dif02 = plus(parts[0], parts[2]), minus(parts[0], parts[2])
    sum13, dif13 = plus(parts[1], parts[3]), turned(minus(parts[1], parts[3]))
    return [plus(sum02, sum13), plus(dif02, dif13), minus(sum02, sum13), minus(dif02, dif13)]


def lane_twiddle(reference, index):
    return (reference[2 * index : 2 * index + 1, :], reference[2 * index + 1 : 2 * index + 2, :])


def forward_lanes(quarters, table, twiddle):
    rows = quarters[0][0].shape[0]
    classes = scatter4(quarters)
    packed = []
    for index, value in enumerate(classes):
        if index > 0:
            value = conj_times(lane_twiddle(twiddle, index), value)
        packed.append(jnp.concatenate(value, axis=1))
    result = right_dot(jnp.concatenate(packed, axis=0), table)
    half = result.shape[1] // 2
    return [
        (result[rows * index : rows * (index + 1), :half], result[rows * index : rows * (index + 1), half:])
        for index in range(4)
    ]


def inverse_lanes(classes, table, twiddle):
    rows = classes[0][0].shape[0]
    packed = jnp.concatenate([jnp.concatenate(value, axis=1) for value in classes], axis=0)
    result = right_dot(packed, table)
    half = result.shape[1] // 2
    parts = []
    for index in range(4):
        value = (result[rows * index : rows * (index + 1), :half], result[rows * index : rows * (index + 1), half:])
        if index > 0:
            value = times(lane_twiddle(twiddle, index), value)
        parts.append(value)
    return gather4(parts)


def forward_rows(quarters, table, twiddle):
    lanes = quarters[0][0].shape[1]
    packed = []
    for index, value in enumerate(scatter4(quarters)):
        if index > 0:
            value = conj_times((twiddle[index, 0], twiddle[index, 1]), value)
        packed.append(jnp.concatenate(value, axis=0))
    result = left_dot(table, jnp.concatenate(packed, axis=1))
    half = result.shape[0] // 2
    return [
        (result[:half, lanes * index : lanes * (index + 1)], result[half:, lanes * index : lanes * (index + 1)])
        for index in range(4)
    ]


def inverse_rows(classes, table, twiddle):
    lanes = classes[0][0].shape[1]
    packed = jnp.concatenate([jnp.concatenate(value, axis=0) for value in classes], axis=1)
    result = left_dot(table, packed)
    half = result.shape[0] // 2
    parts = []
    for index in range(4):
        value = (result[:half, lanes * index : lanes * (index + 1)], result[half:, lanes * index : lanes * (index + 1)])
        if index > 0:
            value = times((twiddle[index, 0], twiddle[index, 1]), value)
        parts.append(value)
    return gather4(parts)


def joined(parts, axis):
    return parts[0] if len(parts) == 1 else jnp.concatenate(parts, axis=axis)


class Plan:
    def __init__(self, number, sections, cores, own_probes, spans, breadth):
        assert own_probes == sections and spans > 1
        self.number, self.sections, self.cores = number, sections, cores
        self.own_probes, self.spans, self.breadth = own_probes, spans, breadth
        self.stride = number // sections
        assert self.stride >= cores
        self.top = (number - cores) // 2
        self.total = cores * own_probes
        half = number // 2
        self.order = [j for i in range(half) for j in ((i, i + half) if i % 2 == 0 else (i + half, i))]

    def home(self, q):
        return self.top + q // self.sections, q % self.sections

    def base(self, q):
        z, x = self.home(q)
        return (z + self.stride * x) % self.number

    def own_base(self, info):
        return lax.rem(info[1] + self.stride * info[2], self.number)

    def served(self, info, j):
        step = lax.rem(info[1] - j - self.top + 2 * self.number, self.number)
        return jnp.minimum(lax.rem(step, self.stride), self.cores - 1), lax.div(step, self.stride)

    def offsets(self, info, j):
        batch, probe = self.served(info, j)
        spot = 3 + probe + jnp.where(batch == info[0], 0, 2 * self.own_probes)
        return info[spot], info[spot + self.own_probes]

    def blocks(self, info, j):
        column = self.offsets(info, j)[1]
        near = lax.div(column, self.breadth)
        far = jnp.where(near + 1 < self.spans, near + 1, near - 1)
        return near, far, lax.rem(column, self.breadth)


def prepare_kernel(info, phase_hbm, measured_hbm, phase_piece, own_pieces, other_pieces, phase, measured, scratch, sems):
    rows = phase.shape[0] // 4
    width = scratch.shape[2]
    tasks = [(pltpu.make_async_copy(phase_hbm, phase, sems.at[0]), phase, (phase_piece,))]
    for probe in range(measured.shape[0]):
        copy = pltpu.make_async_copy(measured_hbm.at[0, probe], measured.at[probe], sems.at[1 + probe])
        tasks.append((copy, measured.at[probe], (own_pieces.at[probe], other_pieces.at[probe])))
    for copy, _, _ in tasks:
        copy.start()
    for copy, source, targets in tasks:
        copy.wait()
        for tile in range(phase.shape[1] // width):
            columns = slice(width * tile, width * (tile + 1))
            scratch[tile] = source[:, columns]
            for index in range(2):
                part = slice(rows * index, rows * (index + 1))
                for flip, target in enumerate(targets):
                    low = scratch[tile, pl.ds(2 * flip + index, rows, stride=4), :]
                    high = scratch[tile, pl.ds(2 - 2 * flip + index, rows, stride=4), :]
                    target[part, columns] = jnp.where(info[0] == 0, low, high)


def exact_turn(value):
    length = value.shape[1]
    quarter = length // 4
    row = lax.broadcasted_iota(jnp.int32, (length, length), 0)
    column = lax.broadcasted_iota(jnp.int32, (length, length), 1)
    wanted = 4 * lax.rem(row, quarter) + lax.div(row, quarter)
    order = (wanted == column).astype(jnp.float32).astype(jnp.bfloat16)
    first = value.astype(jnp.bfloat16)
    rest = value - first.astype(jnp.float32)
    second = rest.astype(jnp.bfloat16)
    third = (rest - second.astype(jnp.float32)).astype(jnp.bfloat16)
    dims = (((1,), (1,)), ((), ()))
    parts = [
        lax.dot_general(order, item, dims, preferred_element_type=jnp.float32) for item in (first, second, third)
    ]
    return (parts[0] + parts[1]) + parts[2]


def class_rows(pieces, index):
    rows = pieces[0].shape[0] // 2
    return joined([piece[rows * index : rows * (index + 1), :] for piece in pieces], 0)


def polynomial(coefficients, value):
    result = jnp.full_like(value, coefficients[-1])
    for item in coefficients[-2::-1]:
        result = result * value + item
    return result


def filter_kernel(info, *refs):
    pieces, field = refs[:-1], refs[-1]
    cosine, sine = circle_polynomials(3.1416)
    quarter = field.shape[2] // 2
    rows = pieces[0].shape[0] // 2
    shift = lax.rem((info[1] + 1) * rows, quarter)
    for index in range(2):
        columns = slice(quarter * index, quarter * (index + 1))
        phase = pltpu.roll(exact_turn(class_rows(pieces, index)), shift, 1)
        square = phase * phase
        field[0, :, columns] = polynomial(cosine, square)
        field[1, :, columns] = polynomial(sine, square) * phase


def target_kernel(plan, info, *refs):
    pieces, target = refs[:-1], refs[-1]
    quarter = target.shape[1] // 2
    shift = plan.own_base(info) * (pieces[0].shape[1] // 2)
    for index in range(2):
        columns = slice(quarter * index, quarter * (index + 1))
        lines = class_rows([piece.at[2] for piece in pieces], index)
        target[:, columns] = pltpu.roll(exact_turn(lines), shift, 1)


def window_delta(info, plan, j, near, far):
    height, breadth = near.shape[1], near.shape[2]
    offset_y = plan.offsets(info, j)[0]
    column = plan.blocks(info, j)[2]
    lane = lax.broadcasted_iota(jnp.int32, (height, breadth), 1)
    line = lax.broadcasted_iota(jnp.int32, (height, breadth), 0)
    vacuum = (line < offset_y) & (info[1] == 0)
    use_near = lane >= column
    return [jnp.where(vacuum, 0.0, jnp.where(use_near, near[part], far[part])) for part in range(2)]


def patch_kernel(plan, j, info, delta, own_pieces, other_pieces, patch, near, far, scratch, sems):
    height, breadth = near.shape[1], near.shape[2]
    copies = []
    for index, target in enumerate((near, far)):
        first = pl.multiple_of(plan.blocks(info, j)[index] * breadth, breadth)
        copies.append(pltpu.make_async_copy(delta.at[0, :, :, pl.ds(first, breadth)], target, sems.at[index]))
        copies[-1].start()
    for copy in copies:
        copy.wait()
    real, imag = window_delta(info, plan, j, near, far)
    scratch[0] = real + 1.0
    scratch[1] = imag
    first = pl.multiple_of(info[0] * (height // 2), height // 2)
    patch[:2] = scratch[:, pl.ds(first, height // 2), :]
    batch, probe = plan.served(info, j)
    patch[2] = jnp.where(batch == info[0], own_pieces[probe], other_pieces[probe])


def launch_kernel(
    plan, j, info, near, far, above, above_other, probe, table, twiddle, message, rolled
):
    height, breadth = near.shape[2], near.shape[3]
    quarter = breadth // 4
    real, imag = window_delta(info, plan, j, near.at[0], far.at[0])
    transmit = (real + 1.0, imag)
    offset_y = plan.offsets(info, j)[0]
    column = plan.blocks(info, j)[2]
    lower = info[0] == 0
    entering = []
    for part in range(2):
        first, second = above[part], above_other[part]
        pieces = [jnp.where(lower, first, second), jnp.where(lower, second, first), probe[part]]
        lines = pltpu.roll(jnp.concatenate(pieces, axis=0), offset_y, 0)[height:]
        entering.append(pltpu.roll(lines, column, 1))
        rolled[part] = entering[part]
    value = times(entering, transmit)
    quarters = [tuple(item[:, quarter * m : quarter * (m + 1)] for item in value) for m in range(4)]
    classes = scatter4(quarters)
    packed = []
    for index in range(2):
        chosen = tuple(jnp.where(lower, classes[index][i], classes[index + 2][i]) for i in range(2))
        low, high = lane_twiddle(twiddle, index), lane_twiddle(twiddle, index + 2)
        factor = tuple(jnp.where(lower, low[i], high[i]) for i in range(2))
        packed.append(jnp.concatenate(conj_times(factor, chosen), axis=1))
    result = right_dot(jnp.concatenate(packed, axis=0), table)
    for index in range(2):
        block = result[height * index : height * (index + 1)]
        message[0, :, quarter * index : quarter * (index + 1)] = block[:, :quarter]
        message[1, :, quarter * index : quarter * (index + 1)] = block[:, quarter:]


def settle_kernel(plan, info, table, twiddle, *refs):
    number = plan.number
    own_spectra, other_spectra = refs[:number], refs[number : 2 * number]
    own_terms, other_terms = refs[2 * number : 3 * number], refs[3 * number : 4 * number]
    rolled = refs[4 * number : 5 * number]
    out, scratch = refs[5 * number :]
    height, breadth = scratch.shape[1], scratch.shape[2]
    quarter = breadth // 4
    lower = info[0] == 0
    lane = lax.broadcasted_iota(jnp.int32, (height, breadth), 1)
    line = lax.broadcasted_iota(jnp.int32, (height, breadth), 0)
    out[...] = jnp.zeros_like(out)
    for i, j in enumerate(plan.order):

        @pl.when(info[2] == 0)
        def _():
            for first in range(0, height, min(height, 32)):
                rows = slice(first, first + min(height, 32))
                inner = inverse_lanes(lane_classes(own_spectra[i], other_spectra[i], lower, rows), table, twiddle)
                for m in range(4):
                    columns = slice(quarter * m, quarter * (m + 1))
                    entering = (rolled[i][0, rows, columns], rolled[i][1, rows, columns])
                    term = conj_times(entering, inner[m])
                    scratch[0, rows, columns] = term[0]
                    scratch[1, rows, columns] = term[1]

        @pl.when(info[2] != 0)
        def _():
            own, other = own_terms[i][...], other_terms[i][...]
            scratch[:, : height // 2, :] = jnp.where(lower, own, other)
            scratch[:, height // 2 :, :] = jnp.where(lower, other, own)

        near_block, far_block, column = plan.blocks(info, j)
        present = (line >= plan.offsets(info, j)[0]) | (info[1] != 0)
        near = pl.ds(pl.multiple_of(near_block * breadth, breadth), breadth)
        far = pl.ds(pl.multiple_of(far_block * breadth, breadth), breadth)
        use_near = lane >= column
        for part in range(2):
            term = jnp.where(present, scratch[part], 0.0)
            out[0, part, :, near] += jnp.where(use_near, term, 0.0)
            out[0, part, :, far] += jnp.where(use_near, 0.0, term)


def split_lines(value, lower, count):
    height = value.shape[0] // count
    firsts, seconds = [], []
    for index in range(count):
        first = value[height * index : height * index + height // 2]
        second = value[height * index + height // 2 : height * (index + 1)]
        firsts.append(jnp.where(lower, first, second))
        seconds.append(jnp.where(lower, second, first))
    return joined(firsts, 0), joined(seconds, 0)


def merge_lines(own, other, lower, count):
    height = own.shape[0] // count
    parts = []
    for index in range(count):
        first = own[height * index : height * (index + 1)]
        second = other[height * index : height * (index + 1)]
        parts.append(jnp.where(lower, first, second))
        parts.append(jnp.where(lower, second, first))
    return jnp.concatenate(parts, axis=0)


def tiles(width):
    quarter = width // 2
    return [slice(quarter * index, quarter * (index + 1)) for index in range(2)]


def merged_quarters(own, other, lower, count, columns):
    lines = own.shape[1] // 4
    quarters = []
    for m in range(4):
        rows = slice(lines * m, lines * (m + 1))
        quarters.append(
            tuple(merge_lines(own[part, rows, columns], other[part, rows, columns], lower, count) for part in range(2))
        )
    return quarters


def hand_over(quarters, lower, count, columns, keep, send):
    lines = keep.shape[1] // 4
    for m in range(4):
        rows = slice(lines * m, lines * (m + 1))
        for part in range(2):
            keep[part, rows, columns], send[part, rows, columns] = split_lines(quarters[m][part], lower, count)


def filtered(classes, field, conjugate, columns):
    quarter = classes[0][0].shape[0]
    result = []
    for index in range(4):
        rows = slice(quarter * index, quarter * (index + 1))
        factor = (field[0, rows, columns], field[1, rows, columns])
        result.append((conj_times if conjugate else times)(factor, classes[index]))
    return result


def enter_kernel(number, info, forward, inverse, twiddle, field, *refs):
    blocks, (keep, send) = refs[:number], refs[number:]
    lower = info[0] == 0
    count = number // 4
    for columns in tiles(keep.shape[2]):
        quarters = [
            tuple(
                joined([blocks[count * m + i][part, :, columns] for i in range(count)], 0) for part in range(2)
            )
            for m in range(4)
        ]
        far = filtered(forward_rows(quarters, forward, twiddle), field, False, columns)
        hand_over(inverse_rows(far, inverse, twiddle), lower, count, columns, keep, send)


def through_kernel(number, conjugate, info, forward, inverse, twiddle, field, own, other, keep, send):
    lower = info[0] == 0
    count = number // 4
    for columns in tiles(keep.shape[2]):
        far = forward_rows(merged_quarters(own, other, lower, count, columns), forward, twiddle)
        far = filtered(far, field, conjugate, columns)
        hand_over(inverse_rows(far, inverse, twiddle), lower, count, columns, keep, send)


def residual_kernel(number, info, forward, inverse, twiddle, target, own, other, keep, send):
    lower = info[0] == 0
    count = number // 4
    for columns in tiles(keep.shape[2]):
        far = forward_rows(merged_quarters(own, other, lower, count, columns), forward, twiddle)
        quarter = far[0][0].shape[0]
        seeded = []
        for index in range(4):
            real, imag = far[index]
            residual = real * real + imag * imag - target[quarter * index : quarter * (index + 1), columns]
            seeded.append((residual * real, residual * imag))
        hand_over(inverse_rows(seeded, inverse, twiddle), lower, count, columns, keep, send)


def leave_kernel(number, info, forward, inverse, twiddle, field, own, other, *blocks):
    lower = info[0] == 0
    count = number // 4
    height = blocks[0].shape[1]
    for columns in tiles(own.shape[2]):
        far = forward_rows(merged_quarters(own, other, lower, count, columns), forward, twiddle)
        quarters = inverse_rows(filtered(far, field, True, columns), inverse, twiddle)
        for m in range(4):
            for i in range(count):
                for part in range(2):
                    blocks[count * m + i][part, :, columns] = quarters[m][part][height * i : height * (i + 1)]


def lane_classes(own, other, lower, rows):
    quarter = own.shape[2] // 2
    classes = []
    for index in range(4):
        columns = slice(quarter * (index % 2), quarter * (index % 2) + quarter)
        pair = []
        for part in range(2):
            first, second = own[part, rows, columns], other[part, rows, columns]
            pair.append(jnp.where(lower, first, second) if index < 2 else jnp.where(lower, second, first))
        classes.append(tuple(pair))
    return classes


def lanes_out(classes, lower, rows, keep, send):
    quarter = keep.shape[2] // 2
    for index in range(2):
        columns = slice(quarter * index, quarter * (index + 1))
        for part in range(2):
            low, high = classes[index][part], classes[index + 2][part]
            keep[part, rows, columns] = jnp.where(lower, low, high)
            send[part, rows, columns] = jnp.where(lower, high, low)


def meet_kernel(plan, info, forward, inverse, twiddle, own, other, *refs):
    number = plan.number
    patches, (entering, keep, send) = refs[:number], refs[number:]
    lower = info[0] == 0
    count = number // 4
    lines = own.shape[1] // 4
    quarter = own.shape[2] // 2
    for m in range(4):
        rows = slice(lines * m, lines * (m + 1))
        group = patches[count * m : count * (m + 1)]
        wave = inverse_lanes(lane_classes(own, other, lower, rows), inverse, twiddle)
        quarters = []
        for piece in range(4):
            columns = slice(quarter * piece, quarter * (piece + 1))
            transmit = tuple(joined([patch[part, :, columns] for patch in group], 0) for part in range(2))
            entering[0, rows, columns] = wave[piece][0]
            entering[1, rows, columns] = wave[piece][1]
            quarters.append(times(wave[piece], transmit))
        lanes_out(forward_lanes(quarters, forward, twiddle), lower, rows, keep, send)


def grade_kernel(plan, info, inverse, twiddle, own, other, entering, *refs):
    number = plan.number
    patches, terms, leaving = refs[:number], refs[number : 2 * number], refs[2 * number]
    lower = info[0] == 0
    count = number // 4
    lines = own.shape[1] // 4
    height = lines // count
    quarter = own.shape[2] // 2
    for m in range(4):
        rows = slice(lines * m, lines * (m + 1))
        group = patches[count * m : count * (m + 1)]
        inner = inverse_lanes(lane_classes(own, other, lower, rows), inverse, twiddle)
        for piece in range(4):
            columns = slice(quarter * piece, quarter * (piece + 1))
            transmit = tuple(joined([patch[part, :, columns] for patch in group], 0) for part in range(2))
            wave = (entering[0, rows, columns], entering[1, rows, columns])
            term = conj_times(wave, inner[piece])
            for i in range(count):
                for part in range(2):
                    terms[count * m + i][part, :, columns] = term[part][height * i : height * (i + 1)]
            behind = conj_times(transmit, inner[piece])
            leaving[0, rows, columns] = behind[0]
            leaving[1, rows, columns] = behind[1]


def onward_kernel(info, forward, twiddle, leaving, keep, send):
    lower = info[0] == 0
    lines = leaving.shape[1] // 4
    quarter = leaving.shape[2] // 4
    for m in range(4):
        rows = slice(lines * m, lines * (m + 1))
        quarters = [
            tuple(leaving[part, rows, quarter * piece : quarter * (piece + 1)] for part in range(2))
            for piece in range(4)
        ]
        lanes_out(forward_lanes(quarters, forward, twiddle), lower, rows, keep, send)


def after(value, *others):
    return lax.optimization_barrier((value, *others))[0]


def on_device(probe, object_delta, measured, pos_y, pos_x, prop_phase):
    number = lax.axis_size("row")
    sections = lax.axis_size("sect")
    cores = lax.axis_size("batch")
    place, section, core = (lax.axis_index(axis) for axis in line_axes)
    height, breadth = probe.shape[1], probe.shape[2]
    spans = object_delta.shape[3] // breadth
    half, wide = height // 2, breadth // 2
    plan = Plan(number, sections, cores, measured.shape[1], spans, breadth)
    total = plan.total
    home_z = [plan.home(q)[0] for q in range(total)]
    home_x = [plan.home(q)[1] for q in range(total)]
    base = [plan.base(q) for q in range(total)]
    assert len(set(base)) == total

    def spot(z, x, c):
        return (z * sections + x) * cores + c

    every = [(q, c) for q in range(total) for c in range(cores)]

    def inward(j, layer):
        return [
            (spot((base[q] + j) % number, layer, c), spot(home_z[q], home_x[q], c)) for q, c in every
        ]

    def outward(j, layer):
        return [(target, source) for source, target in inward(j, layer)]

    def move(value, pairs):
        return lax.ppermute(value, line_axes, pairs)

    def swap(value):
        return lax.ppermute(value, "batch", [(i, (i + 1) % cores) for i in range(cores)])

    column_forward, column_inverse = (jnp.asarray(table) for table in column_tables(breadth))
    row_forward, row_inverse = (jnp.asarray(table) for table in row_tables(breadth))
    lane_factors, line_factors = (jnp.asarray(table) for table in twiddles(breadth))

    params = pltpu.CompilerParams(vmem_limit_bytes=vmem_bytes)
    def beside(*vectors):
        sizes = [value.shape[0] for value in vectors]
        return sum(
            jnp.pad(value, (sum(sizes[:i]), sum(sizes[i + 1 :]))) for i, value in enumerate(vectors)
        ).astype(jnp.int32)

    own_positions = beside(pos_y[0], pos_x[0])
    about = jnp.stack([core, place, section]).astype(jnp.int32)
    info = beside(about, own_positions, swap(own_positions))
    part = jnp.where(after(core, own_positions) == 0, probe[:, :half], probe[:, half:])
    above = lax.ppermute(part, "row", [(i, (i + 1) % number) for i in range(number)])

    def whole(shape):
        return pl.BlockSpec(tuple(shape), lambda i, *_: (0,) * len(shape))

    def floats(*shape):
        return jax.ShapeDtypeStruct(shape, jnp.float32)

    pieces_shape = (plan.own_probes, half, breadth)
    hbm = pl.BlockSpec(memory_space=pltpu.MemorySpace.HBM)
    phase_piece, own_pieces, other_pieces = pl.pallas_call(
        prepare_kernel,
        out_shape=[floats(half, breadth), floats(*pieces_shape), floats(*pieces_shape)],
        in_specs=[pl.BlockSpec(memory_space=smem), hbm, hbm],
        out_specs=[pl.BlockSpec(memory_space=pltpu.VMEM)] * 3,
        scratch_shapes=[
            pltpu.VMEM((height, breadth), jnp.float32),
            pltpu.VMEM((plan.own_probes, height, breadth), jnp.float32),
            pltpu.VMEM((breadth // 128, height, 128), jnp.float32),
            pltpu.SemaphoreType.DMA((1 + plan.own_probes,)),
        ],
        cost_estimate=light,
        compiler_params=params,
    )(after(about, part), prop_phase, measured)
    other_pieces = swap(other_pieces)

    phases = [phase_piece]
    while len(phases) < number:
        step = len(phases)
        if step > 1:
            moved = jnp.stack(phases)
        else:
            moved = phases[0][None]
        if 2 * step < number:
            moved = lax.ppermute(moved, "row", [(i, (i + step) % number) for i in range(number)])
        else:
            moved = move(moved, [(spot((home_z[q] - step) % number, home_x[q], c), spot(home_z[q], home_x[q], c)) for q, c in every])
        phases = phases + [moved[i] for i in range(step)]
    phases = phases[::-1]

    def near_spec(j, far):
        return pl.BlockSpec(
            (1, 2, height, breadth), lambda i, info: (0, 0, 0, plan.blocks(info, j)[1 if far else 0])
        )

    def patch_of(j, info):
        return pl.pallas_call(
            functools.partial(patch_kernel, plan, j),
            out_shape=floats(3, half, breadth),
            in_specs=[pl.BlockSpec(memory_space=smem), hbm] + [pl.BlockSpec(memory_space=pltpu.VMEM)] * 2,
            out_specs=pl.BlockSpec(memory_space=pltpu.VMEM),
            scratch_shapes=[pltpu.VMEM((2, height, breadth), jnp.float32)] * 3 + [pltpu.SemaphoreType.DMA((2,))],
            cost_estimate=light,
            compiler_params=params,
        )(info, object_delta, own_pieces, other_pieces)

    def launch_of(j, info):
        return pl.pallas_call(
            functools.partial(launch_kernel, plan, j),
            out_shape=[floats(2, height, wide), floats(2, height, breadth)],
            grid_spec=pltpu.PrefetchScalarGridSpec(
                num_scalar_prefetch=1,
                grid=(1,),
                in_specs=[
                    near_spec(j, False),
                    near_spec(j, True),
                    whole(above.shape),
                    whole(above.shape),
                    whole(probe.shape),
                    whole(row_forward.shape),
                    whole(lane_factors.shape),
                ],
                out_specs=[whole((2, height, wide)), whole((2, height, breadth))],
            ),
            cost_estimate=light,
            compiler_params=params,
        )(
            info,
            object_delta,
            object_delta,
            above,
            above_other,
            probe,
            row_forward,
            lane_factors,
        )

    later = range(1, sections)
    own_patches = []
    for j in range(number):
        own_patches.append(patch_of(j, info if j == 0 else after(info, own_patches[-1])))
    above_other = swap(above)
    launched = []
    for j in range(number):
        ready = [launched[j - 1][0]] if j else []
        if j == number - 1:
            ready.append(phases[0])
        launched.append(launch_of(j, after(info, *ready) if ready else info))
    patches = {layer: [] for layer in later}
    blocks = []
    for j in range(number):
        value, message = own_patches[j], launched[j][0]
        if j == 0:
            value = after(value, message)
        if j >= 2:
            value = after(value, launched[-1][0], *(patches[layer][j - 2] for layer in later))
            message = after(message, blocks[j - 2])
        for layer in later:
            patches[layer].append(move(value, inward(j, layer)))
        blocks.append(move(message, inward(j, 0)))
    rolled = [launched[j][1] for j in range(number)]
    arrived = (*blocks, *(patches[layer][j] for layer in later for j in range(number)))
    blocks = lax.optimization_barrier(arrived)[:number]

    traded = (2, wide, wide)
    column_set = (column_forward, column_inverse, line_factors)
    row_set = (row_forward, row_inverse, lane_factors)

    def at_home(kernel, outs, *operands):
        return pl.pallas_call(
            kernel,
            out_shape=[floats(*shape) for shape in outs],
            in_specs=[pl.BlockSpec(memory_space=smem)] + [pl.BlockSpec(memory_space=pltpu.VMEM)] * len(operands),
            out_specs=[pl.BlockSpec(memory_space=pltpu.VMEM)] * len(outs),
            cost_estimate=light,
            compiler_params=params,
        )(about, *operands)

    def through(conjugate, own, other):
        kernel = functools.partial(through_kernel, number, conjugate)
        return at_home(kernel, [traded, traded], *column_set, field, own, other)

    entries = {}
    field = at_home(filter_kernel, [(2, breadth, wide)], after(phases[0], launched[-1][0]), *phases[1:])[0]
    keep, send = at_home(
        functools.partial(enter_kernel, number), [traded, traded], *column_set, field, *blocks
    )
    target = at_home(functools.partial(target_kernel, plan), [(breadth, wide)], *patches[1])[0]
    for layer in later:
        other = swap(send)
        entries[layer], keep, send = at_home(
            functools.partial(meet_kernel, plan),
            [(2, wide, breadth), traded, traded],
            *row_set,
            keep,
            other,
            *patches[layer],
        )
        other = swap(send)
        if layer < sections - 1:
            keep, send = through(False, keep, other)
    keep, send = at_home(
        functools.partial(residual_kernel, number), [traded, traded], *column_set, target, keep, other
    )

    terms = None
    for layer in reversed(later):
        other = swap(send)
        found = at_home(
            functools.partial(grade_kernel, plan),
            [(2, half, breadth)] * number + [(2, wide, breadth)],
            row_inverse,
            lane_factors,
            keep,
            other,
            entries[layer],
            *patches[layer],
        )
        keep, send = at_home(onward_kernel, [traded, traded], row_forward, lane_factors, found[number])
        other = swap(send)
        if layer > 1:
            came = [move(found[j], outward(j, layer)) for j in range(number)]
            terms = came if terms is None else [first + second for first, second in zip(terms, came)]
            keep, send = through(True, keep, other)
    leaving = at_home(
        functools.partial(leave_kernel, number), [(2, height, wide)] * number, *column_set, field, keep, other
    )
    came, spectra = [None] * number, [None] * number
    for j in plan.order:
        value = found[j] if j == plan.order[0] else after(found[j], other)
        came[j] = move(value, outward(j, 1))
    for j in plan.order:
        spectra[j] = move(leaving[j], outward(j, 0))
    terms = came if terms is None else [first + second for first, second in zip(terms, came)]

    operands = [
        row_inverse,
        lane_factors,
        *(spectra[j] for j in plan.order),
        *(swap(spectra[j]) for j in plan.order),
        *(terms[j] for j in plan.order),
        *(swap(after(terms[j], leaving[0])) for j in plan.order),
        *(rolled[j] for j in plan.order),
    ]
    return pl.pallas_call(
        functools.partial(settle_kernel, plan),
        out_shape=jax.ShapeDtypeStruct(object_delta.shape, jnp.float32),
        in_specs=[pl.BlockSpec(memory_space=smem)] + [pl.BlockSpec(memory_space=pltpu.VMEM)] * len(operands),
        out_specs=pl.BlockSpec(memory_space=pltpu.VMEM),
        scratch_shapes=[pltpu.VMEM((2, height, breadth), jnp.float32)],
        cost_estimate=light,
        compiler_params=params,
    )(info, *operands)


def solution(mesh):
    in_specs = (
        P(None, "row", None),
        P(("groups", "sect"), None, "row", None),
        P(("groups", "batch"), None, "row", None),
        P(("groups", "batch"), None),
        P(("groups", "batch"), None),
        P("row", None),
    )
    out_specs = P(("groups", "sect"), None, "row", None)
    return jax.shard_map(
        on_device, mesh=mesh, in_specs=in_specs, out_specs=out_specs, check_vma=False
    )
```
